32 devices in a mesh: dp: 8 (over y, x, core), tensor: 4 (over z).
Axes of the slice: x: 2, y: 2, z: 4, core: 2. Of those that a mesh axis runs over, the one named last changes fastest.
Arguments:
- tokens: bfloat16 [8192, 2048], P('dp'), may hold values from -6 to 6
- lengths: int32 [8, 4], P('dp'), may hold values from 0 to 1024, as said below
- cotangent: bfloat16 [8192, 2048], P('dp'), may hold values from -6 to 6
- qk_weight: float32 [2, 2048, 2048], P(None, 'dp', 'tensor'), may hold values from -0.125 to 0.125
- qk_first: float32 [2, 2048, 2048], P(None, 'dp', 'tensor'), may hold values from -28 to 28
- qk_second: float32 [2, 2048, 2048], P(None, 'dp', 'tensor'), may hold values from 40.96 to 655.36
- inner_weight: float32 [4, 2048, 4096], P(None, 'dp', 'tensor'), may hold values from -0.125 to 0.125
- inner_first: float32 [4, 2048, 4096], P(None, 'dp', 'tensor'), may hold values from -24 to 24
- inner_second: float32 [4, 2048, 4096], P(None, 'dp', 'tensor'), may hold values from 32.768 to 573.44
- outer_weight: float32 [2, 2048, 4096], P(None, 'dp', 'tensor'), may hold values from -0.09375 to 0.09375
- outer_first: float32 [2, 2048, 4096], P(None, 'dp', 'tensor'), may hold values from -24 to 24
- outer_second: float32 [2, 2048, 4096], P(None, 'dp', 'tensor'), may hold values from 32.768 to 573.44
- norm_params: float32 [4, 2048], P(None, 'dp')
- norm_first: float32 [4, 2048], P(None, 'dp'), may hold values from -32 to 32
- norm_second: float32 [4, 2048], P(None, 'dp'), may hold values from 53.248 to 819.2
- group_gain: float32 [8, 512], P('tensor', 'dp'), may hold values from 0.5 to 1.5
- group_first: float32 [8, 512], P('tensor', 'dp'), may hold values from -32 to 32
- group_second: float32 [8, 512], P('tensor', 'dp'), may hold values from 53.248 to 819.2
Outputs:
- layer_out: float32 [8192, 2048], P('dp')
- token_grad: float32 [8192, 2048], P('dp')
- qk_first_new: float32 [2, 2048, 2048], P(None, 'dp', 'tensor')
- qk_second_new: float32 [2, 2048, 2048], P(None, 'dp', 'tensor')
- qk_weight_new: float32 [2, 2048, 2048], P(None, 'dp', 'tensor')
- inner_first_new: float32 [4, 2048, 4096], P(None, 'dp', 'tensor')
- inner_second_new: float32 [4, 2048, 4096], P(None, 'dp', 'tensor')
- inner_weight_new: float32 [4, 2048, 4096], P(None, 'dp', 'tensor')
- outer_first_new: float32 [2, 2048, 4096], P(None, 'dp', 'tensor')
- outer_second_new: float32 [2, 2048, 4096], P(None, 'dp', 'tensor')
- outer_weight_new: float32 [2, 2048, 4096], P(None, 'dp', 'tensor')
- norm_first_new: float32 [4, 2048], P(None, 'dp')
- norm_second_new: float32 [4, 2048], P(None, 'dp')
- norm_params_new: float32 [4, 2048], P(None, 'dp')
- group_first_new: float32 [8, 512], P('tensor', 'dp')
- group_second_new: float32 [8, 512], P('tensor', 'dp')
- group_gain_new: float32 [8, 512], P('tensor', 'dp')
The draws below stay inside these ranges and needn't reach their ends.
Inputs may be any that keep to these rules, and one draw needn't show every extreme that they name: Row b holds the lengths of the sequences packed in order into block b of 1024 rows; a row sums to at most 1024, and rows past that sum are padding. Empty slots have length 0. Some block holds a single sequence of 1024 rows.
All inputs are finite; a program needn't handle non-finite values.
Results may differ from the reference program's by a relative error of at most 0.014.
The reference program's roundings to bfloat16 on the way count: a program that leaves them out, or rounds other values in their place, can miss the bound.
Values may be sent and summed in bfloat16 or wider, within the bound.
A program may use at most 320 MiB of HBM per device.

```python
import math
import jax
import jax.numpy as jnp
from jax import lax

D = 2048
HEADS = 8
QK = 2048
FF = 4096
KH = 256
VH = 512
CAP = 1024
SLOTS = 4
STEP = 10
TOKENS = 8192


def draw_lengths(key, part):
    key = jax.random.fold_in(key, 5)
    devices_count = TOKENS // CAP
    jitter_key, cut_key = jax.random.split(key)
    device_index = jnp.arange(devices_count, dtype=jnp.int32)
    base_fill = CAP // 3 + (CAP - CAP // 3) * device_index // max(devices_count - 1, 1)
    jitter = jax.random.randint(jitter_key, (devices_count,), 0, CAP // 8 + 1, dtype=jnp.int32)
    totals = jnp.clip(base_fill - jitter, 1, CAP).astype(jnp.int32)
    cuts = jax.random.randint(cut_key, (devices_count, SLOTS - 1), 0, totals[:, None] + 1, dtype=jnp.int32)
    cuts = jnp.sort(cuts, axis=1)
    edges = jnp.concatenate([jnp.zeros((devices_count, 1), jnp.int32), cuts, totals[:, None]], axis=1)
    spans = edges[:, 1:] - edges[:, :-1]
    single = jnp.zeros((devices_count, SLOTS), jnp.int32).at[:, 0].set(CAP)
    return jnp.where((device_index == devices_count - 1)[:, None], single, spans).astype(jnp.int32)


def draw_norm_params(key, part):
    key = jax.random.fold_in(key, 11)
    noise = jax.random.normal(key, (4, D), jnp.float32)
    is_gain = (jnp.arange(4) % 2 == 0)[:, None]
    return jnp.where(is_gain, 1.0 + 0.1 * noise, 0.2 * noise)


def strengthened(entries, stream_key, source, target, parts, factor):
    def block_of(axis_at):
        return (jnp.arange(entries.shape[axis_at]) // (entries.shape[axis_at] // parts)).reshape((-1,) + (1,) * (entries.ndim - 1 - axis_at))

    first = jax.random.permutation(stream_key, parts)[block_of(target)]
    far = (block_of(target) + parts // 2) % parts
    return jnp.where((block_of(source) == first) | (block_of(source) == far), factor * entries, entries)


def levels(key, shape, cuts, low, largest):
    factor_of, own = 1.0, jax.random.fold_in(key, 6)
    for dim, parts in cuts:
        steps = jnp.exp(jax.random.uniform(jax.random.fold_in(own, dim), (parts,), jnp.float32, low / len(cuts), largest / len(cuts)))
        factor_of = factor_of * jnp.repeat(steps, shape[dim] // parts).reshape([-1 if axis == dim else 1 for axis in range(len(shape))])
    return factor_of


def scatter_about(rng, shape, spread, bound, pieces=(), kind=jnp.bfloat16):
    result = jax.random.normal(rng, shape, jnp.float32) * spread
    if len(pieces) > 0:
        result = levels(rng, shape, pieces, -0.22, 0.18) * result
    return jnp.clip(result, min=-bound, max=bound).astype(kind)


def noise_with(own_key, extent, spread, bound, shards, heavy, kind=jnp.bfloat16):
    drawn = spread * jax.random.normal(own_key, extent, jnp.float32)
    if shards:
        drawn = drawn * levels(own_key, extent, shards, -0.22, 0.18)
    return jnp.clip(strengthened(drawn, jax.random.fold_in(own_key, 3), *heavy), -bound, bound).astype(kind)


def setup_inputs(seed: int = 0) -> dict:
    key_list = jax.random.split(jax.random.key(seed), 19)
    return {
        "tokens": noise_with(key_list[0], (TOKENS, D), 1.0, 6.0, ((0, 8),), (0, 1, 8, 2.0)),
        "lengths": draw_lengths(jax.random.fold_in(key_list[18], 71), 0),
        "cotangent": noise_with(key_list[2], (TOKENS, D), 1.0, 6.0, ((0, 8),), (0, 1, 8, 2.0)),
        "qk_weight": scatter_about(key_list[3], (2, D, QK), D ** -0.5, 0.125, ((1, 8), (2, 4)), jnp.float32),
        "qk_first": scatter_about(key_list[4], (2, D, QK), (0.05 * TOKENS ** 0.5), 28.0, ((1, 8), (2, 4)), jnp.float32),
        "qk_second": jnp.clip(jnp.exp(math.log(655.36) - 2.7725887 * jax.random.uniform(key_list[5], (2, D, QK), jnp.float32) ** levels(key_list[5], (2, D, QK), ((1, 8), (2, 4)), -0.2, 0.2)), 40.96, 655.36),
        "inner_weight": scatter_about(key_list[6], (4, D, FF), D ** -0.5, 0.125, ((1, 8), (2, 4)), jnp.float32),
        "inner_first": scatter_about(key_list[7], (4, D, FF), (0.045 * TOKENS ** 0.5), 24.0, ((1, 8), (2, 4)), jnp.float32),
        "inner_second": jnp.clip(jnp.exp(math.log(573.44) - 2.8622008 * jax.random.uniform(key_list[8], (4, D, FF), jnp.float32) ** levels(key_list[8], (4, D, FF), ((1, 8), (2, 4)), -0.2, 0.2)), 32.768, 573.44),
        "outer_weight": scatter_about(key_list[9], (2, D, FF), FF ** -0.5, 0.09375, ((1, 8), (2, 4)), jnp.float32),
        "outer_first": scatter_about(key_list[10], (2, D, FF), (0.045 * TOKENS ** 0.5), 24.0, ((1, 8), (2, 4)), jnp.float32),
        "outer_second": jnp.clip(jnp.exp(math.log(573.44) - 2.8622008 * jax.random.uniform(key_list[11], (2, D, FF), jnp.float32) ** levels(key_list[11], (2, D, FF), ((1, 8), (2, 4)), -0.2, 0.2)), 32.768, 573.44),
        "norm_params": draw_norm_params(jax.random.fold_in(key_list[18], 71), 0),
        "norm_first": scatter_about(key_list[13], (4, D), (0.055 * TOKENS ** 0.5), 32.0, ((1, 8),), jnp.float32),
        "norm_second": jnp.clip(jnp.exp(math.log(819.2) - 2.733368 * jax.random.uniform(key_list[14], (4, D), jnp.float32) ** levels(key_list[14], (4, D), ((1, 8),), -0.2, 0.2)), 53.248, 819.2),
        "group_gain": jnp.clip(1.0 + 0.1 * jax.random.normal(key_list[15], (HEADS, VH), jnp.float32), 0.5, 1.5),
        "group_first": scatter_about(key_list[16], (HEADS, VH), (0.055 * TOKENS ** 0.5), 32.0, ((0, 4), (1, 8)), jnp.float32),
        "group_second": jnp.clip(jnp.exp(math.log(819.2) - 2.733368 * jax.random.uniform(key_list[17], (HEADS, VH), jnp.float32) ** levels(key_list[17], (HEADS, VH), ((0, 4), (1, 8)), -0.2, 0.2)), 53.248, 819.2),
    }


NORM_EPS = 1e-05
GROUP_EPS = 1.0
BETA_FIRST = 0.9
BETA_SECOND = 0.95
ADAM_EPS = 1e-08
MATRIX_RATE = 0.05
VECTOR_RATE = 0.5
WEIGHT_DECAY = 0.1

@jax.custom_vjp
def low(v):
    return lax.optimization_barrier(v.astype(jnp.bfloat16)).astype(jnp.float32)

@jax.custom_vjp
def low_back(v):
    return v

def low_keep(v):
    return (low(v), None)

def low_pass(kept, grad):
    return (grad,)

def back_keep(v):
    return (v, None)

def back_low(kept, grad):
    return (low(grad),)
low.defvjp(low_keep, low_pass)
low_back.defvjp(back_keep, back_low)

def matmul(left, right):
    return jnp.dot(left, right, precision=lax.Precision.HIGHEST, preferred_element_type=jnp.float32)

def matmul_turned(left, right):
    return lax.dot_general(left, right, (((1,), (1,)), ((), ())), precision=lax.Precision.HIGHEST, preferred_element_type=jnp.float32)

def layer_norm(values, gain_row, shift_row, epsilon):
    center = values - lax.optimization_barrier(jnp.mean(values, axis=-1, keepdims=True))
    inverse = lax.rsqrt(lax.optimization_barrier(jnp.mean(center * center, axis=-1, keepdims=True)) + epsilon)
    return center * inverse * gain_row + shift_row

def sequence_layout(lengths_row, capacity):
    lengths_row = lengths_row.astype(jnp.int32)
    seq_ends = jnp.cumsum(lengths_row).astype(jnp.int32)
    row_index = jnp.arange(capacity, dtype=jnp.int32)
    sequence_id = lax.optimization_barrier(jnp.sum((row_index[:, None] >= seq_ends[None, :]).astype(jnp.int32), axis=1)).astype(jnp.int32)
    starts = (seq_ends - lengths_row).astype(jnp.int32)
    slot_index = jnp.arange(lengths_row.shape[0], dtype=jnp.int32)
    row_start = lax.optimization_barrier(jnp.sum(jnp.where(sequence_id[:, None] == slot_index[None, :], starts[None, :], 0), axis=1)).astype(jnp.int32)
    position = (row_index - row_start).astype(jnp.int32)
    live_rows = row_index < seq_ends[-1]
    return (row_index, sequence_id, position, live_rows)

def decay_table(row_index, sequence_id, live_rows, head_ids):
    allowed = (sequence_id[:, None] == sequence_id[None, :]) & (row_index[:, None] >= row_index[None, :]) & live_rows[:, None] & live_rows[None, :]
    distance = jnp.maximum(row_index[:, None] - row_index[None, :], 0).astype(jnp.float32)
    log_keep = jnp.log1p(-jnp.exp2(-(5.0 + head_ids.astype(jnp.float32))))
    return jnp.where(allowed[None], jnp.exp(distance[None] * log_keep[:, None, None]), 0.0)

def rotation_tables(position, head_size):
    half_size = head_size // 2
    frequency = jnp.exp(-math.log(10000.0) * 2.0 * jnp.arange(half_size, dtype=jnp.float32) / head_size)
    angles = position.astype(jnp.float32)[:, None] * frequency[None, :]
    return (jnp.cos(angles), jnp.sin(angles))

def rotate(values, cosine, sine, head_size):
    row_count = values.shape[0]
    shaped = values.reshape(row_count, -1, 2, head_size // 2)
    front_half = shaped[:, :, 0]
    back_half = shaped[:, :, 1]
    cos_rows = cosine[:, None, :]
    sin_rows = sine[:, None, :]
    turned = jnp.stack([front_half * cos_rows - back_half * sin_rows, front_half * sin_rows + back_half * cos_rows], axis=2)
    return turned.reshape(row_count, -1)

def block_forward(params, inputs, lengths_row):
    qk_w, inner_w, outer_w, norm_w, group_w = params
    capacity = inputs.shape[0]
    row_index, sequence_id, position, live_rows = sequence_layout(lengths_row, capacity)
    cosine, sine = rotation_tables(position, KH)
    decay = decay_table(row_index, sequence_id, live_rows, jnp.arange(HEADS, dtype=jnp.int32))
    first_low = low(layer_norm(inputs, norm_w[0], norm_w[1], NORM_EPS))
    query_proj = low_back(matmul(first_low, qk_w[0]))
    key_proj = low_back(matmul(first_low, qk_w[1]))
    values = low(low_back(matmul(first_low, inner_w[0]))).reshape(capacity, HEADS, VH)
    gate_proj = low_back(matmul(first_low, inner_w[1]))
    queries = low(rotate(query_proj, cosine, sine, KH)).reshape(capacity, HEADS, KH)
    keys_low = low(rotate(key_proj, cosine, sine, KH) * KH ** (-0.5)).reshape(capacity, HEADS, KH)
    scores = low_back(jnp.einsum('nhk,mhk->hnm', queries, keys_low, precision=lax.Precision.HIGHEST))
    weights_low = low(scores * decay)
    retained = low_back(jnp.einsum('hnm,mhv->nhv', weights_low, values, precision=lax.Precision.HIGHEST))
    group_out = layer_norm(retained, group_w, 0.0, GROUP_EPS)
    gated = low(jax.nn.silu(gate_proj) * group_out.reshape(capacity, -1))
    middle = inputs + low_back(matmul_turned(gated, outer_w[0]))
    second_low = low(layer_norm(middle, norm_w[2], norm_w[3], NORM_EPS))
    up_left = low_back(matmul(second_low, inner_w[2]))
    up_right = low_back(matmul(second_low, inner_w[3]))
    hidden = low(jax.nn.gelu(up_left, approximate=False) * up_right)
    return middle + low_back(matmul_turned(hidden, outer_w[1]))

def adam_update(weight, gradient, moment, square, rate, decay_rate):
    moment_new = BETA_FIRST * moment + (1.0 - BETA_FIRST) * gradient
    square_new = BETA_SECOND * square + (1.0 - BETA_SECOND) * gradient * gradient
    first_hat = moment_new / (1.0 - BETA_FIRST ** STEP)
    second_hat = square_new / (1.0 - BETA_SECOND ** STEP)
    weight_new = weight - rate * (first_hat / (jnp.sqrt(second_hat) + ADAM_EPS) + decay_rate * weight)
    return (moment_new, square_new, weight_new)

def reference(tokens, lengths, cotangent, qk_weight, qk_first, qk_second, inner_weight, inner_first, inner_second, outer_weight, outer_first, outer_second, norm_params, norm_first, norm_second, group_gain, group_first, group_second):
    float_params = (qk_weight, inner_weight, outer_weight, norm_params, group_gain)
    inputs = tokens.astype(jnp.float32).reshape(-1, CAP, D)
    live_mask = jnp.arange(CAP, dtype=jnp.int32)[None, :] < lax.optimization_barrier(jnp.sum(lengths, axis=1)).astype(jnp.int32)[:, None]
    grad_top = cotangent.astype(jnp.float32).reshape(-1, CAP, D) * live_mask[:, :, None].astype(jnp.float32)

    def whole(params, blocks):
        working = tuple((low(member) for member in params))
        checked = jax.checkpoint(block_forward)

        def advance(carried, block_pair):
            return (carried, checked(working, block_pair[0], block_pair[1]))
        unused, results = lax.scan(advance, jnp.zeros((), jnp.float32), (blocks, lengths))
        return results
    layer_blocks, pullback = jax.vjp(whole, float_params, inputs)
    param_grads, input_grads = pullback(grad_top)
    qk_m, qk_s, qk_w = adam_update(qk_weight, param_grads[0], qk_first, qk_second, MATRIX_RATE, WEIGHT_DECAY)
    inner_m, inner_s, inner_w = adam_update(inner_weight, param_grads[1], inner_first, inner_second, MATRIX_RATE, WEIGHT_DECAY)
    outer_m, outer_s, outer_w = adam_update(outer_weight, param_grads[2], outer_first, outer_second, MATRIX_RATE, WEIGHT_DECAY)
    norm_m, norm_s, norm_w = adam_update(norm_params, param_grads[3], norm_first, norm_second, VECTOR_RATE, 0.0)
    group_m, group_s, group_w = adam_update(group_gain, param_grads[4], group_first, group_second, VECTOR_RATE, 0.0)
    return (layer_blocks.reshape(-1, D), input_grads.reshape(-1, D), qk_m, qk_s, qk_w, inner_m, inner_s, inner_w, outer_m, outer_s, outer_w, norm_m, norm_s, norm_w, group_m, group_s, group_w)
```

```python
import functools
import math

import jax
import jax.numpy as jnp
from jax import lax
from jax.experimental import pallas as pl
from jax.experimental.pallas import tpu as pltpu
from jax.sharding import PartitionSpec as P

MESH = pl.DeviceIdType.MESH

KH = 256
VH = 512
SLOTS = 4
STEP = 10


NORM_EPS = 1e-05
GROUP_EPS = 1.0
BETA_FIRST = 0.9
BETA_SECOND = 0.95
ADAM_EPS = 1e-08
MATRIX_RATE = 0.05
VECTOR_RATE = 0.5
WEIGHT_DECAY = 0.1


def layer_norm(values, gain_row, shift_row, epsilon):
    center = values - jnp.mean(values, axis=-1, keepdims=True)
    inverse = lax.rsqrt(jnp.mean(center * center, axis=-1, keepdims=True) + epsilon)
    normed = center * inverse
    return (normed * gain_row + shift_row, normed, inverse)


def norm_back(upstream, normed, inverse, gain_row):
    scaled = upstream * gain_row
    plain_mean = jnp.mean(scaled, axis=-1, keepdims=True)
    cross_mean = jnp.mean(scaled * normed, axis=-1, keepdims=True)
    result = inverse * (scaled - plain_mean - normed * cross_mean)
    return (result, jnp.sum(upstream * normed, axis=0), jnp.sum(upstream, axis=0))


def sequence_layout(lengths_row, capacity):
    seq_ends = jnp.cumsum(lengths_row)
    row_index = jnp.arange(capacity, dtype=jnp.int32)
    sequence_id = jnp.sum((row_index[:, None] >= seq_ends[None, :]).astype(jnp.int32), axis=1)
    starts = seq_ends - lengths_row
    slot_index = jnp.arange(lengths_row.shape[0], dtype=jnp.int32)
    row_start = jnp.sum(
        jnp.where(sequence_id[:, None] == slot_index[None, :], starts[None, :], 0), axis=1
    )
    position = row_index - row_start
    live_rows = row_index < seq_ends[-1]
    return (row_index, sequence_id, position, live_rows)


def decay_table(row_index, sequence_id, live_rows, head_ids):
    allowed = (
        (sequence_id[:, None] == sequence_id[None, :])
        & (row_index[:, None] >= row_index[None, :])
        & live_rows[:, None]
        & live_rows[None, :]
    )
    distance = jnp.maximum(row_index[:, None] - row_index[None, :], 0).astype(jnp.float32)
    log_keep = jnp.log1p(-jnp.exp2(-(5.0 + head_ids.astype(jnp.float32))))
    return jnp.where(allowed[None], jnp.exp(distance[None] * log_keep[:, None, None]), 0.0)


def rotation_tables(position, head_size):
    half_size = head_size // 2
    frequency = jnp.exp(
        -math.log(10000.0) * 2.0 * jnp.arange(half_size, dtype=jnp.float32) / head_size
    )
    angles = position.astype(jnp.float32)[:, None] * frequency[None, :]
    return (jnp.cos(angles), jnp.sin(angles))


def rotate(values, cosine, sine, head_size):
    row_count = values.shape[0]
    shaped = values.reshape(row_count, -1, 2, head_size // 2)
    front_half = shaped[:, :, 0]
    back_half = shaped[:, :, 1]
    cos_rows = cosine[:, None, :]
    sin_rows = sine[:, None, :]
    turned = jnp.stack(
        [
            front_half * cos_rows - back_half * sin_rows,
            front_half * sin_rows + back_half * cos_rows,
        ],
        axis=2,
    )
    return turned.reshape(row_count, -1)


def row_product(left, right):
    return jnp.dot(left, right, preferred_element_type=jnp.float32)


def turned_product(left, right):
    return lax.dot_general(
        left, right, (((1,), (1,)), ((), ())), preferred_element_type=jnp.float32
    )


def outer_product(left, right):
    return lax.dot_general(
        left, right, (((0,), (0,)), ((), ())), preferred_element_type=jnp.float32
    )


def adam_update(weight, gradient, moment, square, rate, decay_rate):
    moment_new = BETA_FIRST * moment + (1.0 - BETA_FIRST) * gradient
    square_new = BETA_SECOND * square + (1.0 - BETA_SECOND) * gradient * gradient
    first_hat = moment_new / (1.0 - BETA_FIRST**STEP)
    second_hat = square_new / (1.0 - BETA_SECOND**STEP)
    weight_new = weight - rate * (
        first_hat / (jnp.sqrt(second_hat) + ADAM_EPS) + decay_rate * weight
    )
    return (moment_new, square_new, weight_new)


def zsum_kernel(count, rows, lag_own, lag_fwd, *refs):
    sources = refs[:count]
    (
        total,
        mine,
        from_left,
        from_right,
        stage_sem,
        left_sem,
        right_sem,
        done_sem,
        relay_sem,
        down_sem,
        up_sem,
    ) = refs[count:]
    pairs = total.shape[0] // (2 * rows)
    me = lax.axis_index("tensor")
    stages, start = [], 0
    for index, source in enumerate(sources):
        place = mine.at[pl.ds(start, source.shape[0])]
        stages.append(pltpu.make_async_copy(source, place, stage_sem.at[index]))
        start += source.shape[0]
    for stage in stages:
        stage.start()
    barrier = pltpu.get_barrier_semaphore()

    @pl.when(me > 0)
    def _():
        pl.semaphore_signal(barrier, inc=1, device_id={"tensor": me - 1}, device_id_type=MESH)

    @pl.when(me < 3)
    def _():
        pl.semaphore_signal(barrier, inc=1, device_id={"tensor": me + 1}, device_id_type=MESH)

    @pl.when((me == 0) | (me == 3))
    def _():
        pl.semaphore_wait(barrier, 1)

    @pl.when((me == 1) | (me == 2))
    def _():
        pl.semaphore_wait(barrier, 2)

    for stage in stages:
        stage.wait()

    def at(chunk):
        return pl.ds(pl.multiple_of(chunk * rows, rows), rows)

    def send(source, target, chunk, send_sem, recv_sem, device):
        return pltpu.make_async_remote_copy(
            source.at[at(chunk)],
            target.at[at(chunk)],
            send_sem.at[chunk],
            recv_sem.at[chunk],
            device_id={"tensor": device},
            device_id_type=MESH,
        )

    def add_right(chunk, source):
        return send(source, from_left, chunk, relay_sem, left_sem, me + 1)

    def add_left(chunk, source):
        return send(source, from_right, chunk, relay_sem, right_sem, me - 1)

    def give_right(chunk):
        return send(total, total, chunk, up_sem, done_sem, me + 1)

    def give_left(chunk):
        return send(total, total, chunk, down_sem, done_sem, me - 1)

    def wide(ref, chunk):
        return ref[at(chunk), :].astype(jnp.float32)

    def relay(pair):
        first, second = 2 * pair, 2 * pair + 1

        @pl.when(me == 0)
        def _():
            add_right(second, mine).start()
            add_right(first, mine).start()

        @pl.when(me == 3)
        def _():
            add_left(first, mine).start()
            add_left(second, mine).start()

        @pl.when(me == 1)
        def _():
            add_right(second, mine).wait_recv()
            from_left[at(second), :] = (wide(from_left, second) + wide(mine, second)).astype(
                jnp.bfloat16
            )
            add_right(second, from_left).start()

        @pl.when(me == 2)
        def _():
            add_left(first, mine).wait_recv()
            from_right[at(first), :] = (wide(from_right, first) + wide(mine, first)).astype(
                jnp.bfloat16
            )
            add_left(first, from_right).start()

    def finish(chunk):
        add_right(chunk, mine).wait_recv()
        add_left(chunk, mine).wait_recv()
        total[at(chunk), :] = (
            wide(from_left, chunk) + wide(mine, chunk) + wide(from_right, chunk)
        ).astype(jnp.bfloat16)
        give_right(chunk).start()
        give_left(chunk).start()

    def own(pair):
        @pl.when(me == 1)
        def _():
            finish(2 * pair)

        @pl.when(me == 2)
        def _():
            finish(2 * pair + 1)

    def forward(pair):
        @pl.when(me == 1)
        def _():
            give_left(2 * pair + 1).wait_recv()
            give_left(2 * pair + 1).start()

        @pl.when(me == 2)
        def _():
            give_right(2 * pair).wait_recv()
            give_right(2 * pair).start()

    def step(index, carry):
        @pl.when(index < pairs)
        def _():
            relay(index)

        @pl.when((index >= lag_own) & (index < pairs + lag_own))
        def _():
            own(index - lag_own)

        @pl.when(index >= lag_fwd)
        def _():
            forward(index - lag_fwd)

        return carry

    lax.fori_loop(0, pairs + lag_fwd, step, 0)

    def drain(pair, carry):
        first, second = 2 * pair, 2 * pair + 1

        @pl.when(me == 0)
        def _():
            add_right(second, mine).wait_send()
            add_right(first, mine).wait_send()
            give_left(first).wait_recv()
            give_left(second).wait_recv()

        @pl.when(me == 3)
        def _():
            add_left(first, mine).wait_send()
            add_left(second, mine).wait_send()
            give_right(first).wait_recv()
            give_right(second).wait_recv()

        @pl.when(me == 1)
        def _():
            add_right(second, from_left).wait_send()
            give_left(first).wait_send()
            give_right(first).wait_send()
            give_left(second).wait_send()

        @pl.when(me == 2)
        def _():
            add_left(first, from_right).wait_send()
            give_left(second).wait_send()
            give_right(second).wait_send()
            give_right(first).wait_send()

        return carry

    lax.fori_loop(0, pairs, drain, 0)


def zsum(parts, collective_id, rows=32, lag_own=1, lag_fwd=3):
    heights = [part.shape[0] for part in parts]
    height, width = sum(heights), parts[0].shape[1]
    count, chunks = len(parts), height // rows
    buffer = pltpu.VMEM((height, width), jnp.bfloat16)
    total = pl.pallas_call(
        functools.partial(zsum_kernel, count, rows, lag_own, lag_fwd),
        out_shape=jax.ShapeDtypeStruct((height, width), jnp.bfloat16),
        in_specs=[pl.BlockSpec(memory_space=pl.ANY)] * count,
        out_specs=pl.BlockSpec(memory_space=pltpu.VMEM),
        scratch_shapes=[buffer] * 3
        + [pltpu.SemaphoreType.DMA((count,))]
        + [pltpu.SemaphoreType.DMA((chunks,))] * 6,
        compiler_params=pltpu.CompilerParams(
            collective_id=collective_id, has_side_effects=True, vmem_limit_bytes=48 << 20
        ),
        cost_estimate=pl.CostEstimate(
            flops=100_000_000 * height, bytes_accessed=8 << 20, transcendentals=0
        ),
    )(*parts)
    return jnp.split(total, [sum(heights[:index]) for index in range(1, count)])


def turn(values, cosine, sine):
    half = values.shape[1] // 2
    front, back = values[:, :half], values[:, half:]
    return jnp.concatenate([front * cosine - back * sine, front * sine + back * cosine], axis=1)


def decay_block(ends_ref, log_keep, row_start, col_start, size):
    rows = row_start + lax.broadcasted_iota(jnp.int32, (size, 1), 0)
    cols = col_start + lax.broadcasted_iota(jnp.int32, (1, size), 1)
    row_slot = jnp.zeros((size, 1), jnp.int32)
    col_slot = jnp.zeros((1, size), jnp.int32)
    for slot in range(SLOTS):
        row_slot += (rows >= ends_ref[slot]).astype(jnp.int32)
        col_slot += (cols >= ends_ref[slot]).astype(jnp.int32)
    row_slot = jnp.where(rows < ends_ref[SLOTS - 1], row_slot, -1)
    distance = rows - cols
    allowed = (row_slot == col_slot) & (distance >= 0)
    distance = jnp.maximum(distance, 0).astype(jnp.float32)
    return jnp.where(allowed, jnp.exp(distance * log_keep), 0.0)


def group_stats(values):
    center = values - jnp.mean(values, axis=-1, keepdims=True)
    inverse = lax.rsqrt(jnp.mean(center * center, axis=-1, keepdims=True) + GROUP_EPS)
    return center * inverse, inverse


def retain_kernel(
    ends_ref,
    keep_ref,
    first_ref,
    query_w_ref,
    key_w_ref,
    value_w_ref,
    gate_w_ref,
    cos_ref,
    sin_ref,
    gain_ref,
    query_ref,
    key_ref,
    value_ref,
    gate_ref,
    retained_ref,
    gated_ref,
    keys,
    values,
):
    head, block = pl.program_id(0), pl.program_id(1)
    size = query_ref.shape[0]
    here = pl.ds(pl.multiple_of(block * size, size), size)
    first = first_ref[here, :]
    cosine, sine = cos_ref[here, :], sin_ref[here, :]
    query = turn(row_product(first, query_w_ref[...]), cosine, sine).astype(jnp.bfloat16)
    key = turn(row_product(first, key_w_ref[...]), cosine, sine) * KH ** (-0.5)
    key = key.astype(jnp.bfloat16)
    value = row_product(first, value_w_ref[...]).astype(jnp.bfloat16)
    gate = row_product(first, gate_w_ref[...])
    query_ref[...] = query
    key_ref[...] = key
    value_ref[...] = value
    gate_ref[...] = gate
    keys[here, :] = key
    values[here, :] = value
    retained_ref[...] = jnp.zeros_like(retained_ref)

    def visit(other, carry):
        there = pl.ds(pl.multiple_of(other * size, size), size)
        decay = decay_block(ends_ref, keep_ref[head], block * size, other * size, size)
        weights = (turned_product(query, keys[there, :]) * decay).astype(jnp.bfloat16)
        retained_ref[...] += row_product(weights, values[there, :])
        return carry

    lax.fori_loop(0, block + 1, visit, 0)
    normed, inverse = group_stats(retained_ref[...])
    gated_ref[...] = (gate * jax.nn.sigmoid(gate) * (normed * gain_ref[0])).astype(jnp.bfloat16)


def retain(ends, log_keep, first_low, full, cosine, sine, group_values, size=256):
    capacity, width = first_low.shape
    heads = group_values.shape[0]
    scalar = pl.BlockSpec(memory_space=pltpu.SMEM)
    table = pl.BlockSpec((capacity, KH // 2), lambda h, r: (0, 0))
    key_block = pl.BlockSpec((size, KH), lambda h, r: (r, h))
    value_block = pl.BlockSpec((size, VH), lambda h, r: (r, h))
    ratio = KH * heads * 2 // VH

    def shape(columns, kind):
        return jax.ShapeDtypeStruct((capacity, heads * columns), kind)

    return pl.pallas_call(
        retain_kernel,
        grid=(heads, capacity // size),
        out_shape=(
            shape(KH, jnp.bfloat16),
            shape(KH, jnp.bfloat16),
            shape(VH, jnp.bfloat16),
            shape(VH, jnp.float32),
            shape(VH, jnp.float32),
            shape(VH, jnp.bfloat16),
        ),
        in_specs=[
            scalar,
            scalar,
            pl.BlockSpec((capacity, width), lambda h, r: (0, 0)),
            pl.BlockSpec((width, KH), lambda h, r: (0, h)),
            pl.BlockSpec((width, KH), lambda h, r: (0, heads + h)),
            pl.BlockSpec((width, VH), lambda h, r: (0, ratio + h)),
            pl.BlockSpec((width, VH), lambda h, r: (0, ratio + heads + h)),
            table,
            table,
            pl.BlockSpec((1, 1, VH), lambda h, r: (h, 0, 0)),
        ],
        out_specs=(key_block, key_block, value_block, value_block, value_block, value_block),
        scratch_shapes=[
            pltpu.VMEM((capacity, KH), jnp.bfloat16),
            pltpu.VMEM((capacity, VH), jnp.bfloat16),
        ],
        compiler_params=pltpu.CompilerParams(vmem_limit_bytes=52 << 20),
        cost_estimate=pl.CostEstimate(
            flops=16_000_000_000, bytes_accessed=40 << 20, transcendentals=0
        ),
    )(ends, log_keep, first_low, full, full, full, full, cosine, sine, group_values[:, None, :])


def retain_back_kernel(
    ends_ref,
    keep_ref,
    middle_ref,
    out_w_ref,
    retained_ref,
    gate_ref,
    gain_ref,
    query_ref,
    key_ref,
    value_ref,
    cos_ref,
    sin_ref,
    grad_ref,
    gain_grad_ref,
    query_grad,
    key_grad,
    value_grad,
):
    head, block = pl.program_id(0), pl.program_id(1)
    heads, blocks = pl.num_programs(0), pl.num_programs(1)
    size = retained_ref.shape[0]
    here = pl.ds(pl.multiple_of(block * size, size), size)

    def columns(start, width):
        return pl.ds(pl.multiple_of(start, 128), width)

    @pl.when(block == 0)
    def _():
        key_grad[...] = jnp.zeros_like(key_grad)
        value_grad[...] = jnp.zeros_like(value_grad)
        gain_grad_ref[...] = jnp.zeros_like(gain_grad_ref)

    normed, inverse = group_stats(retained_ref[...])
    gain = gain_ref[0]
    gate = gate_ref[...]
    sigmoid = jax.nn.sigmoid(gate)
    grad_gated = row_product(middle_ref[here, :], out_w_ref[...])
    slope = sigmoid * (1.0 + gate * (1.0 - sigmoid))
    gate_start = heads * (2 * KH + VH) + head * VH
    grad_ref[here, columns(gate_start, VH)] = (grad_gated * (normed * gain) * slope).astype(
        jnp.bfloat16
    )
    grad_out = grad_gated * (gate * sigmoid)
    gain_grad_ref[0] += jnp.sum(grad_out * normed, axis=0, keepdims=True)
    scaled = grad_out * gain
    plain_mean = jnp.mean(scaled, axis=-1, keepdims=True)
    cross_mean = jnp.mean(scaled * normed, axis=-1, keepdims=True)
    upstream = (inverse * (scaled - plain_mean - normed * cross_mean)).astype(jnp.bfloat16)
    query = query_ref[here, :]
    query_grad[...] = jnp.zeros_like(query_grad)

    def visit(other, carry):
        there = pl.ds(pl.multiple_of(other * size, size), size)
        decay = decay_block(ends_ref, keep_ref[head], block * size, other * size, size)
        key = key_ref[there, :]
        weights = (turned_product(query, key) * decay).astype(jnp.bfloat16)
        value_grad[there, :] += outer_product(weights, upstream)
        scores = (turned_product(upstream, value_ref[there, :]) * decay).astype(jnp.bfloat16)
        query_grad[...] += row_product(scores, key)
        key_grad[there, :] += outer_product(scores, query)
        return carry

    lax.fori_loop(0, block + 1, visit, 0)
    cosine, sine = cos_ref[here, :], sin_ref[here, :]
    grad_ref[here, columns(head * KH, KH)] = turn(query_grad[...], cosine, -sine).astype(
        jnp.bfloat16
    )

    @pl.when(block == blocks - 1)
    def _():
        key_turned = turn(key_grad[...] * KH ** (-0.5), cos_ref[...], -sin_ref[...])
        grad_ref[:, columns((heads + head) * KH, KH)] = key_turned.astype(jnp.bfloat16)
        grad_ref[:, columns(heads * 2 * KH + head * VH, VH)] = value_grad[...].astype(jnp.bfloat16)


def retain_back(
    ends, log_keep, middle_low, mix_out, retained, gate, group_values, query, key, value, cosine, sine, size=256
):
    capacity, width = middle_low.shape
    heads = group_values.shape[0]
    total = heads * 2 * (KH + VH)
    scalar = pl.BlockSpec(memory_space=pltpu.SMEM)
    table = pl.BlockSpec((capacity, KH // 2), lambda h, r: (0, 0))
    value_block = pl.BlockSpec((size, VH), lambda h, r: (r, h))
    key_rows = pl.BlockSpec((capacity, KH), lambda h, r: (0, h))
    gain_block = pl.BlockSpec((1, 1, VH), lambda h, r: (h, 0, 0))
    return pl.pallas_call(
        retain_back_kernel,
        grid=(heads, capacity // size),
        out_shape=(
            jax.ShapeDtypeStruct((capacity, total), jnp.bfloat16),
            jax.ShapeDtypeStruct((heads, 1, VH), jnp.float32),
        ),
        in_specs=[
            scalar,
            scalar,
            pl.BlockSpec((capacity, width), lambda h, r: (0, 0)),
            pl.BlockSpec((width, VH), lambda h, r: (0, h)),
            value_block,
            value_block,
            gain_block,
            key_rows,
            key_rows,
            pl.BlockSpec((capacity, VH), lambda h, r: (0, h)),
            table,
            table,
        ],
        out_specs=(pl.BlockSpec((capacity, total), lambda h, r: (0, 0)), gain_block),
        scratch_shapes=[
            pltpu.VMEM((size, KH), jnp.float32),
            pltpu.VMEM((capacity, KH), jnp.float32),
            pltpu.VMEM((capacity, VH), jnp.float32),
        ],
        compiler_params=pltpu.CompilerParams(vmem_limit_bytes=52 << 20),
        cost_estimate=pl.CostEstimate(
            flops=20_000_000_000, bytes_accessed=40 << 20, transcendentals=0
        ),
    )(ends, log_keep, middle_low, mix_out, retained, gate, group_values[:, None, :], query, key, value, cosine, sine)


def local(
    tokens,
    lengths,
    cotangent,
    qk_weight,
    qk_first,
    qk_second,
    inner_weight,
    inner_first,
    inner_second,
    outer_weight,
    outer_first,
    outer_second,
    norm_params,
    norm_first,
    norm_second,
    group_gain,
    group_first,
    group_second,
):
    capacity = tokens.shape[0]
    local_heads = group_gain.shape[0]
    low = jnp.bfloat16
    tensor_index, data_index = lax.axis_index("tensor"), lax.axis_index("dp")

    def gather(shards):
        shard = jnp.concatenate([part.astype(low) for part in shards], axis=1)
        return lax.all_gather(shard, "dp", axis=0, tiled=True)

    def scatter(grad):
        return lax.psum_scatter(grad, "dp", scatter_dimension=0, tiled=True)

    norm_cols, group_cols = norm_params.shape[1], group_gain.shape[1]
    small = lax.all_gather(
        jnp.concatenate([norm_params.reshape(-1), group_gain.reshape(-1)]).astype(low), "dp"
    ).astype(jnp.float32)
    ways = small.shape[0]
    norm_values = small[:, : 4 * norm_cols].reshape(ways, 4, norm_cols)
    norm_values = norm_values.transpose(1, 0, 2).reshape(4, -1)
    group_values = small[:, 4 * norm_cols :].reshape(ways, local_heads, group_cols)
    group_values = group_values.transpose(1, 0, 2).reshape(local_heads, -1)
    first_full = gather([qk_weight[0], qk_weight[1], inner_weight[0], inner_weight[1]])
    mix_out = gather([outer_weight[0]])
    mlp_full = gather([inner_weight[2], inner_weight[3]])
    mlp_out = gather([outer_weight[1]])
    row_index, sequence_id, position, live_rows = sequence_layout(lengths[0], capacity)
    cosine, sine = rotation_tables(position, KH)
    ends = jnp.cumsum(lengths[0])
    head_ids = tensor_index * local_heads + jnp.arange(local_heads, dtype=jnp.int32)
    log_keep = jnp.log1p(-jnp.exp2(-(5.0 + head_ids.astype(jnp.float32))))
    inputs = tokens.astype(jnp.float32)
    first_out, first_normed, first_inverse = layer_norm(
        inputs, norm_values[0], norm_values[1], NORM_EPS
    )
    first_low = first_out.astype(low)
    query, key, value, gate, retained, gated = retain(
        ends, log_keep, first_low, first_full, cosine, sine, group_values
    )
    middle = inputs + zsum([turned_product(gated, mix_out).astype(low)], 0)[0].astype(jnp.float32)
    second_out, second_normed, second_inverse = layer_norm(
        middle, norm_values[2], norm_values[3], NORM_EPS
    )
    second_low = second_out.astype(low)
    up = row_product(second_low, mlp_full)
    up_cols = up.shape[1] // 2
    up_left, up_right = up[:, :up_cols], up[:, up_cols:]
    normal_cdf = 0.5 * (1.0 + lax.erf(up_left * (1.0 / math.sqrt(2.0))))
    normal_pdf = jnp.exp(-0.5 * up_left * up_left) * (1.0 / math.sqrt(2.0 * math.pi))
    gelu_left = up_left * normal_cdf
    hidden = (gelu_left * up_right).astype(low)
    grad_top = cotangent.astype(jnp.float32) * live_rows.astype(jnp.float32)[:, None]
    top_low = grad_top.astype(low)
    grad_hidden = row_product(top_low, mlp_out)
    left_low = (grad_hidden * up_right * (normal_cdf + up_left * normal_pdf)).astype(low)
    right_low = (grad_hidden * gelu_left).astype(low)
    pair_low = jnp.concatenate([left_low, right_low], axis=1)
    back_second = turned_product(pair_low, mlp_full).astype(low)
    branch = turned_product(hidden, mlp_out).astype(low)
    mlp_out_grad = outer_product(top_low, hidden).astype(low)
    mlp_grad = outer_product(second_low, pair_low).astype(low)
    back_second, branch, mlp_out_grad, mlp_grad = lax.optimization_barrier(
        (back_second, branch, mlp_out_grad, mlp_grad)
    )
    mlp_out_grad = scatter(mlp_out_grad)
    mlp_grad = scatter(mlp_grad)
    back_second = zsum([back_second], 1)[0].astype(jnp.float32)
    grad_middle_norm, grad_gain_two, grad_shift_two = norm_back(
        back_second, second_normed, second_inverse, norm_values[2]
    )
    grad_middle = grad_top + grad_middle_norm
    middle_low = grad_middle.astype(low)
    middle_low, mlp_out_grad, mlp_grad = lax.optimization_barrier(
        (middle_low, mlp_out_grad, mlp_grad)
    )
    half = capacity // 2
    branch_head = lax.psum(branch[:half], "tensor")
    first_back, grad_group_gain = retain_back(
        ends,
        log_keep,
        middle_low,
        mix_out,
        retained,
        gate,
        group_values,
        query,
        key,
        value,
        cosine,
        sine,
    )
    grad_group_gain = grad_group_gain[:, 0, :]
    mix_out_grad = outer_product(middle_low, gated).astype(low)
    first_grad = outer_product(first_low, first_back).astype(low)
    back_first = turned_product(first_back, first_full)
    back_first = back_first.astype(low)
    back_first, branch_head, mix_out_grad, first_grad = lax.optimization_barrier(
        (back_first, branch_head, mix_out_grad, first_grad)
    )
    mix_out_grad = scatter(mix_out_grad)
    first_grad = scatter(first_grad)
    back_first, branch_tail = zsum([back_first, branch[half:]], 2)
    back_first = back_first.astype(jnp.float32)
    layer_out = middle + jnp.concatenate([branch_head, branch_tail], axis=0).astype(jnp.float32)
    grad_input_norm, grad_gain_one, grad_shift_one = norm_back(
        back_first, first_normed, first_inverse, norm_values[0]
    )
    token_grad = grad_middle + grad_input_norm
    norm_grad = jnp.stack([grad_gain_one, grad_shift_one, grad_gain_two, grad_shift_two])
    small_grad = jnp.concatenate(
        [
            norm_grad.reshape(4, ways, norm_cols).transpose(1, 0, 2).reshape(ways, -1),
            grad_group_gain.reshape(local_heads, ways, group_cols)
            .transpose(1, 0, 2)
            .reshape(ways, -1),
        ],
        axis=1,
    )
    small_grad = scatter(small_grad).reshape(-1)
    norm_grad = small_grad[: 4 * norm_cols].reshape(4, norm_cols)
    group_grad = small_grad[4 * norm_cols :].reshape(local_heads, group_cols)
    qk_cols, mix_cols = local_heads * KH, local_heads * VH
    starts = [qk_cols, 2 * qk_cols, 2 * qk_cols + mix_cols]
    query_grad, key_grad, value_grad, gate_grad = jnp.split(first_grad, starts, axis=1)
    qk_grad = jnp.stack([query_grad, key_grad]).astype(jnp.float32)
    inner_grad = jnp.stack([value_grad, gate_grad, mlp_grad[:, :up_cols], mlp_grad[:, up_cols:]]).astype(jnp.float32)
    outer_grad = jnp.stack([mix_out_grad, mlp_out_grad]).astype(jnp.float32)
    qk_new = adam_update(qk_weight, qk_grad, qk_first, qk_second, MATRIX_RATE, WEIGHT_DECAY)
    inner_new = adam_update(
        inner_weight, inner_grad, inner_first, inner_second, MATRIX_RATE, WEIGHT_DECAY
    )
    outer_new = adam_update(
        outer_weight, outer_grad, outer_first, outer_second, MATRIX_RATE, WEIGHT_DECAY
    )
    norm_new = adam_update(norm_params, norm_grad, norm_first, norm_second, VECTOR_RATE, 0.0)
    group_new = adam_update(group_gain, group_grad, group_first, group_second, VECTOR_RATE, 0.0)
    return (layer_out, token_grad, *qk_new, *inner_new, *outer_new, *norm_new, *group_new)


def solution(mesh):
    in_specs = (
        P("dp", None),
        P("dp", None),
        P("dp", None),
        P(None, "dp", "tensor"),
        P(None, "dp", "tensor"),
        P(None, "dp", "tensor"),
        P(None, "dp", "tensor"),
        P(None, "dp", "tensor"),
        P(None, "dp", "tensor"),
        P(None, "dp", "tensor"),
        P(None, "dp", "tensor"),
        P(None, "dp", "tensor"),
        P(None, "dp"),
        P(None, "dp"),
        P(None, "dp"),
        P("tensor", "dp"),
        P("tensor", "dp"),
        P("tensor", "dp"),
    )
    out_specs = (
        P("dp", None),
        P("dp", None),
        P(None, "dp", "tensor"),
        P(None, "dp", "tensor"),
        P(None, "dp", "tensor"),
        P(None, "dp", "tensor"),
        P(None, "dp", "tensor"),
        P(None, "dp", "tensor"),
        P(None, "dp", "tensor"),
        P(None, "dp", "tensor"),
        P(None, "dp", "tensor"),
        P(None, "dp"),
        P(None, "dp"),
        P(None, "dp"),
        P("tensor", "dp"),
        P("tensor", "dp"),
        P("tensor", "dp"),
    )
    return jax.shard_map(local, mesh=mesh, in_specs=in_specs, out_specs=out_specs, check_vma=False)
```

```python
import functools
import math

import jax
import jax.numpy as jnp
from jax import lax
from jax.experimental import pallas as pl
from jax.experimental.pallas import tpu as pltpu
from jax.sharding import PartitionSpec as P

MESH = pl.DeviceIdType.MESH

KH = 256
VH = 512
SLOTS = 4
STEP = 10


NORM_EPS = 1e-05
GROUP_EPS = 1.0
BETA_FIRST = 0.9
BETA_SECOND = 0.95
ADAM_EPS = 1e-08
MATRIX_RATE = 0.05
VECTOR_RATE = 0.5
WEIGHT_DECAY = 0.1


def layer_norm(values, gain_row, shift_row, epsilon):
    center = values - jnp.mean(values, axis=-1, keepdims=True)
    inverse = lax.rsqrt(jnp.mean(center * center, axis=-1, keepdims=True) + epsilon)
    normed = center * inverse
    return (normed * gain_row + shift_row, normed, inverse)


def norm_back(upstream, normed, inverse, gain_row):
    scaled = upstream * gain_row
    plain_mean = jnp.mean(scaled, axis=-1, keepdims=True)
    cross_mean = jnp.mean(scaled * normed, axis=-1, keepdims=True)
    result = inverse * (scaled - plain_mean - normed * cross_mean)
    return (result, jnp.sum(upstream * normed, axis=0), jnp.sum(upstream, axis=0))


def sequence_layout(lengths_row, capacity):
    seq_ends = jnp.cumsum(lengths_row)
    row_index = jnp.arange(capacity, dtype=jnp.int32)
    sequence_id = jnp.sum((row_index[:, None] >= seq_ends[None, :]).astype(jnp.int32), axis=1)
    starts = seq_ends - lengths_row
    slot_index = jnp.arange(lengths_row.shape[0], dtype=jnp.int32)
    row_start = jnp.sum(
        jnp.where(sequence_id[:, None] == slot_index[None, :], starts[None, :], 0), axis=1
    )
    position = row_index - row_start
    live_rows = row_index < seq_ends[-1]
    return (row_index, sequence_id, position, live_rows)


def decay_table(row_index, sequence_id, live_rows, head_ids):
    allowed = (
        (sequence_id[:, None] == sequence_id[None, :])
        & (row_index[:, None] >= row_index[None, :])
        & live_rows[:, None]
        & live_rows[None, :]
    )
    distance = jnp.maximum(row_index[:, None] - row_index[None, :], 0).astype(jnp.float32)
    log_keep = jnp.log1p(-jnp.exp2(-(5.0 + head_ids.astype(jnp.float32))))
    return jnp.where(allowed[None], jnp.exp(distance[None] * log_keep[:, None, None]), 0.0)


def rotation_tables(position, head_size):
    half_size = head_size // 2
    frequency = jnp.exp(
        -math.log(10000.0) * 2.0 * jnp.arange(half_size, dtype=jnp.float32) / head_size
    )
    angles = position.astype(jnp.float32)[:, None] * frequency[None, :]
    return (jnp.cos(angles), jnp.sin(angles))


def rotate(values, cosine, sine, head_size):
    row_count = values.shape[0]
    shaped = values.reshape(row_count, -1, 2, head_size // 2)
    front_half = shaped[:, :, 0]
    back_half = shaped[:, :, 1]
    cos_rows = cosine[:, None, :]
    sin_rows = sine[:, None, :]
    turned = jnp.stack(
        [
            front_half * cos_rows - back_half * sin_rows,
            front_half * sin_rows + back_half * cos_rows,
        ],
        axis=2,
    )
    return turned.reshape(row_count, -1)


def row_product(left, right):
    return jnp.dot(left, right, preferred_element_type=jnp.float32)


def turned_product(left, right):
    return lax.dot_general(
        left, right, (((1,), (1,)), ((), ())), preferred_element_type=jnp.float32
    )


def outer_product(left, right):
    return lax.dot_general(
        left, right, (((0,), (0,)), ((), ())), preferred_element_type=jnp.float32
    )


def adam_update(weight, gradient, moment, square, rate, decay_rate):
    moment_new = BETA_FIRST * moment + (1.0 - BETA_FIRST) * gradient
    square_new = BETA_SECOND * square + (1.0 - BETA_SECOND) * gradient * gradient
    first_hat = moment_new / (1.0 - BETA_FIRST**STEP)
    second_hat = square_new / (1.0 - BETA_SECOND**STEP)
    weight_new = weight - rate * (
        first_hat / (jnp.sqrt(second_hat) + ADAM_EPS) + decay_rate * weight
    )
    return (moment_new, square_new, weight_new)


class Ring:
    def __init__(self, count, results, recv_sem, send_sem):
        self.count, self.results, self.recv_sem, self.send_sem = count, results, recv_sem, send_sem
        me = lax.axis_index("dp")
        self.me, self.place = me, self.swap(me)
        self.right, self.left = self.owner(1), self.owner(-1)
        self.reach = count // 2

    def swap(self, index):
        if self.count != 8:
            return index
        return jnp.where(index < 4, index, jnp.where(index < 6, index + 2, index - 2))

    def owner(self, distance):
        return self.swap(lax.rem(self.place + distance + self.count, self.count))

    def copies(self, owner, half, way):
        made = []
        for index, result in enumerate(self.results):
            rows = result.shape[0] // (2 * self.count)
            here = result.at[pl.ds(pl.multiple_of((owner * 2 + half) * rows, rows), rows)]
            made.append(
                pltpu.make_async_remote_copy(
                    here,
                    here,
                    self.send_sem.at[((way * 2 + half) * len(self.results) + index) * self.count + owner],
                    self.recv_sem.at[(half * len(self.results) + index) * self.count + owner],
                    device_id={"dp": self.left if way else self.right},
                    device_id_type=MESH,
                )
            )
        return made

    def streams(self):
        for half in range(2):
            for way in range(2):
                yield half, way, self.reach - (half + way) % 2

    def step(self, distance):
        for half, way, hops in self.streams():
            owner = self.owner(distance if way else -distance)

            @pl.when((distance >= 1) & (distance <= hops))
            def _():
                for copy in self.copies(owner, half, way):
                    copy.wait_recv()

            @pl.when(distance < hops)
            def _():
                for copy in self.copies(owner, half, way):
                    copy.start()

    def drain(self):
        for half, way, hops in self.streams():

            def one(distance, carry):
                for copy in self.copies(self.owner(distance if way else -distance), half, way):
                    copy.wait_send()
                return carry

            lax.fori_loop(0, hops, one, 0)


def ring_scratch(count, results):
    return [
        pltpu.SemaphoreType.DMA((2 * results * count,)),
        pltpu.SemaphoreType.DMA((4 * results * count,)),
    ]


class Line:
    def __init__(self, rows, mine, near, far, total, near_sem, far_sem, done_sem, out_sem, cross_sem, give_sem):
        self.rows, self.mine, self.near, self.far, self.total = rows, mine, near, far, total
        self.near_sem, self.far_sem, self.done_sem = near_sem, far_sem, done_sem
        self.out_sem, self.cross_sem, self.give_sem = out_sem, cross_sem, give_sem
        me = lax.axis_index("tensor")
        self.me = me
        self.inner = (me == 1) | (me == 2)
        self.outer = (me == 0) | (me == 3)
        self.relay_to = jnp.where(self.inner, 3 - me, 1 + me // 3)
        self.away = jnp.where(self.inner, 3 * (me - 1), 1 + me // 3)
        owner = jnp.where(self.inner, me, 1 + me // 3)
        self.kept, self.passed = owner - 1, 2 - owner

    def at(self, chunk):
        return pl.ds(pl.multiple_of(chunk * self.rows, self.rows), self.rows)

    def greet(self, also=()):
        barrier = pltpu.get_barrier_semaphore()
        for device in also:
            pl.semaphore_signal(barrier, inc=1, device_id={"dp": device}, device_id_type=MESH)
        pl.semaphore_signal(barrier, inc=1, device_id={"tensor": self.away}, device_id_type=MESH)

        @pl.when(self.inner)
        def _():
            pl.semaphore_signal(
                barrier, inc=1, device_id={"tensor": self.relay_to}, device_id_type=MESH
            )
            pl.semaphore_wait(barrier, 2 + len(also))

        @pl.when(self.outer)
        def _():
            pl.semaphore_wait(barrier, 1 + len(also))

    def copy(self, source, target, send_sem, recv_sem, device):
        return pltpu.make_async_remote_copy(
            source, target, send_sem, recv_sem, device_id={"tensor": device}, device_id_type=MESH
        )

    def send_in(self, chunk):
        return self.copy(
            self.mine.at[self.at(chunk)],
            self.near.at[self.at(chunk)],
            self.out_sem.at[chunk],
            self.near_sem.at[chunk],
            self.away,
        )

    def send_across(self, pair, chunk):
        return self.copy(
            self.near.at[self.at(chunk)],
            self.far.at[self.at(pair)],
            self.out_sem.at[chunk],
            self.far_sem.at[pair],
            self.relay_to,
        )

    def give(self, chunk, send_sem, device):
        place = self.total.at[self.at(chunk)]
        return self.copy(place, place, send_sem, self.done_sem.at[chunk], device)

    def give_out(self, chunk):
        return self.give(chunk, self.give_sem.at[chunk], self.away)

    def give_across(self, pair, chunk):
        return self.give(chunk, self.cross_sem.at[pair], self.relay_to)

    def wide(self, ref, chunk):
        return ref[self.at(chunk), :].astype(jnp.float32)

    def relay(self, pair):
        passed, kept = 2 * pair + self.passed, 2 * pair + self.kept

        @pl.when(self.outer)
        def _():
            self.send_in(passed).start()
            self.send_in(kept).start()

        @pl.when(self.inner)
        def _():
            self.send_in(passed).wait_recv()
            added = self.wide(self.near, passed) + self.wide(self.mine, passed)
            self.near[self.at(passed), :] = added.astype(jnp.bfloat16)
            self.send_across(pair, passed).start()

    def own(self, pair):
        kept = 2 * pair + self.kept

        @pl.when(self.inner)
        def _():
            self.send_in(kept).wait_recv()
            self.send_across(pair, kept).wait_recv()
            added = self.wide(self.near, kept) + self.wide(self.mine, kept)
            added = added + self.wide(self.far, pair)
            self.total[self.at(kept), :] = added.astype(jnp.bfloat16)
            self.give_across(pair, kept).start()
            self.give_out(kept).start()

    def forward(self, pair):
        passed = 2 * pair + self.passed

        @pl.when(self.inner)
        def _():
            self.give_out(passed).wait_recv()
            self.give_out(passed).start()

    def step(self, index, pairs):
        @pl.when(index < pairs)
        def _():
            self.relay(index)

        @pl.when((index >= 1) & (index < pairs + 1))
        def _():
            self.own(index - 1)

        @pl.when((index >= 3) & (index < pairs + 3))
        def _():
            self.forward(index - 3)

    def arrive(self, pair):
        @pl.when(self.outer)
        def _():
            self.give_out(2 * pair).wait_recv()
            self.give_out(2 * pair + 1).wait_recv()

    def drain(self, pair):
        passed, kept = 2 * pair + self.passed, 2 * pair + self.kept
        self.send_in(passed).wait_send()

        @pl.when(self.outer)
        def _():
            self.send_in(kept).wait_send()

        @pl.when(self.inner)
        def _():
            self.give_across(pair, kept).wait_send()
            self.give_out(kept).wait_send()
            self.give_out(passed).wait_send()


def line_scratch(height, width, rows):
    chunks = height // rows
    wide = pltpu.VMEM((height, width), jnp.bfloat16)
    sems, half_sems = pltpu.SemaphoreType.DMA((chunks,)), pltpu.SemaphoreType.DMA((chunks // 2,))
    return [
        wide,
        wide,
        pltpu.VMEM((height // 2, width), jnp.bfloat16),
        sems,
        half_sems,
        sems,
        sems,
        half_sems,
        sems,
    ]


def zsum_kernel(count, rows, *refs):
    sources = refs[:count]
    (total, mine, near, far, near_sem, far_sem, done_sem, out_sem, cross_sem, give_sem, stage_sem) = refs[count:]
    pairs = total.shape[0] // (2 * rows)
    stages, start = [], 0
    for index, source in enumerate(sources):
        place = mine.at[pl.ds(start, source.shape[0])]
        stages.append(pltpu.make_async_copy(source, place, stage_sem.at[index]))
        start += source.shape[0]
    for stage in stages:
        stage.start()
    line = Line(rows, mine, near, far, total, near_sem, far_sem, done_sem, out_sem, cross_sem, give_sem)
    line.greet()
    for stage in stages:
        stage.wait()

    def step(index, carry):
        line.step(index, pairs)
        return carry

    lax.fori_loop(0, pairs + 3, step, 0)

    def drain(pair, carry):
        line.arrive(pair)
        line.drain(pair)
        return carry

    lax.fori_loop(0, pairs, drain, 0)


def zsum(parts, collective_id, rows=32):
    heights = [part.shape[0] for part in parts]
    height, width = sum(heights), parts[0].shape[1]
    count = len(parts)
    total = pl.pallas_call(
        functools.partial(zsum_kernel, count, rows),
        out_shape=jax.ShapeDtypeStruct((height, width), jnp.bfloat16),
        in_specs=[pl.BlockSpec(memory_space=pl.ANY)] * count,
        out_specs=pl.BlockSpec(memory_space=pltpu.VMEM),
        scratch_shapes=line_scratch(height, width, rows) + [pltpu.SemaphoreType.DMA((count,))],
        compiler_params=pltpu.CompilerParams(
            collective_id=collective_id, has_side_effects=True, vmem_limit_bytes=52 << 20
        ),
        cost_estimate=pl.CostEstimate(
            flops=100_000_000 * height, bytes_accessed=8 << 20, transcendentals=0
        ),
    )(*parts)
    return jnp.split(total, [sum(heights[:index]) for index in range(1, count)])


def middle_kernel(
    rows,
    block,
    branch_ref,
    tokens_ref,
    top_ref,
    gain_ref,
    shift_ref,
    mlp_ref,
    out_w_ref,
    total,
    second_ref,
    hidden_ref,
    pair_ref,
    leave_ref,
    mine,
    near,
    far,
    near_sem,
    far_sem,
    done_sem,
    out_sem,
    cross_sem,
    give_sem,
    mlp_w,
    out_w,
    token_buf,
    top_buf,
    second_buf,
    hidden_buf,
    pair_buf,
    leave_buf,
    load_sem,
    store_sem,
    ring_recv_sem,
    ring_send_sem,
):
    capacity, width = branch_ref.shape
    units = hidden_buf.shape[1]
    ways = width // mlp_ref.shape[0]
    ring = Ring(ways, (mlp_w, out_w), ring_recv_sem, ring_send_sem)
    blocks = capacity // block
    per = block // (2 * rows)
    pairs = 2 * capacity // (2 * rows)
    low = jnp.bfloat16
    line = Line(rows, mine, near, far, total, near_sem, far_sem, done_sem, out_sem, cross_sem, give_sem)

    def part(index):
        return pl.ds(pl.multiple_of(index * block, block), block)

    def load_tokens(index):
        return pltpu.make_async_copy(tokens_ref.at[part(index)], token_buf, load_sem.at[3])

    def load_top(index):
        return pltpu.make_async_copy(top_ref.at[part(index)], top_buf, load_sem.at[4])

    def store(buffer, target, index, place):
        return pltpu.make_async_copy(buffer, target.at[part(index)], store_sem.at[place])

    load_mine = pltpu.make_async_copy(branch_ref, mine.at[pl.ds(0, capacity)], load_sem.at[0])
    shard = pl.ds(pl.multiple_of(ring.me * mlp_ref.shape[0], mlp_ref.shape[0]), mlp_ref.shape[0])
    load_mlp = pltpu.make_async_copy(mlp_ref, mlp_w.at[shard], load_sem.at[1])
    load_out = pltpu.make_async_copy(out_w_ref, out_w.at[shard], load_sem.at[2])
    load_mlp.start()
    load_out.start()
    load_mine.start()
    line.greet((ring.left, ring.right))
    load_mlp.wait()
    load_out.wait()
    load_mine.wait()
    load_tokens(0).start()
    load_top(0).start()

    def normalize(index):
        def wait(pair, carry):
            line.arrive(pair)
            return carry

        lax.fori_loop(index * per, index * per + per, wait, 0)
        load_tokens(index).wait()

        @pl.when(index > 0)
        def _():
            store(second_buf, second_ref, index - 1, 0).wait()

        def normalize_rows(piece, carry):
            here = pl.ds(pl.multiple_of(piece * 32, 32), 32)
            there = pl.ds(pl.multiple_of(index * block + piece * 32, 32), 32)
            values = token_buf[here, :].astype(jnp.float32) + total[there, :].astype(jnp.float32)
            values, unused_normed, unused_inverse = layer_norm(
                values, gain_ref[...], shift_ref[...], NORM_EPS
            )
            second_buf[here, :] = values.astype(low)
            return carry

        lax.fori_loop(0, block // 32, normalize_rows, 0)
        store(second_buf, second_ref, index, 0).start()

        @pl.when(index < blocks - 1)
        def _():
            load_tokens(index + 1).start()

    def units_step(index, start, count):
        @pl.when(start == 0)
        def _():
            load_top(index).wait()

            @pl.when(index > 0)
            def _():
                store(hidden_buf, hidden_ref, index - 1, 1).wait()
                store(pair_buf, pair_ref, index - 1, 2).wait()

        def one(number, carry):
            first = pl.ds(pl.multiple_of(number * 256, 256), 256)
            second = pl.ds(pl.multiple_of(units + number * 256, 256), 256)
            left = row_product(second_buf[...], mlp_w[:, first])
            right = row_product(second_buf[...], mlp_w[:, second])
            back = row_product(top_buf[...], out_w[:, first])
            cdf = 0.5 * (1.0 + lax.erf(left * (1.0 / math.sqrt(2.0))))
            pdf = jnp.exp(-0.5 * left * left) * (1.0 / math.sqrt(2.0 * math.pi))
            gelu = left * cdf
            hidden_buf[:, first] = (gelu * right).astype(low)
            pair_buf[:, first] = (back * right * (cdf + left * pdf)).astype(low)
            pair_buf[:, second] = (back * gelu).astype(low)
            return carry

        lax.fori_loop(start, start + count, one, 0)

    def backward_step(index):
        store(hidden_buf, hidden_ref, index, 1).start()
        store(pair_buf, pair_ref, index, 2).start()

        @pl.when(index < blocks - 1)
        def _():
            load_top(index + 1).start()

        def one(number, carry):
            there = pl.ds(pl.multiple_of(number * 256, 256), 256)
            rows_here = pl.ds(pl.multiple_of(capacity + index * block, block), block)
            mine[rows_here, there] = turned_product(pair_buf[...], mlp_w[there, :]).astype(low)
            return carry

        lax.fori_loop(0, width // 256, one, 0)

    def leave_step(index):
        @pl.when(index > 0)
        def _():
            store(leave_buf, leave_ref, index - 1, 3).wait()

        def one(number, carry):
            there = pl.ds(pl.multiple_of(number * 256, 256), 256)
            leave_buf[:, there] = turned_product(hidden_buf[...], out_w[there, :]).astype(low)
            return carry

        lax.fori_loop(0, width // 256, one, 0)
        store(leave_buf, leave_ref, index, 3).start()

    count = units // 256
    lead = per + 6
    batch = -(-(ring.reach + 1) // (lead // 2))

    def step(index, carry):
        line.step(index, pairs)

        @pl.when((index < lead) & (index % 2 == 0))
        def _():
            for extra in range(batch):
                distance = index // 2 * batch + extra

                @pl.when(distance <= ring.reach)
                def _():
                    ring.step(distance)

        work = index - lead

        @pl.when((work >= 0) & (work < 4 * blocks))
        def _():
            piece, stage = work // 4, work % 4

            @pl.when(stage == 0)
            def _():
                normalize(piece)

            @pl.when((stage == 1) | (stage == 2))
            def _():
                units_step(piece, (stage - 1) * (count // 2), count // 2)

            @pl.when(stage == 3)
            def _():
                backward_step(piece)
                leave_step(piece)

        return carry

    lax.fori_loop(0, pairs + 3, step, 0)

    def arrive(pair, carry):
        line.arrive(pair)
        return carry

    lax.fori_loop(pairs // 2, pairs, arrive, 0)

    def drain(pair, carry):
        line.drain(pair)
        return carry

    lax.fori_loop(0, pairs, drain, 0)
    ring.drain()
    store(second_buf, second_ref, blocks - 1, 0).wait()
    store(hidden_buf, hidden_ref, blocks - 1, 1).wait()
    store(pair_buf, pair_ref, blocks - 1, 2).wait()
    store(leave_buf, leave_ref, blocks - 1, 3).wait()


def middle_stage(
    branch, tokens, top, gain, shift, mlp_shard, out_shard, collective_id, rows=32, block=256
):
    capacity, width = branch.shape
    units = out_shard.shape[1]
    ways = width // out_shard.shape[0]
    low = jnp.bfloat16
    anywhere, held = pl.BlockSpec(memory_space=pl.ANY), pl.BlockSpec(memory_space=pltpu.VMEM)
    total, second, hidden, pair, leave = pl.pallas_call(
        functools.partial(middle_kernel, rows, block),
        out_shape=(
            jax.ShapeDtypeStruct((2 * capacity, width), low),
            jax.ShapeDtypeStruct((capacity, width), low),
            jax.ShapeDtypeStruct((capacity, units), low),
            jax.ShapeDtypeStruct((capacity, 2 * units), low),
            jax.ShapeDtypeStruct((capacity, width), low),
        ),
        in_specs=[anywhere, anywhere, anywhere, held, held, anywhere, anywhere],
        out_specs=(held, anywhere, anywhere, anywhere, anywhere),
        scratch_shapes=line_scratch(2 * capacity, width, rows)
        + [
            pltpu.VMEM((width, 2 * units), low),
            pltpu.VMEM((width, units), low),
            pltpu.VMEM((block, width), low),
            pltpu.VMEM((block, width), low),
            pltpu.VMEM((block, width), low),
            pltpu.VMEM((block, units), low),
            pltpu.VMEM((block, 2 * units), low),
            pltpu.VMEM((block, width), low),
            pltpu.SemaphoreType.DMA((5,)),
            pltpu.SemaphoreType.DMA((4,)),
        ]
        + ring_scratch(ways, 2),
        compiler_params=pltpu.CompilerParams(
            collective_id=collective_id, has_side_effects=True, vmem_limit_bytes=60 << 20
        ),
        cost_estimate=pl.CostEstimate(
            flops=200_000_000_000, bytes_accessed=40 << 20, transcendentals=0
        ),
    )(branch, tokens, top, gain[None], shift[None], mlp_shard, out_shard)
    return total[:capacity], total[capacity:], second, hidden, pair, leave


def turn(values, cosine, sine):
    half = values.shape[1] // 2
    front, back = values[:, :half], values[:, half:]
    return jnp.concatenate([front * cosine - back * sine, front * sine + back * cosine], axis=1)


def decay_block(ends_ref, log_keep, row_start, col_start, size):
    rows = row_start + lax.broadcasted_iota(jnp.int32, (size, 1), 0)
    cols = col_start + lax.broadcasted_iota(jnp.int32, (1, size), 1)
    row_slot = jnp.zeros((size, 1), jnp.int32)
    col_slot = jnp.zeros((1, size), jnp.int32)
    for slot in range(SLOTS):
        row_slot += (rows >= ends_ref[slot]).astype(jnp.int32)
        col_slot += (cols >= ends_ref[slot]).astype(jnp.int32)
    row_slot = jnp.where(rows < ends_ref[SLOTS - 1], row_slot, -1)
    distance = rows - cols
    allowed = (row_slot == col_slot) & (distance >= 0)
    distance = jnp.maximum(distance, 0).astype(jnp.float32)
    return jnp.where(allowed, jnp.exp(distance * log_keep), 0.0)


def group_stats(values):
    center = values - jnp.mean(values, axis=-1, keepdims=True)
    inverse = lax.rsqrt(jnp.mean(center * center, axis=-1, keepdims=True) + GROUP_EPS)
    return center * inverse, inverse


def retain_kernel(
    ends_ref,
    keep_ref,
    first_ref,
    query_w_ref,
    key_w_ref,
    value_w_ref,
    gate_w_ref,
    cos_ref,
    sin_ref,
    gain_ref,
    query_ref,
    key_ref,
    value_ref,
    gate_ref,
    retained_ref,
    gated_ref,
    keys,
    values,
):
    head, block = pl.program_id(0), pl.program_id(1)
    size = query_ref.shape[0]
    here = pl.ds(pl.multiple_of(block * size, size), size)
    first = first_ref[here, :]
    cosine, sine = cos_ref[here, :], sin_ref[here, :]
    query = turn(row_product(first, query_w_ref[...]), cosine, sine).astype(jnp.bfloat16)
    key = turn(row_product(first, key_w_ref[...]), cosine, sine) * KH ** (-0.5)
    key = key.astype(jnp.bfloat16)
    value = row_product(first, value_w_ref[...]).astype(jnp.bfloat16)
    gate = row_product(first, gate_w_ref[...])
    query_ref[...] = query
    key_ref[...] = key
    value_ref[...] = value
    gate_ref[...] = gate
    keys[here, :] = key
    values[here, :] = value
    retained_ref[...] = jnp.zeros_like(retained_ref)

    def visit(other, carry):
        there = pl.ds(pl.multiple_of(other * size, size), size)
        decay = decay_block(ends_ref, keep_ref[head], block * size, other * size, size)
        weights = (turned_product(query, keys[there, :]) * decay).astype(jnp.bfloat16)
        retained_ref[...] += row_product(weights, values[there, :])
        return carry

    lax.fori_loop(0, block + 1, visit, 0)
    normed, inverse = group_stats(retained_ref[...])
    gated_ref[...] = (gate * jax.nn.sigmoid(gate) * (normed * gain_ref[0])).astype(jnp.bfloat16)


def retain(ends, log_keep, first_low, full, cosine, sine, group_values, size=256):
    capacity, width = first_low.shape
    heads = group_values.shape[0]
    scalar = pl.BlockSpec(memory_space=pltpu.SMEM)
    table = pl.BlockSpec((capacity, KH // 2), lambda h, r: (0, 0))
    key_block = pl.BlockSpec((size, KH), lambda h, r: (r, h))
    value_block = pl.BlockSpec((size, VH), lambda h, r: (r, h))
    ratio = KH * heads * 2 // VH

    def shape(columns, kind):
        return jax.ShapeDtypeStruct((capacity, heads * columns), kind)

    return pl.pallas_call(
        retain_kernel,
        grid=(heads, capacity // size),
        out_shape=(
            shape(KH, jnp.bfloat16),
            shape(KH, jnp.bfloat16),
            shape(VH, jnp.bfloat16),
            shape(VH, jnp.float32),
            shape(VH, jnp.float32),
            shape(VH, jnp.bfloat16),
        ),
        in_specs=[
            scalar,
            scalar,
            pl.BlockSpec((capacity, width), lambda h, r: (0, 0)),
            pl.BlockSpec((width, KH), lambda h, r: (0, h)),
            pl.BlockSpec((width, KH), lambda h, r: (0, heads + h)),
            pl.BlockSpec((width, VH), lambda h, r: (0, ratio + h)),
            pl.BlockSpec((width, VH), lambda h, r: (0, ratio + heads + h)),
            table,
            table,
            pl.BlockSpec((1, 1, VH), lambda h, r: (h, 0, 0)),
        ],
        out_specs=(key_block, key_block, value_block, value_block, value_block, value_block),
        scratch_shapes=[
            pltpu.VMEM((capacity, KH), jnp.bfloat16),
            pltpu.VMEM((capacity, VH), jnp.bfloat16),
        ],
        compiler_params=pltpu.CompilerParams(vmem_limit_bytes=52 << 20),
        cost_estimate=pl.CostEstimate(
            flops=16_000_000_000, bytes_accessed=40 << 20, transcendentals=0
        ),
    )(ends, log_keep, first_low, full, full, full, full, cosine, sine, group_values[:, None, :])


def retain_back_kernel(
    ends_ref,
    keep_ref,
    middle_ref,
    out_w_ref,
    retained_ref,
    gate_ref,
    gain_ref,
    query_ref,
    key_ref,
    value_ref,
    cos_ref,
    sin_ref,
    grad_ref,
    gain_grad_ref,
    query_grad,
    key_grad,
    value_grad,
):
    head, block = pl.program_id(0), pl.program_id(1)
    heads, blocks = pl.num_programs(0), pl.num_programs(1)
    size = retained_ref.shape[0]
    here = pl.ds(pl.multiple_of(block * size, size), size)

    def columns(start, width):
        return pl.ds(pl.multiple_of(start, 128), width)

    @pl.when(block == 0)
    def _():
        key_grad[...] = jnp.zeros_like(key_grad)
        value_grad[...] = jnp.zeros_like(value_grad)
        gain_grad_ref[...] = jnp.zeros_like(gain_grad_ref)

    normed, inverse = group_stats(retained_ref[...])
    gain = gain_ref[0]
    gate = gate_ref[...]
    sigmoid = jax.nn.sigmoid(gate)
    grad_gated = row_product(middle_ref[here, :], out_w_ref[...])
    slope = sigmoid * (1.0 + gate * (1.0 - sigmoid))
    gate_start = heads * (2 * KH + VH) + head * VH
    grad_ref[here, columns(gate_start, VH)] = (grad_gated * (normed * gain) * slope).astype(
        jnp.bfloat16
    )
    grad_out = grad_gated * (gate * sigmoid)
    gain_grad_ref[0] += jnp.sum(grad_out * normed, axis=0, keepdims=True)
    scaled = grad_out * gain
    plain_mean = jnp.mean(scaled, axis=-1, keepdims=True)
    cross_mean = jnp.mean(scaled * normed, axis=-1, keepdims=True)
    upstream = (inverse * (scaled - plain_mean - normed * cross_mean)).astype(jnp.bfloat16)
    query = query_ref[here, :]
    query_grad[...] = jnp.zeros_like(query_grad)

    def visit(other, carry):
        there = pl.ds(pl.multiple_of(other * size, size), size)
        decay = decay_block(ends_ref, keep_ref[head], block * size, other * size, size)
        key = key_ref[there, :]
        weights = (turned_product(query, key) * decay).astype(jnp.bfloat16)
        value_grad[there, :] += outer_product(weights, upstream)
        scores = (turned_product(upstream, value_ref[there, :]) * decay).astype(jnp.bfloat16)
        query_grad[...] += row_product(scores, key)
        key_grad[there, :] += outer_product(scores, query)
        return carry

    lax.fori_loop(0, block + 1, visit, 0)
    cosine, sine = cos_ref[here, :], sin_ref[here, :]
    grad_ref[here, columns(head * KH, KH)] = turn(query_grad[...], cosine, -sine).astype(
        jnp.bfloat16
    )

    @pl.when(block == blocks - 1)
    def _():
        key_turned = turn(key_grad[...] * KH ** (-0.5), cos_ref[...], -sin_ref[...])
        grad_ref[:, columns((heads + head) * KH, KH)] = key_turned.astype(jnp.bfloat16)
        grad_ref[:, columns(heads * 2 * KH + head * VH, VH)] = value_grad[...].astype(jnp.bfloat16)


def retain_back(
    ends, log_keep, middle_low, mix_out, retained, gate, group_values, query, key, value, cosine, sine, size=256
):
    capacity, width = middle_low.shape
    heads = group_values.shape[0]
    total = heads * 2 * (KH + VH)
    scalar = pl.BlockSpec(memory_space=pltpu.SMEM)
    table = pl.BlockSpec((capacity, KH // 2), lambda h, r: (0, 0))
    value_block = pl.BlockSpec((size, VH), lambda h, r: (r, h))
    key_rows = pl.BlockSpec((capacity, KH), lambda h, r: (0, h))
    gain_block = pl.BlockSpec((1, 1, VH), lambda h, r: (h, 0, 0))
    return pl.pallas_call(
        retain_back_kernel,
        grid=(heads, capacity // size),
        out_shape=(
            jax.ShapeDtypeStruct((capacity, total), jnp.bfloat16),
            jax.ShapeDtypeStruct((heads, 1, VH), jnp.float32),
        ),
        in_specs=[
            scalar,
            scalar,
            pl.BlockSpec((capacity, width), lambda h, r: (0, 0)),
            pl.BlockSpec((width, VH), lambda h, r: (0, h)),
            value_block,
            value_block,
            gain_block,
            key_rows,
            key_rows,
            pl.BlockSpec((capacity, VH), lambda h, r: (0, h)),
            table,
            table,
        ],
        out_specs=(pl.BlockSpec((capacity, total), lambda h, r: (0, 0)), gain_block),
        scratch_shapes=[
            pltpu.VMEM((size, KH), jnp.float32),
            pltpu.VMEM((capacity, KH), jnp.float32),
            pltpu.VMEM((capacity, VH), jnp.float32),
        ],
        compiler_params=pltpu.CompilerParams(vmem_limit_bytes=52 << 20),
        cost_estimate=pl.CostEstimate(
            flops=20_000_000_000, bytes_accessed=40 << 20, transcendentals=0
        ),
    )(ends, log_keep, middle_low, mix_out, retained, gate, group_values[:, None, :], query, key, value, cosine, sine)


def local(
    tokens,
    lengths,
    cotangent,
    qk_weight,
    qk_first,
    qk_second,
    inner_weight,
    inner_first,
    inner_second,
    outer_weight,
    outer_first,
    outer_second,
    norm_params,
    norm_first,
    norm_second,
    group_gain,
    group_first,
    group_second,
):
    capacity = tokens.shape[0]
    local_heads = group_gain.shape[0]
    low = jnp.bfloat16
    tensor_index, data_index = lax.axis_index("tensor"), lax.axis_index("dp")

    def joined(shards):
        return jnp.concatenate([part.astype(low) for part in shards], axis=1)

    def gather(shards):
        return lax.all_gather(joined(shards), "dp", axis=0, tiled=True)

    def scatter(grad):
        return lax.psum_scatter(grad, "dp", scatter_dimension=0, tiled=True)

    norm_cols, group_cols = norm_params.shape[1], group_gain.shape[1]
    small = lax.all_gather(
        jnp.concatenate([norm_params.reshape(-1), group_gain.reshape(-1)]).astype(low), "dp"
    ).astype(jnp.float32)
    ways = small.shape[0]
    norm_values = small[:, : 4 * norm_cols].reshape(ways, 4, norm_cols)
    norm_values = norm_values.transpose(1, 0, 2).reshape(4, -1)
    group_values = small[:, 4 * norm_cols :].reshape(ways, local_heads, group_cols)
    group_values = group_values.transpose(1, 0, 2).reshape(local_heads, -1)
    first_full = gather([qk_weight[0], qk_weight[1], inner_weight[0], inner_weight[1]])
    mix_out = gather([outer_weight[0]])
    mlp_shard = joined([inner_weight[2], inner_weight[3]])
    out_shard = outer_weight[1].astype(low)
    row_index, sequence_id, position, live_rows = sequence_layout(lengths[0], capacity)
    cosine, sine = rotation_tables(position, KH)
    ends = jnp.cumsum(lengths[0])
    head_ids = tensor_index * local_heads + jnp.arange(local_heads, dtype=jnp.int32)
    log_keep = jnp.log1p(-jnp.exp2(-(5.0 + head_ids.astype(jnp.float32))))
    inputs = tokens.astype(jnp.float32)
    first_out, first_normed, first_inverse = layer_norm(
        inputs, norm_values[0], norm_values[1], NORM_EPS
    )
    first_low = first_out.astype(low)
    query, key, value, gate, retained, gated = retain(
        ends, log_keep, first_low, first_full, cosine, sine, group_values
    )
    grad_top = cotangent.astype(jnp.float32) * live_rows.astype(jnp.float32)[:, None]
    top_low = grad_top.astype(low)
    branch = turned_product(gated, mix_out).astype(low)
    branch_sum, back_second, second_low, hidden, pair_low, branch = middle_stage(
        branch, tokens, top_low, norm_values[2], norm_values[3], mlp_shard, out_shard, 0
    )
    middle = inputs + branch_sum.astype(jnp.float32)
    unused_out, second_normed, second_inverse = layer_norm(
        middle, norm_values[2], norm_values[3], NORM_EPS
    )
    back_second = back_second.astype(jnp.float32)
    up_cols = out_shard.shape[1]
    mlp_out_grad = outer_product(top_low, hidden).astype(low)
    mlp_grad = outer_product(second_low, pair_low).astype(low)
    back_second, mlp_out_grad, mlp_grad = lax.optimization_barrier(
        (back_second, mlp_out_grad, mlp_grad)
    )
    mlp_out_grad = scatter(mlp_out_grad)
    mlp_grad = scatter(mlp_grad)
    grad_middle_norm, grad_gain_two, grad_shift_two = norm_back(
        back_second, second_normed, second_inverse, norm_values[2]
    )
    grad_middle = grad_top + grad_middle_norm
    middle_low = grad_middle.astype(low)
    first_back, grad_group_gain = retain_back(
        ends,
        log_keep,
        middle_low,
        mix_out,
        retained,
        gate,
        group_values,
        query,
        key,
        value,
        cosine,
        sine,
    )
    grad_group_gain = grad_group_gain[:, 0, :]
    mix_out_grad = outer_product(middle_low, gated).astype(low)
    first_grad = outer_product(first_low, first_back).astype(low)
    back_first = turned_product(first_back, first_full)
    back_first = back_first.astype(low)
    back_first, mix_out_grad, first_grad = lax.optimization_barrier(
        (back_first, mix_out_grad, first_grad)
    )
    mix_out_grad = scatter(mix_out_grad)
    first_grad = scatter(first_grad)
    back_first, branch = (part.astype(jnp.float32) for part in zsum([back_first, branch], 1))
    layer_out = middle + branch
    grad_input_norm, grad_gain_one, grad_shift_one = norm_back(
        back_first, first_normed, first_inverse, norm_values[0]
    )
    token_grad = grad_middle + grad_input_norm
    norm_grad = jnp.stack([grad_gain_one, grad_shift_one, grad_gain_two, grad_shift_two])
    small_grad = jnp.concatenate(
        [
            norm_grad.reshape(4, ways, norm_cols).transpose(1, 0, 2).reshape(ways, -1),
            grad_group_gain.reshape(local_heads, ways, group_cols)
            .transpose(1, 0, 2)
            .reshape(ways, -1),
        ],
        axis=1,
    )
    small_grad = scatter(small_grad).reshape(-1)
    norm_grad = small_grad[: 4 * norm_cols].reshape(4, norm_cols)
    group_grad = small_grad[4 * norm_cols :].reshape(local_heads, group_cols)
    qk_cols, mix_cols = local_heads * KH, local_heads * VH
    starts = [qk_cols, 2 * qk_cols, 2 * qk_cols + mix_cols]
    query_grad, key_grad, value_grad, gate_grad = jnp.split(first_grad, starts, axis=1)
    qk_grad = jnp.stack([query_grad, key_grad]).astype(jnp.float32)
    inner_grad = jnp.stack([value_grad, gate_grad, mlp_grad[:, :up_cols], mlp_grad[:, up_cols:]]).astype(jnp.float32)
    outer_grad = jnp.stack([mix_out_grad, mlp_out_grad]).astype(jnp.float32)
    qk_new = adam_update(qk_weight, qk_grad, qk_first, qk_second, MATRIX_RATE, WEIGHT_DECAY)
    inner_new = adam_update(
        inner_weight, inner_grad, inner_first, inner_second, MATRIX_RATE, WEIGHT_DECAY
    )
    outer_new = adam_update(
        outer_weight, outer_grad, outer_first, outer_second, MATRIX_RATE, WEIGHT_DECAY
    )
    norm_new = adam_update(norm_params, norm_grad, norm_first, norm_second, VECTOR_RATE, 0.0)
    group_new = adam_update(group_gain, group_grad, group_first, group_second, VECTOR_RATE, 0.0)
    return (layer_out, token_grad, *qk_new, *inner_new, *outer_new, *norm_new, *group_new)


def solution(mesh):
    in_specs = (
        P("dp", None),
        P("dp", None),
        P("dp", None),
        P(None, "dp", "tensor"),
        P(None, "dp", "tensor"),
        P(None, "dp", "tensor"),
        P(None, "dp", "tensor"),
        P(None, "dp", "tensor"),
        P(None, "dp", "tensor"),
        P(None, "dp", "tensor"),
        P(None, "dp", "tensor"),
        P(None, "dp", "tensor"),
        P(None, "dp"),
        P(None, "dp"),
        P(None, "dp"),
        P("tensor", "dp"),
        P("tensor", "dp"),
        P("tensor", "dp"),
    )
    out_specs = (
        P("dp", None),
        P("dp", None),
        P(None, "dp", "tensor"),
        P(None, "dp", "tensor"),
        P(None, "dp", "tensor"),
        P(None, "dp", "tensor"),
        P(None, "dp", "tensor"),
        P(None, "dp", "tensor"),
        P(None, "dp", "tensor"),
        P(None, "dp", "tensor"),
        P(None, "dp", "tensor"),
        P(None, "dp"),
        P(None, "dp"),
        P(None, "dp"),
        P("tensor", "dp"),
        P("tensor", "dp"),
        P("tensor", "dp"),
    )
    return jax.shard_map(local, mesh=mesh, in_specs=in_specs, out_specs=out_specs, check_vma=False)
```

```python
import functools
import math

import jax
import jax.numpy as jnp
from jax import lax
from jax.experimental import pallas as pl
from jax.experimental.pallas import tpu as pltpu
from jax.sharding import PartitionSpec as P

MESH = pl.DeviceIdType.MESH

KH = 256
VH = 512
SLOTS = 4
STEP = 10


NORM_EPS = 1e-05
GROUP_EPS = 1.0
BETA_FIRST = 0.9
BETA_SECOND = 0.95
ADAM_EPS = 1e-08
MATRIX_RATE = 0.05
VECTOR_RATE = 0.5
WEIGHT_DECAY = 0.1


def layer_norm(values, gain_row, shift_row, epsilon):
    center = values - jnp.mean(values, axis=-1, keepdims=True)
    inverse = lax.rsqrt(jnp.mean(center * center, axis=-1, keepdims=True) + epsilon)
    normed = center * inverse
    return (normed * gain_row + shift_row, normed, inverse)


def norm_back(upstream, normed, inverse, gain_row):
    scaled = upstream * gain_row
    plain_mean = jnp.mean(scaled, axis=-1, keepdims=True)
    cross_mean = jnp.mean(scaled * normed, axis=-1, keepdims=True)
    result = inverse * (scaled - plain_mean - normed * cross_mean)
    return (result, jnp.sum(upstream * normed, axis=0), jnp.sum(upstream, axis=0))


def sequence_layout(lengths_row, capacity):
    seq_ends = jnp.cumsum(lengths_row)
    row_index = jnp.arange(capacity, dtype=jnp.int32)
    sequence_id = jnp.sum((row_index[:, None] >= seq_ends[None, :]).astype(jnp.int32), axis=1)
    starts = seq_ends - lengths_row
    slot_index = jnp.arange(lengths_row.shape[0], dtype=jnp.int32)
    row_start = jnp.sum(
        jnp.where(sequence_id[:, None] == slot_index[None, :], starts[None, :], 0), axis=1
    )
    position = row_index - row_start
    live_rows = row_index < seq_ends[-1]
    return (row_index, sequence_id, position, live_rows)


def decay_table(row_index, sequence_id, live_rows, head_ids):
    allowed = (
        (sequence_id[:, None] == sequence_id[None, :])
        & (row_index[:, None] >= row_index[None, :])
        & live_rows[:, None]
        & live_rows[None, :]
    )
    distance = jnp.maximum(row_index[:, None] - row_index[None, :], 0).astype(jnp.float32)
    log_keep = jnp.log1p(-jnp.exp2(-(5.0 + head_ids.astype(jnp.float32))))
    return jnp.where(allowed[None], jnp.exp(distance[None] * log_keep[:, None, None]), 0.0)


def rotation_tables(position, head_size):
    half_size = head_size // 2
    frequency = jnp.exp(
        -math.log(10000.0) * 2.0 * jnp.arange(half_size, dtype=jnp.float32) / head_size
    )
    angles = position.astype(jnp.float32)[:, None] * frequency[None, :]
    return (jnp.cos(angles), jnp.sin(angles))


def rotate(values, cosine, sine, head_size):
    row_count = values.shape[0]
    shaped = values.reshape(row_count, -1, 2, head_size // 2)
    front_half = shaped[:, :, 0]
    back_half = shaped[:, :, 1]
    cos_rows = cosine[:, None, :]
    sin_rows = sine[:, None, :]
    turned = jnp.stack(
        [
            front_half * cos_rows - back_half * sin_rows,
            front_half * sin_rows + back_half * cos_rows,
        ],
        axis=2,
    )
    return turned.reshape(row_count, -1)


def row_product(left, right):
    return jnp.dot(left, right, preferred_element_type=jnp.float32)


def turned_product(left, right):
    return lax.dot_general(
        left, right, (((1,), (1,)), ((), ())), preferred_element_type=jnp.float32
    )


def outer_product(left, right):
    return lax.dot_general(
        left, right, (((0,), (0,)), ((), ())), preferred_element_type=jnp.float32
    )


def adam_update(weight, gradient, moment, square, rate, decay_rate):
    moment_new = BETA_FIRST * moment + (1.0 - BETA_FIRST) * gradient
    square_new = BETA_SECOND * square + (1.0 - BETA_SECOND) * gradient * gradient
    first_hat = moment_new / (1.0 - BETA_FIRST**STEP)
    second_hat = square_new / (1.0 - BETA_SECOND**STEP)
    weight_new = weight - rate * (
        first_hat / (jnp.sqrt(second_hat) + ADAM_EPS) + decay_rate * weight
    )
    return (moment_new, square_new, weight_new)


class Ring:
    def __init__(self, count, results, recv_sem, send_sem):
        self.count, self.results, self.recv_sem, self.send_sem = count, results, recv_sem, send_sem
        me = lax.axis_index("dp")
        self.me, self.place = me, self.swap(me)
        self.right, self.left = self.owner(1), self.owner(-1)
        self.reach = count // 2

    def swap(self, index):
        if self.count != 8:
            return index
        return jnp.where(index < 4, index, jnp.where(index < 6, index + 2, index - 2))

    def owner(self, distance):
        return self.swap(lax.rem(self.place + distance + self.count, self.count))

    def copies(self, owner, half, way):
        made = []
        for index, result in enumerate(self.results):
            rows = result.shape[0] // (2 * self.count)
            here = result.at[pl.ds(pl.multiple_of((owner * 2 + half) * rows, rows), rows)]
            made.append(
                pltpu.make_async_remote_copy(
                    here,
                    here,
                    self.send_sem.at[((way * 2 + half) * len(self.results) + index) * self.count + owner],
                    self.recv_sem.at[(half * len(self.results) + index) * self.count + owner],
                    device_id={"dp": self.left if way else self.right},
                    device_id_type=MESH,
                )
            )
        return made

    def streams(self):
        for half in range(2):
            for way in range(2):
                yield half, way, self.reach - (half + way) % 2

    def step(self, distance):
        for half, way, hops in self.streams():
            owner = self.owner(distance if way else -distance)

            @pl.when((distance >= 1) & (distance <= hops))
            def _():
                for copy in self.copies(owner, half, way):
                    copy.wait_recv()

            @pl.when(distance < hops)
            def _():
                for copy in self.copies(owner, half, way):
                    copy.start()

    def drain(self):
        for half, way, hops in self.streams():

            def one(distance, carry):
                for copy in self.copies(self.owner(distance if way else -distance), half, way):
                    copy.wait_send()
                return carry

            lax.fori_loop(0, hops, one, 0)


def ring_scratch(count, results):
    return [
        pltpu.SemaphoreType.DMA((2 * results * count,)),
        pltpu.SemaphoreType.DMA((4 * results * count,)),
    ]


class Line:
    def __init__(self, rows, mine, near, far, total, near_sem, far_sem, done_sem, out_sem, cross_sem, give_sem):
        self.rows, self.mine, self.near, self.far, self.total = rows, mine, near, far, total
        self.near_sem, self.far_sem, self.done_sem = near_sem, far_sem, done_sem
        self.out_sem, self.cross_sem, self.give_sem = out_sem, cross_sem, give_sem
        me = lax.axis_index("tensor")
        self.me = me
        self.inner = (me == 1) | (me == 2)
        self.outer = (me == 0) | (me == 3)
        self.relay_to = jnp.where(self.inner, 3 - me, 1 + me // 3)
        self.away = jnp.where(self.inner, 3 * (me - 1), 1 + me // 3)
        owner = jnp.where(self.inner, me, 1 + me // 3)
        self.kept, self.passed = owner - 1, 2 - owner

    def at(self, chunk):
        return pl.ds(pl.multiple_of(chunk * self.rows, self.rows), self.rows)

    def greet(self, also=()):
        barrier = pltpu.get_barrier_semaphore()
        for device in also:
            pl.semaphore_signal(barrier, inc=1, device_id={"dp": device}, device_id_type=MESH)
        pl.semaphore_signal(barrier, inc=1, device_id={"tensor": self.away}, device_id_type=MESH)

        @pl.when(self.inner)
        def _():
            pl.semaphore_signal(
                barrier, inc=1, device_id={"tensor": self.relay_to}, device_id_type=MESH
            )
            pl.semaphore_wait(barrier, 2 + len(also))

        @pl.when(self.outer)
        def _():
            pl.semaphore_wait(barrier, 1 + len(also))

    def copy(self, source, target, send_sem, recv_sem, device):
        return pltpu.make_async_remote_copy(
            source, target, send_sem, recv_sem, device_id={"tensor": device}, device_id_type=MESH
        )

    def send_in(self, chunk):
        return self.copy(
            self.mine.at[self.at(chunk)],
            self.near.at[self.at(chunk)],
            self.out_sem.at[chunk],
            self.near_sem.at[chunk],
            self.away,
        )

    def send_across(self, pair, chunk):
        return self.copy(
            self.near.at[self.at(chunk)],
            self.far.at[self.at(pair)],
            self.out_sem.at[chunk],
            self.far_sem.at[pair],
            self.relay_to,
        )

    def give(self, chunk, send_sem, device):
        place = self.total.at[self.at(chunk)]
        return self.copy(place, place, send_sem, self.done_sem.at[chunk], device)

    def give_out(self, chunk):
        return self.give(chunk, self.give_sem.at[chunk], self.away)

    def give_across(self, pair, chunk):
        return self.give(chunk, self.cross_sem.at[pair], self.relay_to)

    def wide(self, ref, chunk):
        return ref[self.at(chunk), :].astype(jnp.float32)

    def relay(self, pair):
        passed, kept = 2 * pair + self.passed, 2 * pair + self.kept

        @pl.when(self.outer)
        def _():
            self.send_in(passed).start()
            self.send_in(kept).start()

        @pl.when(self.inner)
        def _():
            self.send_in(passed).wait_recv()
            added = self.wide(self.near, passed) + self.wide(self.mine, passed)
            self.near[self.at(passed), :] = added.astype(jnp.bfloat16)
            self.send_across(pair, passed).start()

    def own(self, pair):
        kept = 2 * pair + self.kept

        @pl.when(self.inner)
        def _():
            self.send_in(kept).wait_recv()
            self.send_across(pair, kept).wait_recv()
            added = self.wide(self.near, kept) + self.wide(self.mine, kept)
            added = added + self.wide(self.far, pair)
            self.total[self.at(kept), :] = added.astype(jnp.bfloat16)
            self.give_across(pair, kept).start()
            self.give_out(kept).start()

    def forward(self, pair):
        passed = 2 * pair + self.passed

        @pl.when(self.inner)
        def _():
            self.give_out(passed).wait_recv()
            self.give_out(passed).start()

    def step(self, index, pairs):
        @pl.when(index < pairs)
        def _():
            self.relay(index)

        @pl.when((index >= 1) & (index < pairs + 1))
        def _():
            self.own(index - 1)

        @pl.when((index >= 3) & (index < pairs + 3))
        def _():
            self.forward(index - 3)

    def arrive(self, pair):
        @pl.when(self.outer)
        def _():
            self.give_out(2 * pair).wait_recv()
            self.give_out(2 * pair + 1).wait_recv()

    def drain(self, pair):
        passed, kept = 2 * pair + self.passed, 2 * pair + self.kept
        self.send_in(passed).wait_send()

        @pl.when(self.outer)
        def _():
            self.send_in(kept).wait_send()

        @pl.when(self.inner)
        def _():
            self.give_across(pair, kept).wait_send()
            self.give_out(kept).wait_send()
            self.give_out(passed).wait_send()


def line_scratch(height, width, rows):
    chunks = height // rows
    wide = pltpu.VMEM((height, width), jnp.bfloat16)
    sems, half_sems = pltpu.SemaphoreType.DMA((chunks,)), pltpu.SemaphoreType.DMA((chunks // 2,))
    return [
        wide,
        wide,
        pltpu.VMEM((height // 2, width), jnp.bfloat16),
        sems,
        half_sems,
        sems,
        sems,
        half_sems,
        sems,
    ]


def middle_kernel(
    rows,
    block,
    branch_ref,
    tokens_ref,
    top_ref,
    gain_ref,
    shift_ref,
    mlp_ref,
    out_w_ref,
    total,
    second_ref,
    hidden_ref,
    pair_ref,
    leave_ref,
    mine,
    near,
    far,
    near_sem,
    far_sem,
    done_sem,
    out_sem,
    cross_sem,
    give_sem,
    mlp_w,
    out_w,
    token_buf,
    top_buf,
    second_buf,
    hidden_buf,
    pair_buf,
    leave_buf,
    load_sem,
    store_sem,
    ring_recv_sem,
    ring_send_sem,
):
    capacity, width = branch_ref.shape
    units = hidden_buf.shape[1]
    ways = width // mlp_ref.shape[0]
    ring = Ring(ways, (mlp_w, out_w), ring_recv_sem, ring_send_sem)
    blocks = capacity // block
    per = block // (2 * rows)
    pairs = 2 * capacity // (2 * rows)
    low = jnp.bfloat16
    line = Line(rows, mine, near, far, total, near_sem, far_sem, done_sem, out_sem, cross_sem, give_sem)

    def part(index):
        return pl.ds(pl.multiple_of(index * block, block), block)

    def load_tokens(index):
        return pltpu.make_async_copy(tokens_ref.at[part(index)], token_buf, load_sem.at[3])

    def load_top(index):
        return pltpu.make_async_copy(top_ref.at[part(index)], top_buf, load_sem.at[4])

    def store(buffer, target, index, place):
        return pltpu.make_async_copy(buffer, target.at[part(index)], store_sem.at[place])

    load_mine = pltpu.make_async_copy(branch_ref, mine.at[pl.ds(0, capacity)], load_sem.at[0])
    shard = pl.ds(pl.multiple_of(ring.me * mlp_ref.shape[0], mlp_ref.shape[0]), mlp_ref.shape[0])
    load_mlp = pltpu.make_async_copy(mlp_ref, mlp_w.at[shard], load_sem.at[1])
    load_out = pltpu.make_async_copy(out_w_ref, out_w.at[shard], load_sem.at[2])
    load_mlp.start()
    load_out.start()
    load_mine.start()
    line.greet((ring.left, ring.right))
    load_mlp.wait()
    load_out.wait()
    load_mine.wait()
    load_tokens(0).start()
    load_top(0).start()

    def normalize(index):
        def wait(pair, carry):
            line.arrive(pair)
            return carry

        lax.fori_loop(index * per, index * per + per, wait, 0)
        load_tokens(index).wait()

        @pl.when(index > 0)
        def _():
            store(second_buf, second_ref, index - 1, 0).wait()

        def normalize_rows(piece, carry):
            here = pl.ds(pl.multiple_of(piece * 32, 32), 32)
            there = pl.ds(pl.multiple_of(index * block + piece * 32, 32), 32)
            values = token_buf[here, :].astype(jnp.float32) + total[there, :].astype(jnp.float32)
            values, unused_normed, unused_inverse = layer_norm(
                values, gain_ref[...], shift_ref[...], NORM_EPS
            )
            second_buf[here, :] = values.astype(low)
            return carry

        lax.fori_loop(0, block // 32, normalize_rows, 0)
        store(second_buf, second_ref, index, 0).start()

        @pl.when(index < blocks - 1)
        def _():
            load_tokens(index + 1).start()

    def units_step(index, start, count):
        @pl.when(start == 0)
        def _():
            load_top(index).wait()

            @pl.when(index > 0)
            def _():
                store(hidden_buf, hidden_ref, index - 1, 1).wait()
                store(pair_buf, pair_ref, index - 1, 2).wait()

        def one(number, carry):
            first = pl.ds(pl.multiple_of(number * 256, 256), 256)
            second = pl.ds(pl.multiple_of(units + number * 256, 256), 256)
            left = row_product(second_buf[...], mlp_w[:, first])
            right = row_product(second_buf[...], mlp_w[:, second])
            back = row_product(top_buf[...], out_w[:, first])
            cdf = 0.5 * (1.0 + lax.erf(left * (1.0 / math.sqrt(2.0))))
            pdf = jnp.exp(-0.5 * left * left) * (1.0 / math.sqrt(2.0 * math.pi))
            gelu = left * cdf
            hidden_buf[:, first] = (gelu * right).astype(low)
            pair_buf[:, first] = (back * right * (cdf + left * pdf)).astype(low)
            pair_buf[:, second] = (back * gelu).astype(low)
            return carry

        lax.fori_loop(start, start + count, one, 0)

    def backward_step(index):
        store(hidden_buf, hidden_ref, index, 1).start()
        store(pair_buf, pair_ref, index, 2).start()

        @pl.when(index < blocks - 1)
        def _():
            load_top(index + 1).start()

        def one(number, carry):
            there = pl.ds(pl.multiple_of(number * 256, 256), 256)
            rows_here = pl.ds(pl.multiple_of(capacity + index * block, block), block)
            mine[rows_here, there] = turned_product(pair_buf[...], mlp_w[there, :]).astype(low)
            return carry

        lax.fori_loop(0, width // 256, one, 0)

    def leave_step(index):
        @pl.when(index > 0)
        def _():
            store(leave_buf, leave_ref, index - 1, 3).wait()

        def one(number, carry):
            there = pl.ds(pl.multiple_of(number * 256, 256), 256)
            leave_buf[:, there] = turned_product(hidden_buf[...], out_w[there, :]).astype(low)
            return carry

        lax.fori_loop(0, width // 256, one, 0)
        store(leave_buf, leave_ref, index, 3).start()

    count = units // 256
    lead = per + 6
    batch = -(-ring.reach // (lead // 2 - 1))

    def step(index, carry):
        line.step(index, pairs)

        @pl.when(index == 0)
        def _():
            ring.step(0)

        @pl.when((index > 1) & (index < lead) & (index % 2 == 1))
        def _():
            for extra in range(batch):
                distance = (index - 3) // 2 * batch + extra + 1

                @pl.when(distance <= ring.reach)
                def _():
                    ring.step(distance)

        work = index - lead

        @pl.when((work >= 0) & (work < 4 * blocks))
        def _():
            piece, stage = work // 4, work % 4

            @pl.when(stage == 0)
            def _():
                normalize(piece)

            @pl.when((stage == 1) | (stage == 2))
            def _():
                units_step(piece, (stage - 1) * (count // 2), count // 2)

            @pl.when(stage == 3)
            def _():
                backward_step(piece)
                leave_step(piece)

        return carry

    lax.fori_loop(0, pairs + 3, step, 0)

    def arrive(pair, carry):
        line.arrive(pair)
        return carry

    lax.fori_loop(pairs // 2, pairs, arrive, 0)

    def drain(pair, carry):
        line.drain(pair)
        return carry

    lax.fori_loop(0, pairs, drain, 0)
    ring.drain()
    store(second_buf, second_ref, blocks - 1, 0).wait()
    store(hidden_buf, hidden_ref, blocks - 1, 1).wait()
    store(pair_buf, pair_ref, blocks - 1, 2).wait()
    store(leave_buf, leave_ref, blocks - 1, 3).wait()


def middle_stage(
    branch, tokens, top, gain, shift, mlp_shard, out_shard, collective_id, rows=32, block=256
):
    capacity, width = branch.shape
    units = out_shard.shape[1]
    ways = width // out_shard.shape[0]
    low = jnp.bfloat16
    anywhere, held = pl.BlockSpec(memory_space=pl.ANY), pl.BlockSpec(memory_space=pltpu.VMEM)
    total, second, hidden, pair, leave = pl.pallas_call(
        functools.partial(middle_kernel, rows, block),
        out_shape=(
            jax.ShapeDtypeStruct((2 * capacity, width), low),
            jax.ShapeDtypeStruct((capacity, width), low),
            jax.ShapeDtypeStruct((capacity, units), low),
            jax.ShapeDtypeStruct((capacity, 2 * units), low),
            jax.ShapeDtypeStruct((capacity, width), low),
        ),
        in_specs=[anywhere, anywhere, anywhere, held, held, anywhere, anywhere],
        out_specs=(held, anywhere, anywhere, anywhere, anywhere),
        scratch_shapes=line_scratch(2 * capacity, width, rows)
        + [
            pltpu.VMEM((width, 2 * units), low),
            pltpu.VMEM((width, units), low),
            pltpu.VMEM((block, width), low),
            pltpu.VMEM((block, width), low),
            pltpu.VMEM((block, width), low),
            pltpu.VMEM((block, units), low),
            pltpu.VMEM((block, 2 * units), low),
            pltpu.VMEM((block, width), low),
            pltpu.SemaphoreType.DMA((5,)),
            pltpu.SemaphoreType.DMA((4,)),
        ]
        + ring_scratch(ways, 2),
        compiler_params=pltpu.CompilerParams(
            collective_id=collective_id, has_side_effects=True, vmem_limit_bytes=60 << 20
        ),
        cost_estimate=pl.CostEstimate(
            flops=200_000_000_000, bytes_accessed=40 << 20, transcendentals=0
        ),
    )(branch, tokens, top, gain[None], shift[None], mlp_shard, out_shard)
    return total, second, hidden, pair, leave


def turn(values, cosine, sine):
    half = values.shape[1] // 2
    front, back = values[:, :half], values[:, half:]
    return jnp.concatenate([front * cosine - back * sine, front * sine + back * cosine], axis=1)


def decay_block(ends_ref, log_keep, row_start, col_start, size):
    rows = row_start + lax.broadcasted_iota(jnp.int32, (size, 1), 0)
    cols = col_start + lax.broadcasted_iota(jnp.int32, (1, size), 1)
    row_slot = jnp.zeros((size, 1), jnp.int32)
    col_slot = jnp.zeros((1, size), jnp.int32)
    for slot in range(SLOTS):
        row_slot += (rows >= ends_ref[slot]).astype(jnp.int32)
        col_slot += (cols >= ends_ref[slot]).astype(jnp.int32)
    row_slot = jnp.where(rows < ends_ref[SLOTS - 1], row_slot, -1)
    distance = rows - cols
    allowed = (row_slot == col_slot) & (distance >= 0)
    distance = jnp.maximum(distance, 0).astype(jnp.float32)
    return jnp.where(allowed, jnp.exp(distance * log_keep), 0.0)


def group_stats(values):
    center = values - jnp.mean(values, axis=-1, keepdims=True)
    inverse = lax.rsqrt(jnp.mean(center * center, axis=-1, keepdims=True) + GROUP_EPS)
    return center * inverse, inverse


def retain_kernel(
    ends_ref,
    keep_ref,
    first_ref,
    query_w_ref,
    key_w_ref,
    value_w_ref,
    gate_w_ref,
    cos_ref,
    sin_ref,
    gain_ref,
    query_ref,
    key_ref,
    value_ref,
    gate_ref,
    retained_ref,
    gated_ref,
    keys,
    values,
):
    head, block = pl.program_id(0), pl.program_id(1)
    size = query_ref.shape[0]
    here = pl.ds(pl.multiple_of(block * size, size), size)
    first = first_ref[here, :]
    cosine, sine = cos_ref[here, :], sin_ref[here, :]
    query = turn(row_product(first, query_w_ref[...]), cosine, sine).astype(jnp.bfloat16)
    key = turn(row_product(first, key_w_ref[...]), cosine, sine) * KH ** (-0.5)
    key = key.astype(jnp.bfloat16)
    value = row_product(first, value_w_ref[...]).astype(jnp.bfloat16)
    gate = row_product(first, gate_w_ref[...])
    query_ref[...] = query
    key_ref[...] = key
    value_ref[...] = value
    gate_ref[...] = gate
    keys[here, :] = key
    values[here, :] = value
    retained_ref[...] = jnp.zeros_like(retained_ref)

    def visit(other, carry):
        there = pl.ds(pl.multiple_of(other * size, size), size)
        decay = decay_block(ends_ref, keep_ref[head], block * size, other * size, size)
        weights = (turned_product(query, keys[there, :]) * decay).astype(jnp.bfloat16)
        retained_ref[...] += row_product(weights, values[there, :])
        return carry

    lax.fori_loop(0, block + 1, visit, 0)
    normed, inverse = group_stats(retained_ref[...])
    gated_ref[...] = (gate * jax.nn.sigmoid(gate) * (normed * gain_ref[0])).astype(jnp.bfloat16)


def retain(ends, log_keep, first_low, full, cosine, sine, group_values, size=256):
    capacity, width = first_low.shape
    heads = group_values.shape[0]
    scalar = pl.BlockSpec(memory_space=pltpu.SMEM)
    table = pl.BlockSpec((capacity, KH // 2), lambda h, r: (0, 0))
    key_block = pl.BlockSpec((size, KH), lambda h, r: (r, h))
    value_block = pl.BlockSpec((size, VH), lambda h, r: (r, h))
    ratio = KH * heads * 2 // VH

    def shape(columns, kind):
        return jax.ShapeDtypeStruct((capacity, heads * columns), kind)

    return pl.pallas_call(
        retain_kernel,
        grid=(heads, capacity // size),
        out_shape=(
            shape(KH, jnp.bfloat16),
            shape(KH, jnp.bfloat16),
            shape(VH, jnp.bfloat16),
            shape(VH, jnp.float32),
            shape(VH, jnp.float32),
            shape(VH, jnp.bfloat16),
        ),
        in_specs=[
            scalar,
            scalar,
            pl.BlockSpec((capacity, width), lambda h, r: (0, 0)),
            pl.BlockSpec((width, KH), lambda h, r: (0, h)),
            pl.BlockSpec((width, KH), lambda h, r: (0, heads + h)),
            pl.BlockSpec((width, VH), lambda h, r: (0, ratio + h)),
            pl.BlockSpec((width, VH), lambda h, r: (0, ratio + heads + h)),
            table,
            table,
            pl.BlockSpec((1, 1, VH), lambda h, r: (h, 0, 0)),
        ],
        out_specs=(key_block, key_block, value_block, value_block, value_block, value_block),
        scratch_shapes=[
            pltpu.VMEM((capacity, KH), jnp.bfloat16),
            pltpu.VMEM((capacity, VH), jnp.bfloat16),
        ],
        compiler_params=pltpu.CompilerParams(vmem_limit_bytes=52 << 20),
        cost_estimate=pl.CostEstimate(
            flops=16_000_000_000, bytes_accessed=40 << 20, transcendentals=0
        ),
    )(ends, log_keep, first_low, full, full, full, full, cosine, sine, group_values[:, None, :])


def back_kernel(
    rows,
    block,
    heads,
    ends_ref,
    keep_ref,
    leave_ref,
    tokens_ref,
    both_ref,
    top_ref,
    norm_gain_ref,
    out_w_ref,
    retained_ref,
    gate_ref,
    group_gain_ref,
    query_ref,
    key_ref,
    value_ref,
    cos_ref,
    sin_ref,
    gated_ref,
    first_ref,
    full_ref,
    total,
    middle_ref,
    weight_grad_ref,
    input_grad_ref,
    norm_grad_ref,
    group_grad_ref,
    mine,
    near,
    far,
    near_sem,
    far_sem,
    done_sem,
    out_sem,
    cross_sem,
    give_sem,
    out_w,
    query_buf,
    key_buf,
    value_buf,
    gated_buf,
    first_buf,
    middle_low,
    flip_buf,
    grad_buf,
    stream_buf,
    tile_buf,
    wide_buf,
    input_grad_buf,
    retained_buf,
    gate_buf,
    grad_gated_buf,
    upstream_buf,
    query_grad,
    key_grad,
    value_grad,
    load_sem,
    stream_sem,
    group_sem,
    store_sem,
):
    capacity, width = leave_ref.shape
    blocks, tiles = capacity // block, width // block
    pairs = capacity // (2 * rows)
    attend, finish = blocks, blocks + heads * blocks
    low, f32 = jnp.bfloat16, jnp.float32
    line = Line(rows, mine, near, far, total, near_sem, far_sem, done_sem, out_sem, cross_sem, give_sem)

    def part(index, size=block):
        return pl.ds(pl.multiple_of(index * size, size), size)

    held = [
        pltpu.make_async_copy(source, target, load_sem.at[index])
        for index, (source, target) in enumerate(
            (
                (leave_ref, mine),
                (out_w_ref, out_w),
                (query_ref, query_buf),
                (key_ref, key_buf),
                (value_ref, value_buf),
                (gated_ref, gated_buf),
                (first_ref, first_buf),
            )
        )
    ]

    def load_rows(index):
        lower, upper = pl.ds(0, width), pl.ds(width, width)
        return [
            pltpu.make_async_copy(
                tokens_ref.at[part(index)], stream_buf.at[0, :, lower], stream_sem.at[0]
            ),
            pltpu.make_async_copy(
                both_ref.at[part(index)], stream_buf.at[1, :, lower], stream_sem.at[1]
            ),
            pltpu.make_async_copy(
                both_ref.at[part(blocks + index)], tile_buf.at[:, lower], stream_sem.at[2]
            ),
            pltpu.make_async_copy(
                top_ref.at[part(index)], tile_buf.at[:, upper], stream_sem.at[3]
            ),
        ]

    def load_group(index):
        slot = index % 2
        here, there = part(index % blocks), part(index // blocks, VH)
        return [
            pltpu.make_async_copy(
                retained_ref.at[here, there], retained_buf.at[slot], group_sem.at[2 * slot]
            ),
            pltpu.make_async_copy(
                gate_ref.at[here, there], gate_buf.at[slot], group_sem.at[2 * slot + 1]
            ),
        ]

    def load_tile(index):
        slot = index % 2
        return pltpu.make_async_copy(
            full_ref.at[part(index)], stream_buf.at[slot], stream_sem.at[4 + slot]
        )

    def store_middle(index):
        return pltpu.make_async_copy(wide_buf, middle_ref.at[part(index)], store_sem.at[0])

    def store_tile(index):
        return pltpu.make_async_copy(tile_buf, weight_grad_ref.at[part(index)], store_sem.at[1])

    def store_input(index):
        return pltpu.make_async_copy(
            input_grad_buf, input_grad_ref.at[:, part(index)], store_sem.at[2]
        )

    held[0].start()
    for copy in load_rows(0):
        copy.start()
    for copy in held[1:]:
        copy.start()
    line.greet()
    held[0].wait()
    norm_grad_ref[...] = jnp.zeros_like(norm_grad_ref)
    group_grad_ref[...] = jnp.zeros_like(group_grad_ref)

    def norm_stage(index):
        for copy in load_rows(index):
            copy.wait()

        @pl.when(index > 0)
        def _():
            store_middle(index - 1).wait()

        def one(piece, carry):
            here = pl.ds(pl.multiple_of(piece * 256, 256), 256)
            there = pl.ds(pl.multiple_of(index * block + piece * 256, 256), 256)
            values = stream_buf[0, here, :width].astype(f32) + stream_buf[1, here, :width].astype(
                f32
            )
            back = tile_buf[here, :width].astype(f32)
            center = values - jnp.mean(values, axis=-1, keepdims=True)
            inverse = lax.rsqrt(jnp.mean(center * center, axis=-1, keepdims=True) + NORM_EPS)
            normed = center * inverse
            scaled = back * norm_gain_ref[...]
            plain_mean = jnp.mean(scaled, axis=-1, keepdims=True)
            cross_mean = jnp.mean(scaled * normed, axis=-1, keepdims=True)
            middle = tile_buf[here, width:].astype(f32) + inverse * (
                scaled - plain_mean - normed * cross_mean
            )
            wide_buf[here, :] = middle
            middle_low[there, :] = middle.astype(low)
            norm_grad_ref[0:1, :] += jnp.sum(back * normed, axis=0, keepdims=True)
            norm_grad_ref[1:2, :] += jnp.sum(back, axis=0, keepdims=True)
            return carry

        lax.fori_loop(0, block // 256, one, 0)
        store_middle(index).start()

        @pl.when(index < blocks - 1)
        def _():
            for copy in load_rows(index + 1):
                copy.start()

        @pl.when(index == blocks - 1)
        def _():
            for copy in load_group(0):
                copy.start()
            load_tile(0).start()

    def attend_stage(index):
        head, place = index // blocks, index % blocks

        @pl.when(index == 0)
        def _():
            for copy in held[1:]:
                copy.wait()

        for copy in load_group(index):
            copy.wait()

        @pl.when(index < heads * blocks - 1)
        def _():
            for copy in load_group(index + 1):
                copy.start()

        @pl.when(place == 0)
        def _():
            key_grad[...] = jnp.zeros_like(key_grad)
            value_grad[...] = jnp.zeros_like(value_grad)

        slot = index % 2
        here = part(place)
        keys_here, values_here = part(head, KH), part(head, VH)
        gain = group_gain_ref[pl.ds(head, 1), :]
        gate_place = pl.ds(pl.multiple_of(heads * (2 * KH + VH) + head * VH, VH), VH)
        grad_gated_buf[...] = row_product(middle_low[here, :], out_w[:, values_here])

        def gate_rows(piece, carry):
            few = pl.ds(pl.multiple_of(piece * 32, 32), 32)
            there = pl.ds(pl.multiple_of(place * block + piece * 32, 32), 32)
            normed, inverse = group_stats(retained_buf[slot, few, :])
            gate, grad_gated = gate_buf[slot, few, :], grad_gated_buf[few, :]
            sigmoid = jax.nn.sigmoid(gate)
            slope = sigmoid * (1.0 + gate * (1.0 - sigmoid))
            grad_buf[there, gate_place] = (grad_gated * (normed * gain) * slope).astype(low)
            grad_out = grad_gated * (gate * sigmoid)
            group_grad_ref[pl.ds(head, 1), :] += jnp.sum(grad_out * normed, axis=0, keepdims=True)
            scaled = grad_out * gain
            plain_mean = jnp.mean(scaled, axis=-1, keepdims=True)
            cross_mean = jnp.mean(scaled * normed, axis=-1, keepdims=True)
            upstream_buf[few, :] = (
                inverse * (scaled - plain_mean - normed * cross_mean)
            ).astype(low)
            return carry

        lax.fori_loop(0, block // 32, gate_rows, 0, unroll=4)
        upstream = upstream_buf[...]
        query = query_buf[here, keys_here]
        query_grad[...] = jnp.zeros_like(query_grad)

        def visit(other, carry):
            there = part(other)
            decay = decay_block(ends_ref, keep_ref[head], place * block, other * block, block)
            key = key_buf[there, keys_here]
            weights = (turned_product(query, key) * decay).astype(low)
            value_grad[there, :] += outer_product(weights, upstream)
            scores = turned_product(upstream, value_buf[there, values_here]) * decay
            scores = scores.astype(low)
            query_grad[...] += row_product(scores, key)
            key_grad[there, :] += outer_product(scores, query)
            return carry

        lax.fori_loop(0, place + 1, visit, 0)
        cosine, sine = cos_ref[here, :], sin_ref[here, :]
        grad_buf[here, keys_here] = turn(query_grad[...], cosine, -sine).astype(low)

        @pl.when(place == blocks - 1)
        def _():
            def one(other, carry):
                there = part(other)
                turned = turn(key_grad[there, :] * KH ** (-0.5), cos_ref[there, :], -sin_ref[there, :])
                grad_buf[there, part(heads + head, KH)] = turned.astype(low)
                value_place = pl.ds(pl.multiple_of(heads * 2 * KH + head * VH, VH), VH)
                grad_buf[there, value_place] = value_grad[there, :].astype(low)
                return carry

            lax.fori_loop(0, blocks, one, 0)

    def tile_stage(index):
        columns = grad_buf.shape[1]

        @pl.when(index == 0)
        def _():
            store_middle(blocks - 1).wait()

        @pl.when(index < tiles - 1)
        def _():
            load_tile(index + 1).start()

        @pl.when(index > 0)
        def _():
            store_tile(index - 1).wait()
            store_input(index - 1).wait()

        load_tile(index).wait()
        here = part(index)
        flip_buf[...] = first_buf[:, here].T

        def one(number, carry):
            there = part(number, 512)
            tile_buf[:, there] = row_product(flip_buf[...], grad_buf[:, there]).astype(low)
            return carry

        lax.fori_loop(0, columns // 512, one, 0)

        flip_buf[...] = middle_low[:, here].T

        def last(number, carry):
            there = pl.ds(pl.multiple_of(columns + number * 512, 512), 512)
            tile_buf[:, there] = row_product(
                flip_buf[...], gated_buf[:, part(number, 512)]
            ).astype(low)
            return carry

        lax.fori_loop(0, gated_buf.shape[1] // 512, last, 0)
        store_tile(index).start()

        def inward(number, carry):
            there = part(number)
            input_grad_buf[there, :] = turned_product(
                grad_buf[there, :], stream_buf[index % 2]
            ).astype(low)
            return carry

        lax.fori_loop(0, blocks, inward, 0)
        store_input(index).start()

    def step(index, carry):
        line.step(index, pairs)

        @pl.when(index < attend)
        def _():
            norm_stage(index)

        @pl.when((index >= attend) & (index < finish))
        def _():
            attend_stage(index - attend)

        @pl.when((index >= finish) & (index < finish + tiles))
        def _():
            tile_stage(index - finish)

        return carry

    lax.fori_loop(0, max(pairs + 3, finish + tiles), step, 0)

    def drain(pair, carry):
        line.arrive(pair)
        line.drain(pair)
        return carry

    lax.fori_loop(0, pairs, drain, 0)
    store_tile(tiles - 1).wait()
    store_input(tiles - 1).wait()


def back_stage(
    ends,
    log_keep,
    leave,
    tokens,
    both,
    top,
    norm_gain,
    mix_out,
    retained,
    gate,
    group_values,
    query,
    key,
    value,
    cosine,
    sine,
    gated,
    first_low,
    full,
    collective_id,
    rows=32,
    block=256,
):
    capacity, width = leave.shape
    heads = group_values.shape[0]
    columns, units = full.shape[1], gated.shape[1]
    low, f32 = jnp.bfloat16, jnp.float32
    anywhere, kept = pl.BlockSpec(memory_space=pl.ANY), pl.BlockSpec(memory_space=pltpu.VMEM)
    scalar = pl.BlockSpec(memory_space=pltpu.SMEM)
    return pl.pallas_call(
        functools.partial(back_kernel, rows, block, heads),
        out_shape=(
            jax.ShapeDtypeStruct((capacity, width), low),
            jax.ShapeDtypeStruct((capacity, width), f32),
            jax.ShapeDtypeStruct((width, columns + units), low),
            jax.ShapeDtypeStruct((capacity, width), low),
            jax.ShapeDtypeStruct((2, width), f32),
            jax.ShapeDtypeStruct((heads, VH), f32),
        ),
        in_specs=[scalar] * 2
        + [anywhere] * 4
        + [kept]
        + [anywhere] * 3
        + [kept]
        + [anywhere] * 3
        + [kept] * 2
        + [anywhere] * 3,
        out_specs=(kept, anywhere, anywhere, anywhere, kept, kept),
        scratch_shapes=line_scratch(capacity, width, rows)
        + [
            pltpu.VMEM((width, units), low),
            pltpu.VMEM(query.shape, low),
            pltpu.VMEM(key.shape, low),
            pltpu.VMEM(value.shape, low),
            pltpu.VMEM(gated.shape, low),
            pltpu.VMEM((capacity, width), low),
            pltpu.VMEM((capacity, width), low),
            pltpu.VMEM((block, capacity), low),
            pltpu.VMEM((capacity, columns), low),
            pltpu.VMEM((2, block, columns), low),
            pltpu.VMEM((block, columns + units), low),
            pltpu.VMEM((block, width), f32),
            pltpu.VMEM((capacity, block), low),
            pltpu.VMEM((2, block, VH), f32),
            pltpu.VMEM((2, block, VH), f32),
            pltpu.VMEM((block, VH), f32),
            pltpu.VMEM((block, VH), low),
            pltpu.VMEM((block, KH), f32),
            pltpu.VMEM((capacity, KH), f32),
            pltpu.VMEM((capacity, VH), f32),
            pltpu.SemaphoreType.DMA((7,)),
            pltpu.SemaphoreType.DMA((6,)),
            pltpu.SemaphoreType.DMA((4,)),
            pltpu.SemaphoreType.DMA((3,)),
        ],
        compiler_params=pltpu.CompilerParams(
            collective_id=collective_id, has_side_effects=True, vmem_limit_bytes=62 << 20
        ),
        cost_estimate=pl.CostEstimate(
            flops=100_000_000_000, bytes_accessed=40 << 20, transcendentals=0
        ),
    )(
        ends,
        log_keep,
        leave,
        tokens,
        both,
        top,
        norm_gain[None],
        mix_out,
        retained,
        gate,
        group_values,
        query,
        key,
        value,
        cosine,
        sine,
        gated,
        first_low,
        full,
    )


def last_kernel(
    rows,
    ways,
    back_ref,
    tokens_ref,
    middle_ref,
    norm_gain_ref,
    norm_grad_ref,
    group_grad_ref,
    token_grad_ref,
    small_ref,
    total,
    mine,
    near,
    far,
    near_sem,
    far_sem,
    done_sem,
    out_sem,
    cross_sem,
    give_sem,
    token_buf,
    middle_buf,
    small_buf,
    small_in,
    load_sem,
    store_sem,
    small_send_sem,
    small_recv_sem,
):
    capacity, width = back_ref.shape
    pairs = capacity // (2 * rows)
    heads, group = group_grad_ref.shape
    f32 = jnp.float32
    line = Line(rows, mine, near, far, total, near_sem, far_sem, done_sem, out_sem, cross_sem, give_sem)
    me = lax.axis_index("dp")
    peers = [lax.rem(me + distance, ways) for distance in range(1, ways)]
    loads = [
        pltpu.make_async_copy(source, target, load_sem.at[index])
        for index, (source, target) in enumerate(
            ((back_ref, mine), (tokens_ref, token_buf), (middle_ref, middle_buf))
        )
    ]

    def part(pair):
        return pl.ds(pl.multiple_of(pair * 2 * rows, 2 * rows), 2 * rows)

    def store(pair):
        return pltpu.make_async_copy(
            middle_buf.at[part(pair)], token_grad_ref.at[part(pair)], store_sem.at[pair]
        )

    def share(distance):
        return pltpu.make_async_remote_copy(
            small_buf,
            small_in.at[distance],
            small_send_sem.at[distance],
            small_recv_sem.at[distance],
            device_id={"dp": peers[distance]},
            device_id_type=MESH,
        )

    for copy in loads:
        copy.start()
    line.greet(peers)
    small_buf[...] = jnp.zeros_like(small_buf)
    small_buf[2:4, :] = norm_grad_ref[...]
    for head in range(heads):
        small_buf[4:5, head * group : (head + 1) * group] = group_grad_ref[head : head + 1, :]
    loads[0].wait()

    def norm_stage(pair):
        line.arrive(pair)

        @pl.when(pair == 0)
        def _():
            loads[1].wait()
            loads[2].wait()

        def one(piece, carry):
            here = pl.ds(pl.multiple_of(pair * 2 * rows + piece * 32, 32), 32)
            values = token_buf[here, :].astype(f32)
            back = total[here, :].astype(f32)
            center = values - jnp.mean(values, axis=-1, keepdims=True)
            inverse = lax.rsqrt(jnp.mean(center * center, axis=-1, keepdims=True) + NORM_EPS)
            normed = center * inverse
            scaled = back * norm_gain_ref[...]
            plain_mean = jnp.mean(scaled, axis=-1, keepdims=True)
            cross_mean = jnp.mean(scaled * normed, axis=-1, keepdims=True)
            middle_buf[here, :] += inverse * (scaled - plain_mean - normed * cross_mean)
            small_buf[0:1, :] += jnp.sum(back * normed, axis=0, keepdims=True)
            small_buf[1:2, :] += jnp.sum(back, axis=0, keepdims=True)
            return carry

        lax.fori_loop(0, 2 * rows // 32, one, 0)
        store(pair).start()

    def step(index, carry):
        line.step(index, pairs)

        @pl.when(index >= 5)
        def _():
            norm_stage(index - 5)

        return carry

    lax.fori_loop(0, pairs + 5, step, 0)
    for distance in range(ways - 1):
        share(distance).start()

    def drain(pair, carry):
        line.drain(pair)
        store(pair).wait()
        return carry

    lax.fori_loop(0, pairs, drain, 0)
    for distance in range(ways - 1):
        share(distance).wait()
    small_ref[...] = small_buf[...]
    for distance in range(ways - 1):
        small_ref[...] += small_in[distance]


def last_stage(back, tokens, middle, norm_gain, norm_grad, group_grad, ways, collective_id, rows=32):
    capacity, width = back.shape
    low, f32 = jnp.bfloat16, jnp.float32
    anywhere, kept = pl.BlockSpec(memory_space=pl.ANY), pl.BlockSpec(memory_space=pltpu.VMEM)
    small = (8, width)
    return pl.pallas_call(
        functools.partial(last_kernel, rows, ways),
        out_shape=(jax.ShapeDtypeStruct((capacity, width), f32), jax.ShapeDtypeStruct(small, f32)),
        in_specs=[anywhere] * 3 + [kept] * 3,
        out_specs=(anywhere, kept),
        scratch_shapes=[pltpu.VMEM((capacity, width), low)]
        + line_scratch(capacity, width, rows)
        + [
            pltpu.VMEM((capacity, width), low),
            pltpu.VMEM((capacity, width), f32),
            pltpu.VMEM(small, f32),
            pltpu.VMEM((ways - 1, *small), f32),
            pltpu.SemaphoreType.DMA((3,)),
            pltpu.SemaphoreType.DMA((capacity // (2 * rows),)),
            pltpu.SemaphoreType.DMA((ways - 1,)),
            pltpu.SemaphoreType.DMA((ways - 1,)),
        ],
        compiler_params=pltpu.CompilerParams(
            collective_id=collective_id, has_side_effects=True, vmem_limit_bytes=52 << 20
        ),
        cost_estimate=pl.CostEstimate(
            flops=100_000_000_000, bytes_accessed=40 << 20, transcendentals=0
        ),
    )(back, tokens, middle, norm_gain[None], norm_grad, group_grad)


def local(
    tokens,
    lengths,
    cotangent,
    qk_weight,
    qk_first,
    qk_second,
    inner_weight,
    inner_first,
    inner_second,
    outer_weight,
    outer_first,
    outer_second,
    norm_params,
    norm_first,
    norm_second,
    group_gain,
    group_first,
    group_second,
):
    capacity = tokens.shape[0]
    local_heads = group_gain.shape[0]
    low = jnp.bfloat16
    tensor_index, data_index = lax.axis_index("tensor"), lax.axis_index("dp")

    def joined(shards):
        return jnp.concatenate([part.astype(low) for part in shards], axis=1)

    def gather(shards):
        return lax.all_gather(joined(shards), "dp", axis=0, tiled=True)

    def scatter(grad):
        return lax.psum_scatter(grad, "dp", scatter_dimension=0, tiled=True)

    norm_cols, group_cols = norm_params.shape[1], group_gain.shape[1]
    small = lax.all_gather(
        jnp.concatenate([norm_params.reshape(-1), group_gain.reshape(-1)]).astype(low), "dp"
    ).astype(jnp.float32)
    ways = small.shape[0]
    norm_values = small[:, : 4 * norm_cols].reshape(ways, 4, norm_cols)
    norm_values = norm_values.transpose(1, 0, 2).reshape(4, -1)
    group_values = small[:, 4 * norm_cols :].reshape(ways, local_heads, group_cols)
    group_values = group_values.transpose(1, 0, 2).reshape(local_heads, -1)
    first_full = gather([qk_weight[0], qk_weight[1], inner_weight[0], inner_weight[1]])
    mix_out = gather([outer_weight[0]])
    mlp_shard = joined([inner_weight[2], inner_weight[3]])
    out_shard = outer_weight[1].astype(low)
    row_index, sequence_id, position, live_rows = sequence_layout(lengths[0], capacity)
    cosine, sine = rotation_tables(position, KH)
    ends = jnp.cumsum(lengths[0])
    head_ids = tensor_index * local_heads + jnp.arange(local_heads, dtype=jnp.int32)
    log_keep = jnp.log1p(-jnp.exp2(-(5.0 + head_ids.astype(jnp.float32))))
    inputs = tokens.astype(jnp.float32)
    first_out, unused_normed, unused_inverse = layer_norm(
        inputs, norm_values[0], norm_values[1], NORM_EPS
    )
    first_low = first_out.astype(low)
    query, key, value, gate, retained, gated = retain(
        ends, log_keep, first_low, first_full, cosine, sine, group_values
    )
    grad_top = cotangent.astype(jnp.float32) * live_rows.astype(jnp.float32)[:, None]
    top_low = grad_top.astype(low)
    branch = turned_product(gated, mix_out).astype(low)
    both, second_low, hidden, pair_low, leave = middle_stage(
        branch, tokens, top_low, norm_values[2], norm_values[3], mlp_shard, out_shard, 0
    )
    up_cols = out_shard.shape[1]
    mlp_out_grad = outer_product(top_low, hidden).astype(low)
    mlp_grad = outer_product(second_low, pair_low).astype(low)
    mlp_out_part, mlp_part = scatter(mlp_out_grad), scatter(mlp_grad)
    both, unused_out, unused_mlp = lax.optimization_barrier((both, mlp_out_grad, mlp_grad))
    leave_sum, grad_middle, first_grad, back_first, norm_two, grad_group_gain = back_stage(
        ends,
        log_keep,
        leave,
        tokens,
        both,
        top_low,
        norm_values[2],
        mix_out,
        retained,
        gate,
        group_values,
        query,
        key,
        value,
        cosine,
        sine,
        gated,
        first_low,
        first_full,
        1,
    )
    first_part = scatter(first_grad)
    back_first, mlp_out_part, mlp_part = lax.optimization_barrier(
        (back_first, mlp_out_part, mlp_part)
    )
    layer_out = (
        inputs + both[:capacity].astype(jnp.float32) + leave_sum.astype(jnp.float32)
    )
    token_grad, small_grad = last_stage(
        back_first, tokens, grad_middle, norm_values[0], norm_two, grad_group_gain, ways, 2
    )
    norm_grad = lax.dynamic_slice(small_grad, (0, data_index * norm_cols), (4, norm_cols))
    group_grad = lax.dynamic_slice(
        small_grad[4, : local_heads * VH].reshape(local_heads, VH),
        (0, data_index * group_cols),
        (local_heads, group_cols),
    )
    qk_cols, mix_cols = local_heads * KH, local_heads * VH
    starts = [qk_cols, 2 * qk_cols, 2 * qk_cols + mix_cols, 2 * qk_cols + 2 * mix_cols]
    query_grad, key_grad, value_grad, gate_grad, mix_out_part = jnp.split(
        first_part, starts, axis=1
    )
    qk_grad = jnp.stack([query_grad, key_grad]).astype(jnp.float32)
    inner_grad = jnp.stack(
        [value_grad, gate_grad, mlp_part[:, :up_cols], mlp_part[:, up_cols:]]
    ).astype(jnp.float32)
    outer_grad = jnp.stack([mix_out_part, mlp_out_part]).astype(jnp.float32)
    qk_new = adam_update(qk_weight, qk_grad, qk_first, qk_second, MATRIX_RATE, WEIGHT_DECAY)
    inner_new = adam_update(
        inner_weight, inner_grad, inner_first, inner_second, MATRIX_RATE, WEIGHT_DECAY
    )
    outer_new = adam_update(
        outer_weight, outer_grad, outer_first, outer_second, MATRIX_RATE, WEIGHT_DECAY
    )
    norm_new = adam_update(norm_params, norm_grad, norm_first, norm_second, VECTOR_RATE, 0.0)
    group_new = adam_update(group_gain, group_grad, group_first, group_second, VECTOR_RATE, 0.0)
    return (layer_out, token_grad, *qk_new, *inner_new, *outer_new, *norm_new, *group_new)


def solution(mesh):
    in_specs = (
        P("dp", None),
        P("dp", None),
        P("dp", None),
        P(None, "dp", "tensor"),
        P(None, "dp", "tensor"),
        P(None, "dp", "tensor"),
        P(None, "dp", "tensor"),
        P(None, "dp", "tensor"),
        P(None, "dp", "tensor"),
        P(None, "dp", "tensor"),
        P(None, "dp", "tensor"),
        P(None, "dp", "tensor"),
        P(None, "dp"),
        P(None, "dp"),
        P(None, "dp"),
        P("tensor", "dp"),
        P("tensor", "dp"),
        P("tensor", "dp"),
    )
    out_specs = (
        P("dp", None),
        P("dp", None),
        P(None, "dp", "tensor"),
        P(None, "dp", "tensor"),
        P(None, "dp", "tensor"),
        P(None, "dp", "tensor"),
        P(None, "dp", "tensor"),
        P(None, "dp", "tensor"),
        P(None, "dp", "tensor"),
        P(None, "dp", "tensor"),
        P(None, "dp", "tensor"),
        P(None, "dp"),
        P(None, "dp"),
        P(None, "dp"),
        P("tensor", "dp"),
        P("tensor", "dp"),
        P("tensor", "dp"),
    )
    return jax.shard_map(local, mesh=mesh, in_specs=in_specs, out_specs=out_specs, check_vma=False)
```

```python
import functools
import math

import jax
import jax.numpy as jnp
from jax import lax
from jax.experimental import pallas as pl
from jax.experimental.pallas import tpu as pltpu
from jax.sharding import PartitionSpec as P

MESH = pl.DeviceIdType.MESH

KH = 256
VH = 512
SLOTS = 4
STEP = 10


NORM_EPS = 1e-05
GROUP_EPS = 1.0
BETA_FIRST = 0.9
BETA_SECOND = 0.95
ADAM_EPS = 1e-08
MATRIX_RATE = 0.05
VECTOR_RATE = 0.5
WEIGHT_DECAY = 0.1


def layer_norm(values, gain_row, shift_row, epsilon):
    center = values - jnp.mean(values, axis=-1, keepdims=True)
    inverse = lax.rsqrt(jnp.mean(center * center, axis=-1, keepdims=True) + epsilon)
    normed = center * inverse
    return (normed * gain_row + shift_row, normed, inverse)


def norm_back(upstream, normed, inverse, gain_row):
    scaled = upstream * gain_row
    plain_mean = jnp.mean(scaled, axis=-1, keepdims=True)
    cross_mean = jnp.mean(scaled * normed, axis=-1, keepdims=True)
    result = inverse * (scaled - plain_mean - normed * cross_mean)
    return (result, jnp.sum(upstream * normed, axis=0), jnp.sum(upstream, axis=0))


def sequence_layout(lengths_row, capacity):
    seq_ends = jnp.cumsum(lengths_row)
    row_index = jnp.arange(capacity, dtype=jnp.int32)
    sequence_id = jnp.sum((row_index[:, None] >= seq_ends[None, :]).astype(jnp.int32), axis=1)
    starts = seq_ends - lengths_row
    slot_index = jnp.arange(lengths_row.shape[0], dtype=jnp.int32)
    row_start = jnp.sum(
        jnp.where(sequence_id[:, None] == slot_index[None, :], starts[None, :], 0), axis=1
    )
    position = row_index - row_start
    live_rows = row_index < seq_ends[-1]
    return (row_index, sequence_id, position, live_rows)


def decay_table(row_index, sequence_id, live_rows, head_ids):
    allowed = (
        (sequence_id[:, None] == sequence_id[None, :])
        & (row_index[:, None] >= row_index[None, :])
        & live_rows[:, None]
        & live_rows[None, :]
    )
    distance = jnp.maximum(row_index[:, None] - row_index[None, :], 0).astype(jnp.float32)
    log_keep = jnp.log1p(-jnp.exp2(-(5.0 + head_ids.astype(jnp.float32))))
    return jnp.where(allowed[None], jnp.exp(distance[None] * log_keep[:, None, None]), 0.0)


def rotation_tables(position, head_size):
    half_size = head_size // 2
    frequency = jnp.exp(
        -math.log(10000.0) * 2.0 * jnp.arange(half_size, dtype=jnp.float32) / head_size
    )
    angles = position.astype(jnp.float32)[:, None] * frequency[None, :]
    return (jnp.cos(angles), jnp.sin(angles))


def rotate(values, cosine, sine, head_size):
    row_count = values.shape[0]
    shaped = values.reshape(row_count, -1, 2, head_size // 2)
    front_half = shaped[:, :, 0]
    back_half = shaped[:, :, 1]
    cos_rows = cosine[:, None, :]
    sin_rows = sine[:, None, :]
    turned = jnp.stack(
        [
            front_half * cos_rows - back_half * sin_rows,
            front_half * sin_rows + back_half * cos_rows,
        ],
        axis=2,
    )
    return turned.reshape(row_count, -1)


def row_product(left, right):
    return jnp.dot(left, right, preferred_element_type=jnp.float32)


def turned_product(left, right):
    return lax.dot_general(
        left, right, (((1,), (1,)), ((), ())), preferred_element_type=jnp.float32
    )


def outer_product(left, right):
    return lax.dot_general(
        left, right, (((0,), (0,)), ((), ())), preferred_element_type=jnp.float32
    )


def adam_update(weight, gradient, moment, square, rate, decay_rate):
    moment_new = BETA_FIRST * moment + (1.0 - BETA_FIRST) * gradient
    square_new = BETA_SECOND * square + (1.0 - BETA_SECOND) * gradient * gradient
    first_hat = moment_new / (1.0 - BETA_FIRST**STEP)
    second_hat = square_new / (1.0 - BETA_SECOND**STEP)
    weight_new = weight - rate * (
        first_hat / (jnp.sqrt(second_hat) + ADAM_EPS) + decay_rate * weight
    )
    return (moment_new, square_new, weight_new)


class Ring:
    def __init__(self, count, results, recv_sem, send_sem):
        self.count, self.results, self.recv_sem, self.send_sem = count, results, recv_sem, send_sem
        me = lax.axis_index("dp")
        self.me, self.place = me, self.swap(me)
        self.right, self.left = self.owner(1), self.owner(-1)
        self.reach = count // 2

    def swap(self, index):
        if self.count != 8:
            return index
        return jnp.where(index < 4, index, jnp.where(index < 6, index + 2, index - 2))

    def owner(self, distance):
        return self.swap(lax.rem(self.place + distance + self.count, self.count))

    def greet(self):
        barrier = pltpu.get_barrier_semaphore()
        for device in (self.left, self.right):
            pl.semaphore_signal(barrier, inc=1, device_id={"dp": device}, device_id_type=MESH)
        pl.semaphore_wait(barrier, 2)

    def copies(self, owner, half, way):
        made = []
        for index, result in enumerate(self.results):
            rows = result.shape[0] // (2 * self.count)
            here = result.at[pl.ds(pl.multiple_of((owner * 2 + half) * rows, rows), rows)]
            made.append(
                pltpu.make_async_remote_copy(
                    here,
                    here,
                    self.send_sem.at[((way * 2 + half) * len(self.results) + index) * self.count + owner],
                    self.recv_sem.at[(half * len(self.results) + index) * self.count + owner],
                    device_id={"dp": self.left if way else self.right},
                    device_id_type=MESH,
                )
            )
        return made

    def streams(self):
        for half in range(2):
            for way in range(2):
                yield half, way, self.reach - (half + way) % 2

    def step(self, distance):
        for half, way, hops in self.streams():
            owner = self.owner(distance if way else -distance)

            @pl.when((distance >= 1) & (distance <= hops))
            def _():
                for copy in self.copies(owner, half, way):
                    copy.wait_recv()

            @pl.when(distance < hops)
            def _():
                for copy in self.copies(owner, half, way):
                    copy.start()

    def drain(self):
        for half, way, hops in self.streams():

            def one(distance, carry):
                for copy in self.copies(self.owner(distance if way else -distance), half, way):
                    copy.wait_send()
                return carry

            lax.fori_loop(0, hops, one, 0)


def ring_scratch(count, results):
    return [
        pltpu.SemaphoreType.DMA((2 * results * count,)),
        pltpu.SemaphoreType.DMA((4 * results * count,)),
    ]


class Line:
    def __init__(self, rows, mine, near, far, total, near_sem, far_sem, done_sem, out_sem, cross_sem, give_sem):
        self.rows, self.mine, self.near, self.far, self.total = rows, mine, near, far, total
        self.near_sem, self.far_sem, self.done_sem = near_sem, far_sem, done_sem
        self.out_sem, self.cross_sem, self.give_sem = out_sem, cross_sem, give_sem
        me = lax.axis_index("tensor")
        self.me = me
        self.inner = (me == 1) | (me == 2)
        self.outer = (me == 0) | (me == 3)
        self.relay_to = jnp.where(self.inner, 3 - me, 1 + me // 3)
        self.away = jnp.where(self.inner, 3 * (me - 1), 1 + me // 3)
        owner = jnp.where(self.inner, me, 1 + me // 3)
        self.kept, self.passed = owner - 1, 2 - owner

    def at(self, chunk):
        return pl.ds(pl.multiple_of(chunk * self.rows, self.rows), self.rows)

    def greet(self, also=()):
        barrier = pltpu.get_barrier_semaphore()
        for device in also:
            pl.semaphore_signal(barrier, inc=1, device_id={"dp": device}, device_id_type=MESH)
        pl.semaphore_signal(barrier, inc=1, device_id={"tensor": self.away}, device_id_type=MESH)

        @pl.when(self.inner)
        def _():
            pl.semaphore_signal(
                barrier, inc=1, device_id={"tensor": self.relay_to}, device_id_type=MESH
            )
            pl.semaphore_wait(barrier, 2 + len(also))

        @pl.when(self.outer)
        def _():
            pl.semaphore_wait(barrier, 1 + len(also))

    def copy(self, source, target, send_sem, recv_sem, device):
        return pltpu.make_async_remote_copy(
            source, target, send_sem, recv_sem, device_id={"tensor": device}, device_id_type=MESH
        )

    def send_in(self, chunk):
        return self.copy(
            self.mine.at[self.at(chunk)],
            self.near.at[self.at(chunk)],
            self.out_sem.at[chunk],
            self.near_sem.at[chunk],
            self.away,
        )

    def send_across(self, pair, chunk):
        return self.copy(
            self.near.at[self.at(chunk)],
            self.far.at[self.at(pair)],
            self.out_sem.at[chunk],
            self.far_sem.at[pair],
            self.relay_to,
        )

    def give(self, chunk, send_sem, device):
        place = self.total.at[self.at(chunk)]
        return self.copy(place, place, send_sem, self.done_sem.at[chunk], device)

    def give_out(self, chunk):
        return self.give(chunk, self.give_sem.at[chunk], self.away)

    def give_across(self, pair, chunk):
        return self.give(chunk, self.cross_sem.at[pair], self.relay_to)

    def wide(self, ref, chunk):
        return ref[self.at(chunk), :].astype(jnp.float32)

    def relay(self, pair):
        passed, kept = 2 * pair + self.passed, 2 * pair + self.kept

        @pl.when(self.outer)
        def _():
            self.send_in(passed).start()
            self.send_in(kept).start()

        @pl.when(self.inner)
        def _():
            self.send_in(passed).wait_recv()
            added = self.wide(self.near, passed) + self.wide(self.mine, passed)
            self.near[self.at(passed), :] = added.astype(jnp.bfloat16)
            self.send_across(pair, passed).start()

    def own(self, pair):
        kept = 2 * pair + self.kept

        @pl.when(self.inner)
        def _():
            self.send_in(kept).wait_recv()
            self.send_across(pair, kept).wait_recv()
            added = self.wide(self.near, kept) + self.wide(self.mine, kept)
            added = added + self.wide(self.far, pair)
            self.total[self.at(kept), :] = added.astype(jnp.bfloat16)
            self.give_across(pair, kept).start()
            self.give_out(kept).start()

    def forward(self, pair):
        passed = 2 * pair + self.passed

        @pl.when(self.inner)
        def _():
            self.give_out(passed).wait_recv()
            self.give_out(passed).start()

    def step(self, index, pairs):
        @pl.when(index < pairs)
        def _():
            self.relay(index)

        @pl.when((index >= 1) & (index < pairs + 1))
        def _():
            self.own(index - 1)

        @pl.when((index >= 3) & (index < pairs + 3))
        def _():
            self.forward(index - 3)

    def arrive(self, pair):
        @pl.when(self.outer)
        def _():
            self.give_out(2 * pair).wait_recv()
            self.give_out(2 * pair + 1).wait_recv()

    def release(self, pair):
        @pl.when(self.outer)
        def _():
            self.send_in(2 * pair).wait_send()
            self.send_in(2 * pair + 1).wait_send()

    def drain(self, pair):
        passed, kept = 2 * pair + self.passed, 2 * pair + self.kept

        @pl.when(self.inner)
        def _():
            self.send_across(pair, passed).wait_send()
            self.give_across(pair, kept).wait_send()
            self.give_out(kept).wait_send()
            self.give_out(passed).wait_send()


def line_scratch(height, width, rows):
    chunks = height // rows
    wide = pltpu.VMEM((height, width), jnp.bfloat16)
    sems, half_sems = pltpu.SemaphoreType.DMA((chunks,)), pltpu.SemaphoreType.DMA((chunks // 2,))
    return [
        wide,
        wide,
        pltpu.VMEM((height // 2, width), jnp.bfloat16),
        sems,
        half_sems,
        sems,
        sems,
        half_sems,
        sems,
    ]


def norm_back_rows(values, back, gain_row):
    center = values - jnp.mean(values, axis=-1, keepdims=True)
    inverse = lax.rsqrt(jnp.mean(center * center, axis=-1, keepdims=True) + NORM_EPS)
    normed = center * inverse
    result, gain_grad, shift_grad = norm_back(back, normed, inverse, gain_row)
    return result, gain_grad[None], shift_grad[None]


def middle_kernel(
    rows,
    block,
    branch_ref,
    tokens_ref,
    top_ref,
    gain_ref,
    shift_ref,
    mlp_ref,
    out_w_ref,
    sum_ref,
    leave_ref,
    weight_grad_ref,
    middle_ref,
    middle_low_ref,
    norm_grad_ref,
    total,
    mine,
    near,
    far,
    near_sem,
    far_sem,
    done_sem,
    out_sem,
    cross_sem,
    give_sem,
    mlp_w,
    out_w,
    top_buf,
    hidden_buf,
    pair_buf,
    token_buf,
    leave_buf,
    tile_buf,
    flip_buf,
    piece_buf,
    wide_buf,
    low_buf,
    load_sem,
    piece_sem,
    store_sem,
    wide_sem,
    low_sem,
    ring_recv_sem,
    ring_send_sem,
):
    capacity, width = branch_ref.shape
    units = hidden_buf.shape[1]
    ways = width // mlp_ref.shape[0]
    ring = Ring(ways, (mlp_w, out_w), ring_recv_sem, ring_send_sem)
    blocks, tiles = capacity // block, width // block
    span = 2 * rows
    per, half = block // span, capacity // span
    pairs = 2 * half
    low, f32 = jnp.bfloat16, jnp.float32
    line = Line(rows, mine, near, far, total, near_sem, far_sem, done_sem, out_sem, cross_sem, give_sem)

    def part(index, size=block):
        return pl.ds(pl.multiple_of(index * size, size), size)

    def load_tokens(index):
        return pltpu.make_async_copy(tokens_ref.at[part(index)], token_buf, load_sem.at[3])

    def load_piece(index):
        slot = index % 2
        return pltpu.make_async_copy(
            tokens_ref.at[part(index, span)], piece_buf.at[slot], piece_sem.at[slot]
        )

    def store_leave(index):
        return pltpu.make_async_copy(leave_buf, leave_ref.at[part(index)], store_sem.at[0])

    def store_tile(index):
        return pltpu.make_async_copy(tile_buf, weight_grad_ref.at[part(index)], store_sem.at[1])

    store_sum = pltpu.make_async_copy(total.at[pl.ds(0, capacity)], sum_ref, store_sem.at[2])

    def store_middle(index):
        slot = index % 2
        return [
            pltpu.make_async_copy(
                wide_buf.at[slot], middle_ref.at[part(index, span)], wide_sem.at[slot]
            ),
            pltpu.make_async_copy(
                low_buf.at[slot], middle_low_ref.at[part(index, span)], low_sem.at[slot]
            ),
        ]

    shard = part(ring.me, mlp_ref.shape[0])
    load_mlp = pltpu.make_async_copy(mlp_ref, mlp_w.at[shard], load_sem.at[1])
    load_out = pltpu.make_async_copy(out_w_ref, out_w.at[shard], load_sem.at[2])
    load_mine = pltpu.make_async_copy(branch_ref, mine.at[pl.ds(0, capacity)], load_sem.at[0])
    load_top = pltpu.make_async_copy(top_ref, top_buf, load_sem.at[4])
    load_mlp.start()
    load_out.start()
    load_mine.start()
    line.greet((ring.left, ring.right))
    load_mlp.wait()
    load_out.wait()
    load_mine.wait()
    load_tokens(0).start()
    load_top.start()
    load_piece(0).start()
    norm_grad_ref[...] = jnp.zeros_like(norm_grad_ref)

    def normalize(index):
        def wait(pair, carry):
            line.arrive(pair)
            line.release(pair)
            return carry

        lax.fori_loop(index * per, index * per + per, wait, 0)
        load_tokens(index).wait()

        def normalize_rows(piece, carry):
            here = part(piece, 32)
            there = part(index * (block // 32) + piece, 32)
            values = token_buf[here, :].astype(f32) + total[there, :].astype(f32)
            values, unused_normed, unused_inverse = layer_norm(
                values, gain_ref[...], shift_ref[...], NORM_EPS
            )
            mine[there, :] = values.astype(low)
            return carry

        lax.fori_loop(0, block // 32, normalize_rows, 0)

        @pl.when(index < blocks - 1)
        def _():
            load_tokens(index + 1).start()

        @pl.when(index == blocks - 1)
        def _():
            store_sum.start()

    def units_step(index, start, count):
        @pl.when((index == 0) & (start == 0))
        def _():
            load_top.wait()

        here = part(index)

        def one(number, carry):
            first = part(number, 256)
            second = pl.ds(pl.multiple_of(units + number * 256, 256), 256)
            left = row_product(mine[here, :], mlp_w[:, first])
            right = row_product(mine[here, :], mlp_w[:, second])
            back = row_product(top_buf[here, :], out_w[:, first])
            cdf = 0.5 * (1.0 + lax.erf(left * (1.0 / math.sqrt(2.0))))
            pdf = jnp.exp(-0.5 * left * left) * (1.0 / math.sqrt(2.0 * math.pi))
            gelu = left * cdf
            hidden_buf[here, first] = (gelu * right).astype(low)
            pair_buf[here, first] = (back * right * (cdf + left * pdf)).astype(low)
            pair_buf[here, second] = (back * gelu).astype(low)
            return carry

        lax.fori_loop(start, start + count, one, 0)

    def backward_step(index):
        here = part(index)

        def one(number, carry):
            there = part(number, 256)
            mine[part(blocks + index), there] = turned_product(
                pair_buf[here, :], mlp_w[there, :]
            ).astype(low)
            return carry

        lax.fori_loop(0, width // 256, one, 0)

    def leave_step(index):
        @pl.when(index > 0)
        def _():
            store_leave(index - 1).wait()

        here = part(index)

        def one(number, carry):
            there = part(number, 256)
            leave_buf[:, there] = turned_product(hidden_buf[here, :], out_w[there, :]).astype(low)
            return carry

        lax.fori_loop(0, width // 256, one, 0)
        store_leave(index).start()

    def tile_stage(index):
        @pl.when(index > 0)
        def _():
            store_tile(index - 1).wait()

        here = part(index)
        flip_buf[...] = mine[pl.ds(0, capacity), here].T

        def one(number, carry):
            there = part(number, 512)
            tile_buf[:, there] = row_product(flip_buf[...], pair_buf[:, there]).astype(low)
            return carry

        lax.fori_loop(0, 2 * units // 512, one, 0)
        flip_buf[...] = top_buf[:, here].T

        def last(number, carry):
            there = pl.ds(pl.multiple_of(2 * units + number * 512, 512), 512)
            tile_buf[:, there] = row_product(
                flip_buf[...], hidden_buf[:, part(number, 512)]
            ).astype(low)
            return carry

        lax.fori_loop(0, units // 512, last, 0)
        store_tile(index).start()

    def norm_stage(index):
        line.arrive(half + index)
        load_piece(index).wait()

        @pl.when(index < half - 1)
        def _():
            load_piece(index + 1).start()

        @pl.when(index > 1)
        def _():
            for copy in store_middle(index - 2):
                copy.wait()

        slot, here = index % 2, part(index, span)
        values = piece_buf[slot].astype(f32) + total[here, :].astype(f32)
        back = total[part(half + index, span), :].astype(f32)
        result, gain_grad, shift_grad = norm_back_rows(values, back, gain_ref[...])
        middle = top_buf[here, :].astype(f32) + result
        wide_buf[slot] = middle
        low_buf[slot] = middle.astype(low)
        norm_grad_ref[0:1, :] += gain_grad
        norm_grad_ref[1:2, :] += shift_grad
        for copy in store_middle(index):
            copy.start()

    count = units // 256
    lead = per + 6
    batch = -(-ring.reach // (lead // 2 - 1))

    def step(index, carry):
        line.step(index, pairs)

        @pl.when(index == 0)
        def _():
            ring.step(0)

        @pl.when((index > 1) & (index < lead) & (index % 2 == 1))
        def _():
            for extra in range(batch):
                distance = (index - 3) // 2 * batch + extra + 1

                @pl.when(distance <= ring.reach)
                def _():
                    ring.step(distance)

        work = index - lead

        @pl.when((work >= 0) & (work < 4 * blocks))
        def _():
            piece, stage = work // 4, work % 4

            @pl.when(stage == 0)
            def _():
                normalize(piece)

            @pl.when((stage == 1) | (stage == 2))
            def _():
                units_step(piece, (stage - 1) * (count // 2), count // 2)

            @pl.when(stage == 3)
            def _():
                backward_step(piece)
                leave_step(piece)

        @pl.when((work >= 4 * blocks) & (work < 4 * blocks + tiles))
        def _():
            tile_stage(work - 4 * blocks)

        @pl.when(index >= half + 5)
        def _():
            norm_stage(index - half - 5)

        return carry

    lax.fori_loop(0, pairs + 5, step, 0)

    def drain(pair, carry):
        line.drain(pair)

        @pl.when(pair >= half)
        def _():
            line.release(pair)

        return carry

    lax.fori_loop(0, pairs, drain, 0)
    ring.drain()
    store_leave(blocks - 1).wait()
    store_tile(tiles - 1).wait()
    store_sum.wait()
    for index in (half - 2, half - 1):
        for copy in store_middle(index):
            copy.wait()


def middle_stage(
    branch, tokens, top, gain, shift, mlp_shard, out_shard, collective_id, rows=32, block=256
):
    capacity, width = branch.shape
    units = out_shard.shape[1]
    ways = width // out_shard.shape[0]
    low, f32 = jnp.bfloat16, jnp.float32
    anywhere, held = pl.BlockSpec(memory_space=pl.ANY), pl.BlockSpec(memory_space=pltpu.VMEM)
    pair_sems = pltpu.SemaphoreType.DMA((2,))
    return pl.pallas_call(
        functools.partial(middle_kernel, rows, block),
        out_shape=(
            jax.ShapeDtypeStruct((capacity, width), low),
            jax.ShapeDtypeStruct((capacity, width), low),
            jax.ShapeDtypeStruct((width, 3 * units), low),
            jax.ShapeDtypeStruct((capacity, width), f32),
            jax.ShapeDtypeStruct((capacity, width), low),
            jax.ShapeDtypeStruct((2, width), f32),
        ),
        in_specs=[anywhere, anywhere, anywhere, held, held, anywhere, anywhere],
        out_specs=(anywhere,) * 5 + (held,),
        scratch_shapes=[pltpu.VMEM((2 * capacity, width), low)]
        + line_scratch(2 * capacity, width, rows)
        + [
            pltpu.VMEM((width, 2 * units), low),
            pltpu.VMEM((width, units), low),
            pltpu.VMEM((capacity, width), low),
            pltpu.VMEM((capacity, units), low),
            pltpu.VMEM((capacity, 2 * units), low),
            pltpu.VMEM((block, width), low),
            pltpu.VMEM((block, width), low),
            pltpu.VMEM((block, 3 * units), low),
            pltpu.VMEM((block, capacity), low),
            pltpu.VMEM((2, 2 * rows, width), low),
            pltpu.VMEM((2, 2 * rows, width), f32),
            pltpu.VMEM((2, 2 * rows, width), low),
            pltpu.SemaphoreType.DMA((5,)),
            pair_sems,
            pltpu.SemaphoreType.DMA((3,)),
            pair_sems,
            pair_sems,
        ]
        + ring_scratch(ways, 2),
        compiler_params=pltpu.CompilerParams(
            collective_id=collective_id, has_side_effects=True, vmem_limit_bytes=62 << 20
        ),
        cost_estimate=pl.CostEstimate(
            flops=200_000_000_000, bytes_accessed=40 << 20, transcendentals=0
        ),
    )(branch, tokens, top, gain[None], shift[None], mlp_shard, out_shard)


def turn(values, cosine, sine):
    half = values.shape[1] // 2
    front, back = values[:, :half], values[:, half:]
    return jnp.concatenate([front * cosine - back * sine, front * sine + back * cosine], axis=1)


def decay_block(ends_ref, log_keep, row_start, col_start, size):
    rows = row_start + lax.broadcasted_iota(jnp.int32, (size, 1), 0)
    cols = col_start + lax.broadcasted_iota(jnp.int32, (1, size), 1)
    row_slot = jnp.zeros((size, 1), jnp.int32)
    col_slot = jnp.zeros((1, size), jnp.int32)
    for slot in range(SLOTS):
        row_slot += (rows >= ends_ref[slot]).astype(jnp.int32)
        col_slot += (cols >= ends_ref[slot]).astype(jnp.int32)
    row_slot = jnp.where(rows < ends_ref[SLOTS - 1], row_slot, -1)
    distance = rows - cols
    allowed = (row_slot == col_slot) & (distance >= 0)
    distance = jnp.maximum(distance, 0).astype(jnp.float32)
    return jnp.where(allowed, jnp.exp(distance * log_keep), 0.0)


def group_stats(values):
    center = values - jnp.mean(values, axis=-1, keepdims=True)
    inverse = lax.rsqrt(jnp.mean(center * center, axis=-1, keepdims=True) + GROUP_EPS)
    return center * inverse, inverse


def retain_kernel(
    ends_ref,
    keep_ref,
    first_ref,
    query_w_ref,
    key_w_ref,
    value_w_ref,
    gate_w_ref,
    cos_ref,
    sin_ref,
    gain_ref,
    out_shard_ref,
    query_ref,
    key_ref,
    value_ref,
    gate_ref,
    retained_ref,
    gated_ref,
    branch_ref,
    out_w_ref,
    keys,
    values,
    gated_buf,
    out_w,
    out_sem,
    ring_recv_sem,
    ring_send_sem,
):
    head, block = pl.program_id(0), pl.program_id(1)
    blocks = pl.num_programs(1)
    index, final = head * blocks + block, pl.num_programs(0) * blocks - 1
    size = query_ref.shape[0]
    shard = out_shard_ref.shape[0]
    ring = Ring(out_w.shape[0] // shard, (out_w,), ring_recv_sem, ring_send_sem)
    batch = -(-ring.reach // 4)
    store = pltpu.make_async_copy(out_w, out_w_ref, out_sem.at[1])

    @pl.when(index == 0)
    def _():
        place = pl.ds(pl.multiple_of(ring.me * shard, shard), shard)
        load = pltpu.make_async_copy(out_shard_ref, out_w.at[place], out_sem.at[0])
        load.start()
        ring.greet()
        load.wait()
        ring.step(0)

    def ring_round(number):
        for extra in range(batch):
            distance = number * batch + extra + 1

            @pl.when(distance <= ring.reach)
            def _():
                ring.step(distance)

    @pl.when((index >= 2) & (index < final) & (index % 2 == 0))
    def _():
        ring_round(index // 2 - 1)

    here = pl.ds(pl.multiple_of(block * size, size), size)
    first = first_ref[here, :]
    cosine, sine = cos_ref[here, :], sin_ref[here, :]
    query = turn(row_product(first, query_w_ref[...]), cosine, sine).astype(jnp.bfloat16)
    key = turn(row_product(first, key_w_ref[...]), cosine, sine) * KH ** (-0.5)
    key = key.astype(jnp.bfloat16)
    value = row_product(first, value_w_ref[...]).astype(jnp.bfloat16)
    gate = row_product(first, gate_w_ref[...])
    query_ref[...] = query
    key_ref[...] = key
    value_ref[...] = value
    gate_ref[...] = gate
    keys[here, :] = key
    values[here, :] = value
    retained_ref[...] = jnp.zeros_like(retained_ref)

    def visit(other, carry):
        there = pl.ds(pl.multiple_of(other * size, size), size)
        decay = decay_block(ends_ref, keep_ref[head], block * size, other * size, size)
        weights = (turned_product(query, keys[there, :]) * decay).astype(jnp.bfloat16)
        retained_ref[...] += row_product(weights, values[there, :])
        return carry

    lax.fori_loop(0, block + 1, visit, 0)
    normed, inverse = group_stats(retained_ref[...])
    gated = (gate * jax.nn.sigmoid(gate) * (normed * gain_ref[0])).astype(jnp.bfloat16)
    gated_ref[...] = gated
    gated_buf[here, pl.ds(pl.multiple_of(head * VH, VH), VH)] = gated

    @pl.when(index == final)
    def _():
        ring_round(3)
        store.start()

        def one(number, carry):
            there = pl.ds(pl.multiple_of(number * 256, 256), 256)
            branch_ref[:, there] = turned_product(gated_buf[...], out_w[there, :]).astype(
                jnp.bfloat16
            )
            return carry

        lax.fori_loop(0, out_w.shape[0] // 256, one, 0, unroll=True)
        ring.drain()
        store.wait()


def retain(
    ends, log_keep, first_low, full, cosine, sine, group_values, out_shard, collective_id, size=256
):
    capacity, width = first_low.shape
    heads = group_values.shape[0]
    scalar = pl.BlockSpec(memory_space=pltpu.SMEM)
    table = pl.BlockSpec((capacity, KH // 2), lambda h, r: (0, 0))
    key_block = pl.BlockSpec((size, KH), lambda h, r: (r, h))
    value_block = pl.BlockSpec((size, VH), lambda h, r: (r, h))
    ratio = KH * heads * 2 // VH

    def shape(columns, kind):
        return jax.ShapeDtypeStruct((capacity, heads * columns), kind)

    return pl.pallas_call(
        retain_kernel,
        grid=(heads, capacity // size),
        out_shape=(
            shape(KH, jnp.bfloat16),
            shape(KH, jnp.bfloat16),
            shape(VH, jnp.bfloat16),
            shape(VH, jnp.float32),
            shape(VH, jnp.float32),
            shape(VH, jnp.bfloat16),
            jax.ShapeDtypeStruct((capacity, width), jnp.bfloat16),
            jax.ShapeDtypeStruct((width, heads * VH), jnp.bfloat16),
        ),
        in_specs=[
            scalar,
            scalar,
            pl.BlockSpec((capacity, width), lambda h, r: (0, 0)),
            pl.BlockSpec((width, KH), lambda h, r: (0, h)),
            pl.BlockSpec((width, KH), lambda h, r: (0, heads + h)),
            pl.BlockSpec((width, VH), lambda h, r: (0, ratio + h)),
            pl.BlockSpec((width, VH), lambda h, r: (0, ratio + heads + h)),
            table,
            table,
            pl.BlockSpec((1, 1, VH), lambda h, r: (h, 0, 0)),
            pl.BlockSpec(memory_space=pl.ANY),
        ],
        out_specs=(key_block, key_block, value_block, value_block, value_block, value_block)
        + (
            pl.BlockSpec((capacity, width), lambda h, r: (0, 0)),
            pl.BlockSpec(memory_space=pl.ANY),
        ),
        scratch_shapes=[
            pltpu.VMEM((capacity, KH), jnp.bfloat16),
            pltpu.VMEM((capacity, VH), jnp.bfloat16),
            pltpu.VMEM((capacity, heads * VH), jnp.bfloat16),
            pltpu.VMEM((width, heads * VH), jnp.bfloat16),
            pltpu.SemaphoreType.DMA((2,)),
        ]
        + ring_scratch(width // out_shard.shape[0], 1),
        compiler_params=pltpu.CompilerParams(
            collective_id=collective_id, has_side_effects=True, vmem_limit_bytes=56 << 20
        ),
        cost_estimate=pl.CostEstimate(
            flops=16_000_000_000, bytes_accessed=40 << 20, transcendentals=0
        ),
    )(
        ends,
        log_keep,
        first_low,
        full,
        full,
        full,
        full,
        cosine,
        sine,
        group_values[:, None, :],
        out_shard,
    )


def back_kernel(
    rows,
    block,
    heads,
    ends_ref,
    keep_ref,
    leave_ref,
    middle_low_ref,
    out_w_ref,
    retained_ref,
    gate_ref,
    group_gain_ref,
    query_ref,
    key_ref,
    value_ref,
    cos_ref,
    sin_ref,
    gated_ref,
    first_ref,
    full_ref,
    total,
    weight_grad_ref,
    input_grad_ref,
    group_grad_ref,
    mine,
    near,
    far,
    near_sem,
    far_sem,
    done_sem,
    out_sem,
    cross_sem,
    give_sem,
    out_w,
    query_buf,
    key_buf,
    value_buf,
    gated_buf,
    first_buf,
    middle_low,
    flip_buf,
    grad_buf,
    stream_buf,
    tile_buf,
    input_grad_buf,
    retained_buf,
    gate_buf,
    grad_gated_buf,
    upstream_buf,
    query_grad,
    key_grad,
    value_grad,
    load_sem,
    stream_sem,
    group_sem,
    store_sem,
):
    capacity, width = leave_ref.shape
    blocks, tiles = capacity // block, width // block
    pairs = capacity // (2 * rows)
    finish = heads * blocks
    low, f32 = jnp.bfloat16, jnp.float32
    line = Line(rows, mine, near, far, total, near_sem, far_sem, done_sem, out_sem, cross_sem, give_sem)

    def part(index, size=block):
        return pl.ds(pl.multiple_of(index * size, size), size)

    held = [
        pltpu.make_async_copy(source, target, load_sem.at[index])
        for index, (source, target) in enumerate(
            (
                (leave_ref, mine),
                (middle_low_ref, middle_low),
                (out_w_ref, out_w),
                (query_ref, query_buf),
                (key_ref, key_buf),
                (value_ref, value_buf),
                (gated_ref, gated_buf),
                (first_ref, first_buf),
            )
        )
    ]

    def load_group(index):
        slot = index % 2
        here, there = part(index % blocks), part(index // blocks, VH)
        return [
            pltpu.make_async_copy(
                retained_ref.at[here, there], retained_buf.at[slot], group_sem.at[2 * slot]
            ),
            pltpu.make_async_copy(
                gate_ref.at[here, there], gate_buf.at[slot], group_sem.at[2 * slot + 1]
            ),
        ]

    def load_tile(index):
        slot = index % 2
        return pltpu.make_async_copy(
            full_ref.at[part(index)], stream_buf.at[slot], stream_sem.at[slot]
        )

    def store_tile(index):
        return pltpu.make_async_copy(tile_buf, weight_grad_ref.at[part(index)], store_sem.at[0])

    def store_input(index):
        return pltpu.make_async_copy(
            input_grad_buf, input_grad_ref.at[:, part(index)], store_sem.at[1]
        )

    for copy in held + load_group(0):
        copy.start()
    load_tile(0).start()
    line.greet()
    held[0].wait()
    group_grad_ref[...] = jnp.zeros_like(group_grad_ref)

    def attend_stage(index):
        head, place = index // blocks, index % blocks

        @pl.when(index == 0)
        def _():
            for copy in held[1:-2]:
                copy.wait()

        for copy in load_group(index):
            copy.wait()

        @pl.when(index < heads * blocks - 1)
        def _():
            for copy in load_group(index + 1):
                copy.start()

        @pl.when(place == 0)
        def _():
            key_grad[...] = jnp.zeros_like(key_grad)
            value_grad[...] = jnp.zeros_like(value_grad)

        slot = index % 2
        here = part(place)
        keys_here, values_here = part(head, KH), part(head, VH)
        gain = group_gain_ref[pl.ds(head, 1), :]
        gate_place = pl.ds(pl.multiple_of(heads * (2 * KH + VH) + head * VH, VH), VH)
        grad_gated_buf[...] = row_product(middle_low[here, :], out_w[:, values_here])

        def gate_rows(piece, carry):
            few = pl.ds(pl.multiple_of(piece * 32, 32), 32)
            there = pl.ds(pl.multiple_of(place * block + piece * 32, 32), 32)
            normed, inverse = group_stats(retained_buf[slot, few, :])
            gate, grad_gated = gate_buf[slot, few, :], grad_gated_buf[few, :]
            sigmoid = jax.nn.sigmoid(gate)
            slope = sigmoid * (1.0 + gate * (1.0 - sigmoid))
            grad_buf[there, gate_place] = (grad_gated * (normed * gain) * slope).astype(low)
            grad_out = grad_gated * (gate * sigmoid)
            group_grad_ref[pl.ds(head, 1), :] += jnp.sum(grad_out * normed, axis=0, keepdims=True)
            scaled = grad_out * gain
            plain_mean = jnp.mean(scaled, axis=-1, keepdims=True)
            cross_mean = jnp.mean(scaled * normed, axis=-1, keepdims=True)
            upstream_buf[few, :] = (
                inverse * (scaled - plain_mean - normed * cross_mean)
            ).astype(low)
            return carry

        lax.fori_loop(0, block // 32, gate_rows, 0, unroll=4)
        upstream = upstream_buf[...]
        query = query_buf[here, keys_here]
        query_grad[...] = jnp.zeros_like(query_grad)

        def visit(other, carry):
            there = part(other)
            decay = decay_block(ends_ref, keep_ref[head], place * block, other * block, block)
            key = key_buf[there, keys_here]
            weights = (turned_product(query, key) * decay).astype(low)
            value_grad[there, :] += outer_product(weights, upstream)
            scores = turned_product(upstream, value_buf[there, values_here]) * decay
            scores = scores.astype(low)
            query_grad[...] += row_product(scores, key)
            key_grad[there, :] += outer_product(scores, query)
            return carry

        lax.fori_loop(0, place + 1, visit, 0)
        cosine, sine = cos_ref[here, :], sin_ref[here, :]
        grad_buf[here, keys_here] = turn(query_grad[...], cosine, -sine).astype(low)

        @pl.when(place == blocks - 1)
        def _():
            def one(other, carry):
                there = part(other)
                turned = turn(key_grad[there, :] * KH ** (-0.5), cos_ref[there, :], -sin_ref[there, :])
                grad_buf[there, part(heads + head, KH)] = turned.astype(low)
                value_place = pl.ds(pl.multiple_of(heads * 2 * KH + head * VH, VH), VH)
                grad_buf[there, value_place] = value_grad[there, :].astype(low)
                return carry

            lax.fori_loop(0, blocks, one, 0)

    def tile_stage(index):
        columns = grad_buf.shape[1]

        @pl.when(index == 0)
        def _():
            for copy in held[-2:]:
                copy.wait()

        @pl.when(index < tiles - 1)
        def _():
            load_tile(index + 1).start()

        @pl.when(index > 0)
        def _():
            store_tile(index - 1).wait()
            store_input(index - 1).wait()

        load_tile(index).wait()
        here = part(index)
        flip_buf[...] = first_buf[:, here].T

        def one(number, carry):
            there = part(number, 512)
            tile_buf[:, there] = row_product(flip_buf[...], grad_buf[:, there]).astype(low)
            return carry

        lax.fori_loop(0, columns // 512, one, 0, unroll=True)

        flip_buf[...] = middle_low[:, here].T

        def last(number, carry):
            there = pl.ds(pl.multiple_of(columns + number * 512, 512), 512)
            tile_buf[:, there] = row_product(
                flip_buf[...], gated_buf[:, part(number, 512)]
            ).astype(low)
            return carry

        lax.fori_loop(0, gated_buf.shape[1] // 512, last, 0, unroll=True)
        store_tile(index).start()

        def inward(number, carry):
            there = part(number)
            input_grad_buf[there, :] = turned_product(
                grad_buf[there, :], stream_buf[index % 2]
            ).astype(low)
            return carry

        lax.fori_loop(0, blocks, inward, 0, unroll=True)
        store_input(index).start()

    def step(index, carry):
        line.step(index, pairs)

        @pl.when(index < finish)
        def _():
            attend_stage(index)

        @pl.when((index >= finish) & (index < finish + tiles))
        def _():
            tile_stage(index - finish)

        return carry

    lax.fori_loop(0, max(pairs + 3, finish + tiles), step, 0)

    def drain(pair, carry):
        line.arrive(pair)
        line.release(pair)
        line.drain(pair)
        return carry

    lax.fori_loop(0, pairs, drain, 0)
    store_tile(tiles - 1).wait()
    store_input(tiles - 1).wait()


def back_stage(
    ends,
    log_keep,
    leave,
    middle_low,
    mix_out,
    retained,
    gate,
    group_values,
    query,
    key,
    value,
    cosine,
    sine,
    gated,
    first_low,
    full,
    collective_id,
    rows=32,
    block=256,
):
    capacity, width = leave.shape
    heads = group_values.shape[0]
    columns, units = full.shape[1], gated.shape[1]
    low, f32 = jnp.bfloat16, jnp.float32
    anywhere, kept = pl.BlockSpec(memory_space=pl.ANY), pl.BlockSpec(memory_space=pltpu.VMEM)
    scalar = pl.BlockSpec(memory_space=pltpu.SMEM)
    return pl.pallas_call(
        functools.partial(back_kernel, rows, block, heads),
        out_shape=(
            jax.ShapeDtypeStruct((capacity, width), low),
            jax.ShapeDtypeStruct((width, columns + units), low),
            jax.ShapeDtypeStruct((capacity, width), low),
            jax.ShapeDtypeStruct((heads, VH), f32),
        ),
        in_specs=[scalar] * 2
        + [anywhere] * 5
        + [kept]
        + [anywhere] * 3
        + [kept] * 2
        + [anywhere] * 3,
        out_specs=(kept, anywhere, anywhere, kept),
        scratch_shapes=line_scratch(capacity, width, rows)
        + [
            pltpu.VMEM((width, units), low),
            pltpu.VMEM(query.shape, low),
            pltpu.VMEM(key.shape, low),
            pltpu.VMEM(value.shape, low),
            pltpu.VMEM(gated.shape, low),
            pltpu.VMEM((capacity, width), low),
            pltpu.VMEM((capacity, width), low),
            pltpu.VMEM((block, capacity), low),
            pltpu.VMEM((capacity, columns), low),
            pltpu.VMEM((2, block, columns), low),
            pltpu.VMEM((block, columns + units), low),
            pltpu.VMEM((capacity, block), low),
            pltpu.VMEM((2, block, VH), f32),
            pltpu.VMEM((2, block, VH), f32),
            pltpu.VMEM((block, VH), f32),
            pltpu.VMEM((block, VH), low),
            pltpu.VMEM((block, KH), f32),
            pltpu.VMEM((capacity, KH), f32),
            pltpu.VMEM((capacity, VH), f32),
            pltpu.SemaphoreType.DMA((8,)),
            pltpu.SemaphoreType.DMA((2,)),
            pltpu.SemaphoreType.DMA((4,)),
            pltpu.SemaphoreType.DMA((2,)),
        ],
        compiler_params=pltpu.CompilerParams(
            collective_id=collective_id, has_side_effects=True, vmem_limit_bytes=62 << 20
        ),
        cost_estimate=pl.CostEstimate(
            flops=100_000_000_000, bytes_accessed=40 << 20, transcendentals=0
        ),
    )(
        ends,
        log_keep,
        leave,
        middle_low,
        mix_out,
        retained,
        gate,
        group_values,
        query,
        key,
        value,
        cosine,
        sine,
        gated,
        first_low,
        full,
    )


def last_kernel(
    rows,
    ways,
    back_ref,
    tokens_ref,
    middle_ref,
    sum_ref,
    leave_ref,
    norm_gain_ref,
    norm_grad_ref,
    group_grad_ref,
    token_grad_ref,
    layer_ref,
    small_ref,
    total,
    mine,
    near,
    far,
    near_sem,
    far_sem,
    done_sem,
    out_sem,
    cross_sem,
    give_sem,
    token_buf,
    middle_buf,
    sum_buf,
    leave_buf,
    layer_buf,
    small_buf,
    small_in,
    load_sem,
    store_sem,
    layer_sem,
    small_send_sem,
    small_recv_sem,
):
    capacity, width = back_ref.shape
    pairs = capacity // (2 * rows)
    heads, group = group_grad_ref.shape
    f32 = jnp.float32
    line = Line(rows, mine, near, far, total, near_sem, far_sem, done_sem, out_sem, cross_sem, give_sem)
    me = lax.axis_index("dp")
    peers = [lax.rem(me + distance, ways) for distance in range(1, ways)]
    loads = [
        pltpu.make_async_copy(source, target, load_sem.at[index])
        for index, (source, target) in enumerate(
            (
                (back_ref, mine),
                (tokens_ref, token_buf),
                (middle_ref, middle_buf),
                (sum_ref, sum_buf),
                (leave_ref, leave_buf),
            )
        )
    ]

    def part(pair):
        return pl.ds(pl.multiple_of(pair * 2 * rows, 2 * rows), 2 * rows)

    def store(pair):
        return pltpu.make_async_copy(
            middle_buf.at[part(pair)], token_grad_ref.at[part(pair)], store_sem.at[pair]
        )

    def store_layer(pair):
        slot = pair % 2
        return pltpu.make_async_copy(
            layer_buf.at[slot], layer_ref.at[part(pair)], layer_sem.at[slot]
        )

    def share(distance):
        return pltpu.make_async_remote_copy(
            small_buf,
            small_in.at[distance],
            small_send_sem.at[distance],
            small_recv_sem.at[distance],
            device_id={"dp": peers[distance]},
            device_id_type=MESH,
        )

    for copy in loads:
        copy.start()
    line.greet(peers)
    small_buf[...] = jnp.zeros_like(small_buf)
    small_buf[2:4, :] = norm_grad_ref[...]
    for head in range(heads):
        small_buf[4:5, head * group : (head + 1) * group] = group_grad_ref[head : head + 1, :]
    loads[0].wait()

    def norm_stage(pair):
        line.arrive(pair)

        @pl.when(pair == 0)
        def _():
            for copy in loads[1:]:
                copy.wait()

        @pl.when(pair > 1)
        def _():
            store_layer(pair - 2).wait()

        here = part(pair)
        values = token_buf[here, :].astype(f32)
        layer_buf[pair % 2] = (
            values + sum_buf[here, :].astype(f32) + leave_buf[here, :].astype(f32)
        )
        result, gain_grad, shift_grad = norm_back_rows(
            values, total[here, :].astype(f32), norm_gain_ref[...]
        )
        middle_buf[here, :] += result
        small_buf[0:1, :] += gain_grad
        small_buf[1:2, :] += shift_grad
        store(pair).start()
        store_layer(pair).start()

    def step(index, carry):
        line.step(index, pairs)

        @pl.when(index >= 5)
        def _():
            norm_stage(index - 5)

        return carry

    lax.fori_loop(0, pairs + 5, step, 0)
    for distance in range(ways - 1):
        share(distance).start()

    def drain(pair, carry):
        line.release(pair)
        line.drain(pair)
        store(pair).wait()
        return carry

    lax.fori_loop(0, pairs, drain, 0)
    store_layer(pairs - 2).wait()
    store_layer(pairs - 1).wait()
    for distance in range(ways - 1):
        share(distance).wait()
    small_ref[...] = small_buf[...]
    for distance in range(ways - 1):
        small_ref[...] += small_in[distance]


def last_stage(
    back,
    tokens,
    middle,
    branch_sum,
    leave_sum,
    norm_gain,
    norm_grad,
    group_grad,
    ways,
    collective_id,
    rows=32,
):
    capacity, width = back.shape
    low, f32 = jnp.bfloat16, jnp.float32
    anywhere, kept = pl.BlockSpec(memory_space=pl.ANY), pl.BlockSpec(memory_space=pltpu.VMEM)
    small = (8, width)
    return pl.pallas_call(
        functools.partial(last_kernel, rows, ways),
        out_shape=(
            jax.ShapeDtypeStruct((capacity, width), f32),
            jax.ShapeDtypeStruct((capacity, width), f32),
            jax.ShapeDtypeStruct(small, f32),
        ),
        in_specs=[anywhere] * 5 + [kept] * 3,
        out_specs=(anywhere, anywhere, kept),
        scratch_shapes=[pltpu.VMEM((capacity, width), low)]
        + line_scratch(capacity, width, rows)
        + [
            pltpu.VMEM((capacity, width), low),
            pltpu.VMEM((capacity, width), f32),
            pltpu.VMEM((capacity, width), low),
            pltpu.VMEM((capacity, width), low),
            pltpu.VMEM((2, 2 * rows, width), f32),
            pltpu.VMEM(small, f32),
            pltpu.VMEM((ways - 1, *small), f32),
            pltpu.SemaphoreType.DMA((5,)),
            pltpu.SemaphoreType.DMA((capacity // (2 * rows),)),
            pltpu.SemaphoreType.DMA((2,)),
            pltpu.SemaphoreType.DMA((ways - 1,)),
            pltpu.SemaphoreType.DMA((ways - 1,)),
        ],
        compiler_params=pltpu.CompilerParams(
            collective_id=collective_id, has_side_effects=True, vmem_limit_bytes=52 << 20
        ),
        cost_estimate=pl.CostEstimate(
            flops=100_000_000_000, bytes_accessed=40 << 20, transcendentals=0
        ),
    )(back, tokens, middle, branch_sum, leave_sum, norm_gain[None], norm_grad, group_grad)


def local(
    tokens,
    lengths,
    cotangent,
    qk_weight,
    qk_first,
    qk_second,
    inner_weight,
    inner_first,
    inner_second,
    outer_weight,
    outer_first,
    outer_second,
    norm_params,
    norm_first,
    norm_second,
    group_gain,
    group_first,
    group_second,
):
    capacity = tokens.shape[0]
    local_heads = group_gain.shape[0]
    low = jnp.bfloat16
    tensor_index, data_index = lax.axis_index("tensor"), lax.axis_index("dp")

    def joined(shards):
        return jnp.concatenate([part.astype(low) for part in shards], axis=1)

    def gather(shards):
        return lax.all_gather(joined(shards), "dp", axis=0, tiled=True)

    def scatter(grad):
        return lax.psum_scatter(grad, "dp", scatter_dimension=0, tiled=True)

    norm_cols, group_cols = norm_params.shape[1], group_gain.shape[1]
    small = lax.all_gather(
        jnp.concatenate([norm_params.reshape(-1), group_gain.reshape(-1)]).astype(low), "dp"
    ).astype(jnp.float32)
    ways = small.shape[0]
    norm_values = small[:, : 4 * norm_cols].reshape(ways, 4, norm_cols)
    norm_values = norm_values.transpose(1, 0, 2).reshape(4, -1)
    group_values = small[:, 4 * norm_cols :].reshape(ways, local_heads, group_cols)
    group_values = group_values.transpose(1, 0, 2).reshape(local_heads, -1)
    first_full = gather([qk_weight[0], qk_weight[1], inner_weight[0], inner_weight[1]])
    mix_shard = outer_weight[0].astype(low)
    mlp_shard = joined([inner_weight[2], inner_weight[3]])
    out_shard = outer_weight[1].astype(low)
    row_index, sequence_id, position, live_rows = sequence_layout(lengths[0], capacity)
    cosine, sine = rotation_tables(position, KH)
    ends = jnp.cumsum(lengths[0])
    head_ids = tensor_index * local_heads + jnp.arange(local_heads, dtype=jnp.int32)
    log_keep = jnp.log1p(-jnp.exp2(-(5.0 + head_ids.astype(jnp.float32))))
    inputs = tokens.astype(jnp.float32)
    first_out, unused_normed, unused_inverse = layer_norm(
        inputs, norm_values[0], norm_values[1], NORM_EPS
    )
    first_low = first_out.astype(low)
    query, key, value, gate, retained, gated, branch, mix_out = retain(
        ends, log_keep, first_low, first_full, cosine, sine, group_values, mix_shard, 3
    )
    grad_top = cotangent.astype(jnp.float32) * live_rows.astype(jnp.float32)[:, None]
    top_low = grad_top.astype(low)
    branch_sum, leave, mlp_grad, grad_middle, middle_low, norm_two = middle_stage(
        branch, tokens, top_low, norm_values[2], norm_values[3], mlp_shard, out_shard, 0
    )
    mlp_part = scatter(mlp_grad)
    leave_sum, first_grad, back_first, grad_group_gain = back_stage(
        ends,
        log_keep,
        leave,
        middle_low,
        mix_out,
        retained,
        gate,
        group_values,
        query,
        key,
        value,
        cosine,
        sine,
        gated,
        first_low,
        first_full,
        1,
    )
    first_part = scatter(first_grad)
    back_first, mlp_part = lax.optimization_barrier((back_first, mlp_part))
    token_grad, layer_out, small_grad = last_stage(
        back_first,
        tokens,
        grad_middle,
        branch_sum,
        leave_sum,
        norm_values[0],
        norm_two,
        grad_group_gain,
        ways,
        2,
    )
    norm_grad = lax.dynamic_slice(small_grad, (0, data_index * norm_cols), (4, norm_cols))
    group_grad = lax.dynamic_slice(
        small_grad[4, : local_heads * VH].reshape(local_heads, VH),
        (0, data_index * group_cols),
        (local_heads, group_cols),
    )
    qk_cols, mix_cols = local_heads * KH, local_heads * VH
    starts = [qk_cols, 2 * qk_cols, 2 * qk_cols + mix_cols, 2 * qk_cols + 2 * mix_cols]
    query_grad, key_grad, value_grad, gate_grad, mix_out_part = jnp.split(
        first_part, starts, axis=1
    )
    qk_grad = jnp.stack([query_grad, key_grad]).astype(jnp.float32)
    units = out_shard.shape[1]
    left_grad, right_grad, mlp_out_part = jnp.split(mlp_part, [units, 2 * units], axis=1)
    inner_grad = jnp.stack([value_grad, gate_grad, left_grad, right_grad]).astype(jnp.float32)
    outer_grad = jnp.stack([mix_out_part, mlp_out_part]).astype(jnp.float32)
    qk_new = adam_update(qk_weight, qk_grad, qk_first, qk_second, MATRIX_RATE, WEIGHT_DECAY)
    inner_new = adam_update(
        inner_weight, inner_grad, inner_first, inner_second, MATRIX_RATE, WEIGHT_DECAY
    )
    outer_new = adam_update(
        outer_weight, outer_grad, outer_first, outer_second, MATRIX_RATE, WEIGHT_DECAY
    )
    norm_new = adam_update(norm_params, norm_grad, norm_first, norm_second, VECTOR_RATE, 0.0)
    group_new = adam_update(group_gain, group_grad, group_first, group_second, VECTOR_RATE, 0.0)
    return (layer_out, token_grad, *qk_new, *inner_new, *outer_new, *norm_new, *group_new)


def solution(mesh):
    in_specs = (
        P("dp", None),
        P("dp", None),
        P("dp", None),
        P(None, "dp", "tensor"),
        P(None, "dp", "tensor"),
        P(None, "dp", "tensor"),
        P(None, "dp", "tensor"),
        P(None, "dp", "tensor"),
        P(None, "dp", "tensor"),
        P(None, "dp", "tensor"),
        P(None, "dp", "tensor"),
        P(None, "dp", "tensor"),
        P(None, "dp"),
        P(None, "dp"),
        P(None, "dp"),
        P("tensor", "dp"),
        P("tensor", "dp"),
        P("tensor", "dp"),
    )
    out_specs = (
        P("dp", None),
        P("dp", None),
        P(None, "dp", "tensor"),
        P(None, "dp", "tensor"),
        P(None, "dp", "tensor"),
        P(None, "dp", "tensor"),
        P(None, "dp", "tensor"),
        P(None, "dp", "tensor"),
        P(None, "dp", "tensor"),
        P(None, "dp", "tensor"),
        P(None, "dp", "tensor"),
        P(None, "dp"),
        P(None, "dp"),
        P(None, "dp"),
        P("tensor", "dp"),
        P("tensor", "dp"),
        P("tensor", "dp"),
    )
    return jax.shard_map(local, mesh=mesh, in_specs=in_specs, out_specs=out_specs, check_vma=False)
```

```python
import functools
import math

import jax
import jax.numpy as jnp
from jax import lax
from jax.experimental import pallas as pl
from jax.experimental.pallas import tpu as pltpu
from jax.sharding import PartitionSpec as P

MESH = pl.DeviceIdType.MESH

KH = 256
VH = 512
SLOTS = 4
STEP = 10


NORM_EPS = 1e-05
GROUP_EPS = 1.0
BETA_FIRST = 0.9
BETA_SECOND = 0.95
ADAM_EPS = 1e-08
MATRIX_RATE = 0.05
VECTOR_RATE = 0.5
WEIGHT_DECAY = 0.1


def layer_norm(values, gain_row, shift_row, epsilon):
    center = values - jnp.mean(values, axis=-1, keepdims=True)
    inverse = lax.rsqrt(jnp.mean(center * center, axis=-1, keepdims=True) + epsilon)
    normed = center * inverse
    return (normed * gain_row + shift_row, normed, inverse)


def norm_back(upstream, normed, inverse, gain_row):
    scaled = upstream * gain_row
    plain_mean = jnp.mean(scaled, axis=-1, keepdims=True)
    cross_mean = jnp.mean(scaled * normed, axis=-1, keepdims=True)
    result = inverse * (scaled - plain_mean - normed * cross_mean)
    return (result, jnp.sum(upstream * normed, axis=0), jnp.sum(upstream, axis=0))


def sequence_layout(lengths_row, capacity):
    seq_ends = jnp.cumsum(lengths_row)
    row_index = jnp.arange(capacity, dtype=jnp.int32)
    sequence_id = jnp.sum((row_index[:, None] >= seq_ends[None, :]).astype(jnp.int32), axis=1)
    starts = seq_ends - lengths_row
    slot_index = jnp.arange(lengths_row.shape[0], dtype=jnp.int32)
    row_start = jnp.sum(
        jnp.where(sequence_id[:, None] == slot_index[None, :], starts[None, :], 0), axis=1
    )
    position = row_index - row_start
    live_rows = row_index < seq_ends[-1]
    return (row_index, sequence_id, position, live_rows)


def decay_table(row_index, sequence_id, live_rows, head_ids):
    allowed = (
        (sequence_id[:, None] == sequence_id[None, :])
        & (row_index[:, None] >= row_index[None, :])
        & live_rows[:, None]
        & live_rows[None, :]
    )
    distance = jnp.maximum(row_index[:, None] - row_index[None, :], 0).astype(jnp.float32)
    log_keep = jnp.log1p(-jnp.exp2(-(5.0 + head_ids.astype(jnp.float32))))
    return jnp.where(allowed[None], jnp.exp(distance[None] * log_keep[:, None, None]), 0.0)


def rotation_tables(position, head_size):
    half_size = head_size // 2
    frequency = jnp.exp(
        -math.log(10000.0) * 2.0 * jnp.arange(half_size, dtype=jnp.float32) / head_size
    )
    angles = position.astype(jnp.float32)[:, None] * frequency[None, :]
    return (jnp.cos(angles), jnp.sin(angles))


def rotate(values, cosine, sine, head_size):
    row_count = values.shape[0]
    shaped = values.reshape(row_count, -1, 2, head_size // 2)
    front_half = shaped[:, :, 0]
    back_half = shaped[:, :, 1]
    cos_rows = cosine[:, None, :]
    sin_rows = sine[:, None, :]
    turned = jnp.stack(
        [
            front_half * cos_rows - back_half * sin_rows,
            front_half * sin_rows + back_half * cos_rows,
        ],
        axis=2,
    )
    return turned.reshape(row_count, -1)


def row_product(left, right):
    return jnp.dot(left, right, preferred_element_type=jnp.float32)


def turned_product(left, right):
    return lax.dot_general(
        left, right, (((1,), (1,)), ((), ())), preferred_element_type=jnp.float32
    )


def outer_product(left, right):
    return lax.dot_general(
        left, right, (((0,), (0,)), ((), ())), preferred_element_type=jnp.float32
    )


def adam_update(weight, gradient, moment, square, rate, decay_rate):
    moment_new = BETA_FIRST * moment + (1.0 - BETA_FIRST) * gradient
    square_new = BETA_SECOND * square + (1.0 - BETA_SECOND) * gradient * gradient
    first_hat = moment_new / (1.0 - BETA_FIRST**STEP)
    second_hat = square_new / (1.0 - BETA_SECOND**STEP)
    weight_new = weight - rate * (
        first_hat / (jnp.sqrt(second_hat) + ADAM_EPS) + decay_rate * weight
    )
    return (moment_new, square_new, weight_new)


class Ring:
    def __init__(self, count, results, recv_sem, send_sem):
        self.count, self.results, self.recv_sem, self.send_sem = count, results, recv_sem, send_sem
        me = lax.axis_index("dp")
        self.me, self.place = me, self.swap(me)
        self.right, self.left = self.owner(1), self.owner(-1)
        self.reach = count // 2

    def swap(self, index):
        if self.count != 8:
            return index
        return jnp.where(index < 4, index, jnp.where(index < 6, index + 2, index - 2))

    def owner(self, distance):
        return self.swap(lax.rem(self.place + distance + self.count, self.count))

    def greet(self):
        barrier = pltpu.get_barrier_semaphore()
        for device in (self.left, self.right):
            pl.semaphore_signal(barrier, inc=1, device_id={"dp": device}, device_id_type=MESH)
        pl.semaphore_wait(barrier, 2)

    def copies(self, owner, half, way):
        made = []
        for index, result in enumerate(self.results):
            rows = result.shape[0] // (2 * self.count)
            here = result.at[pl.ds(pl.multiple_of((owner * 2 + half) * rows, rows), rows)]
            made.append(
                pltpu.make_async_remote_copy(
                    here,
                    here,
                    self.send_sem.at[((way * 2 + half) * len(self.results) + index) * self.count + owner],
                    self.recv_sem.at[(half * len(self.results) + index) * self.count + owner],
                    device_id={"dp": self.left if way else self.right},
                    device_id_type=MESH,
                )
            )
        return made

    def streams(self):
        for half in range(2):
            for way in range(2):
                yield half, way, self.reach - (half + way) % 2

    def step(self, distance):
        for half, way, hops in self.streams():
            owner = self.owner(distance if way else -distance)

            @pl.when((distance >= 1) & (distance <= hops))
            def _():
                for copy in self.copies(owner, half, way):
                    copy.wait_recv()

            @pl.when(distance < hops)
            def _():
                for copy in self.copies(owner, half, way):
                    copy.start()

    def drain(self):
        for half, way, hops in self.streams():

            def one(distance, carry):
                for copy in self.copies(self.owner(distance if way else -distance), half, way):
                    copy.wait_send()
                return carry

            lax.fori_loop(0, hops, one, 0)


def ring_scratch(count, results):
    return [
        pltpu.SemaphoreType.DMA((2 * results * count,)),
        pltpu.SemaphoreType.DMA((4 * results * count,)),
    ]


class Line:
    def __init__(self, rows, mine, near, far, total, near_sem, far_sem, done_sem, out_sem, cross_sem, give_sem, lags=(1, 3)):
        self.lags = lags
        self.rows, self.mine, self.near, self.far, self.total = rows, mine, near, far, total
        self.near_sem, self.far_sem, self.done_sem = near_sem, far_sem, done_sem
        self.out_sem, self.cross_sem, self.give_sem = out_sem, cross_sem, give_sem
        me = lax.axis_index("tensor")
        self.me = me
        self.inner = (me == 1) | (me == 2)
        self.outer = (me == 0) | (me == 3)
        self.relay_to = jnp.where(self.inner, 3 - me, 1 + me // 3)
        self.away = jnp.where(self.inner, 3 * (me - 1), 1 + me // 3)
        owner = jnp.where(self.inner, me, 1 + me // 3)
        self.kept, self.passed = owner - 1, 2 - owner

    def at(self, chunk):
        return pl.ds(pl.multiple_of(chunk * self.rows, self.rows), self.rows)

    def greet(self, also=()):
        barrier = pltpu.get_barrier_semaphore()
        for device in also:
            pl.semaphore_signal(barrier, inc=1, device_id={"dp": device}, device_id_type=MESH)
        pl.semaphore_signal(barrier, inc=1, device_id={"tensor": self.away}, device_id_type=MESH)

        @pl.when(self.inner)
        def _():
            pl.semaphore_signal(
                barrier, inc=1, device_id={"tensor": self.relay_to}, device_id_type=MESH
            )
            pl.semaphore_wait(barrier, 2 + len(also))

        @pl.when(self.outer)
        def _():
            pl.semaphore_wait(barrier, 1 + len(also))

    def copy(self, source, target, send_sem, recv_sem, device):
        return pltpu.make_async_remote_copy(
            source, target, send_sem, recv_sem, device_id={"tensor": device}, device_id_type=MESH
        )

    def send_in(self, chunk):
        return self.copy(
            self.mine.at[self.at(chunk)],
            self.near.at[self.at(chunk)],
            self.out_sem.at[chunk],
            self.near_sem.at[chunk],
            self.away,
        )

    def send_across(self, pair, chunk):
        return self.copy(
            self.near.at[self.at(chunk)],
            self.far.at[self.at(pair)],
            self.out_sem.at[chunk],
            self.far_sem.at[pair],
            self.relay_to,
        )

    def give(self, chunk, send_sem, device):
        place = self.total.at[self.at(chunk)]
        return self.copy(place, place, send_sem, self.done_sem.at[chunk], device)

    def give_out(self, chunk):
        return self.give(chunk, self.give_sem.at[chunk], self.away)

    def give_across(self, pair, chunk):
        return self.give(chunk, self.cross_sem.at[pair], self.relay_to)

    def wide(self, ref, chunk):
        return ref[self.at(chunk), :].astype(jnp.float32)

    def relay(self, pair):
        passed, kept = 2 * pair + self.passed, 2 * pair + self.kept

        @pl.when(self.outer)
        def _():
            self.send_in(passed).start()
            self.send_in(kept).start()

        @pl.when(self.inner)
        def _():
            self.send_in(passed).wait_recv()
            added = self.wide(self.near, passed) + self.wide(self.mine, passed)
            self.near[self.at(passed), :] = added.astype(jnp.bfloat16)
            self.send_across(pair, passed).start()

    def own(self, pair):
        kept = 2 * pair + self.kept

        @pl.when(self.inner)
        def _():
            self.send_in(kept).wait_recv()
            self.send_across(pair, kept).wait_recv()
            added = self.wide(self.near, kept) + self.wide(self.mine, kept)
            added = added + self.wide(self.far, pair)
            self.total[self.at(kept), :] = added.astype(jnp.bfloat16)
            self.give_across(pair, kept).start()
            self.give_out(kept).start()

    def forward(self, pair):
        passed = 2 * pair + self.passed

        @pl.when(self.inner)
        def _():
            self.give_out(passed).wait_recv()
            self.give_out(passed).start()

    def step(self, index, pairs):
        own_lag, forward_lag = self.lags

        @pl.when(index < pairs)
        def _():
            self.relay(index)

        @pl.when((index >= own_lag) & (index < pairs + own_lag))
        def _():
            self.own(index - own_lag)

        @pl.when((index >= forward_lag) & (index < pairs + forward_lag))
        def _():
            self.forward(index - forward_lag)

    def arrive(self, pair):
        @pl.when(self.outer)
        def _():
            self.give_out(2 * pair).wait_recv()
            self.give_out(2 * pair + 1).wait_recv()

    def release(self, pair):
        @pl.when(self.outer)
        def _():
            self.send_in(2 * pair).wait_send()
            self.send_in(2 * pair + 1).wait_send()

    def drain(self, pair):
        passed, kept = 2 * pair + self.passed, 2 * pair + self.kept

        @pl.when(self.inner)
        def _():
            self.send_across(pair, passed).wait_send()
            self.give_across(pair, kept).wait_send()
            self.give_out(kept).wait_send()
            self.give_out(passed).wait_send()


def line_scratch(height, width, rows):
    chunks = height // rows
    wide = pltpu.VMEM((height, width), jnp.bfloat16)
    sems, half_sems = pltpu.SemaphoreType.DMA((chunks,)), pltpu.SemaphoreType.DMA((chunks // 2,))
    return [
        wide,
        wide,
        pltpu.VMEM((height // 2, width), jnp.bfloat16),
        sems,
        half_sems,
        sems,
        sems,
        half_sems,
        sems,
    ]


def norm_back_rows(values, back, gain_row):
    center = values - jnp.mean(values, axis=-1, keepdims=True)
    inverse = lax.rsqrt(jnp.mean(center * center, axis=-1, keepdims=True) + NORM_EPS)
    normed = center * inverse
    result, gain_grad, shift_grad = norm_back(back, normed, inverse, gain_row)
    return result, gain_grad[None], shift_grad[None]


def middle_kernel(
    rows,
    block,
    branch_ref,
    tokens_ref,
    top_ref,
    gain_ref,
    shift_ref,
    mlp_ref,
    out_w_ref,
    sum_ref,
    leave_ref,
    weight_grad_ref,
    middle_ref,
    middle_low_ref,
    norm_grad_ref,
    total,
    mine,
    near,
    far,
    near_sem,
    far_sem,
    done_sem,
    out_sem,
    cross_sem,
    give_sem,
    mlp_w,
    out_w,
    top_buf,
    hidden_buf,
    pair_buf,
    token_buf,
    leave_buf,
    tile_buf,
    flip_buf,
    piece_buf,
    wide_buf,
    low_buf,
    load_sem,
    piece_sem,
    store_sem,
    wide_sem,
    low_sem,
    ring_recv_sem,
    ring_send_sem,
):
    capacity, width = branch_ref.shape
    units = hidden_buf.shape[1]
    ways = width // mlp_ref.shape[0]
    ring = Ring(ways, (mlp_w, out_w), ring_recv_sem, ring_send_sem)
    blocks, tiles = capacity // block, width // block
    span = 2 * rows
    per, half = block // span, capacity // span
    pairs = 2 * half
    low, f32 = jnp.bfloat16, jnp.float32
    line = Line(rows, mine, near, far, total, near_sem, far_sem, done_sem, out_sem, cross_sem, give_sem)

    def part(index, size=block):
        return pl.ds(pl.multiple_of(index * size, size), size)

    def load_tokens(index):
        return pltpu.make_async_copy(tokens_ref.at[part(index)], token_buf, load_sem.at[3])

    def load_piece(index):
        slot = index % 2
        return pltpu.make_async_copy(
            tokens_ref.at[part(index, span)], piece_buf.at[slot], piece_sem.at[slot]
        )

    def store_leave(index):
        return pltpu.make_async_copy(leave_buf, leave_ref.at[part(index)], store_sem.at[0])

    def store_tile(index):
        return pltpu.make_async_copy(tile_buf, weight_grad_ref.at[part(index)], store_sem.at[1])

    store_sum = pltpu.make_async_copy(total.at[pl.ds(0, capacity)], sum_ref, store_sem.at[2])

    def store_middle(index):
        slot = index % 2
        return [
            pltpu.make_async_copy(
                wide_buf.at[slot], middle_ref.at[part(index, span)], wide_sem.at[slot]
            ),
            pltpu.make_async_copy(
                low_buf.at[slot], middle_low_ref.at[part(index, span)], low_sem.at[slot]
            ),
        ]

    shard = part(ring.me, mlp_ref.shape[0])
    load_mlp = pltpu.make_async_copy(mlp_ref, mlp_w.at[shard], load_sem.at[1])
    load_out = pltpu.make_async_copy(out_w_ref, out_w.at[shard], load_sem.at[2])
    load_mine = pltpu.make_async_copy(branch_ref, mine.at[pl.ds(0, capacity)], load_sem.at[0])
    load_top = pltpu.make_async_copy(top_ref, top_buf, load_sem.at[4])
    load_mine.start()
    norm_grad_ref[...] = jnp.zeros_like(norm_grad_ref)
    line.greet((ring.left, ring.right))
    load_mine.wait()
    load_mlp.start()
    load_out.start()

    def normalize(index):
        def wait(pair, carry):
            line.arrive(pair)
            line.release(pair)
            return carry

        lax.fori_loop(index * per, index * per + per, wait, 0)
        load_tokens(index).wait()

        def normalize_rows(piece, carry):
            here = part(piece, 32)
            there = part(index * (block // 32) + piece, 32)
            values = token_buf[here, :].astype(f32) + total[there, :].astype(f32)
            values, unused_normed, unused_inverse = layer_norm(
                values, gain_ref[...], shift_ref[...], NORM_EPS
            )
            mine[there, :] = values.astype(low)
            return carry

        lax.fori_loop(0, block // 32, normalize_rows, 0)

        @pl.when(index < blocks - 1)
        def _():
            load_tokens(index + 1).start()

        @pl.when(index == blocks - 1)
        def _():
            store_sum.start()

    def units_step(index, start, count):
        @pl.when((index == 0) & (start == 0))
        def _():
            load_top.wait()

        here = part(index)

        def one(number, carry):
            first = part(number, 256)
            second = pl.ds(pl.multiple_of(units + number * 256, 256), 256)
            left = row_product(mine[here, :], mlp_w[:, first])
            right = row_product(mine[here, :], mlp_w[:, second])
            back = row_product(top_buf[here, :], out_w[:, first])
            cdf = 0.5 * (1.0 + lax.erf(left * (1.0 / math.sqrt(2.0))))
            pdf = jnp.exp(-0.5 * left * left) * (1.0 / math.sqrt(2.0 * math.pi))
            gelu = left * cdf
            hidden_buf[here, first] = (gelu * right).astype(low)
            pair_buf[here, first] = (back * right * (cdf + left * pdf)).astype(low)
            pair_buf[here, second] = (back * gelu).astype(low)
            return carry

        lax.fori_loop(start, start + count, one, 0)

    def backward_step(index):
        here = part(index)

        def one(number, carry):
            there = part(number, 256)
            mine[part(blocks + index), there] = turned_product(
                pair_buf[here, :], mlp_w[there, :]
            ).astype(low)
            return carry

        lax.fori_loop(0, width // 256, one, 0, unroll=True)

    def leave_step(index):
        @pl.when(index > 0)
        def _():
            store_leave(index - 1).wait()

        here = part(index)

        def one(number, carry):
            there = part(number, 256)
            leave_buf[:, there] = turned_product(hidden_buf[here, :], out_w[there, :]).astype(low)
            return carry

        lax.fori_loop(0, width // 256, one, 0, unroll=True)
        store_leave(index).start()

    def tile_stage(index):
        @pl.when(index > 0)
        def _():
            store_tile(index - 1).wait()

        here = part(index)
        flip_buf[...] = mine[pl.ds(0, capacity), here].T

        def one(number, carry):
            there = part(number, 512)
            tile_buf[:, there] = row_product(flip_buf[...], pair_buf[:, there]).astype(low)
            return carry

        lax.fori_loop(0, 2 * units // 512, one, 0, unroll=True)
        flip_buf[...] = top_buf[:, here].T

        def last(number, carry):
            there = pl.ds(pl.multiple_of(2 * units + number * 512, 512), 512)
            tile_buf[:, there] = row_product(
                flip_buf[...], hidden_buf[:, part(number, 512)]
            ).astype(low)
            return carry

        lax.fori_loop(0, units // 512, last, 0, unroll=True)
        store_tile(index).start()

    def norm_stage(index):
        line.arrive(half + index)
        load_piece(index).wait()

        @pl.when(index < half - 1)
        def _():
            load_piece(index + 1).start()

        @pl.when(index > 1)
        def _():
            for copy in store_middle(index - 2):
                copy.wait()

        slot, here = index % 2, part(index, span)
        values = piece_buf[slot].astype(f32) + total[here, :].astype(f32)
        back = total[part(half + index, span), :].astype(f32)
        result, gain_grad, shift_grad = norm_back_rows(values, back, gain_ref[...])
        middle = top_buf[here, :].astype(f32) + result
        wide_buf[slot] = middle
        low_buf[slot] = middle.astype(low)
        norm_grad_ref[0:1, :] += gain_grad
        norm_grad_ref[1:2, :] += shift_grad
        for copy in store_middle(index):
            copy.start()

    count = units // 256
    lead = per + 8
    batch = -(-ring.reach // (lead // 3))

    def step(index, carry):
        line.step(index, pairs)

        @pl.when(index == 0)
        def _():
            load_mlp.wait()
            load_out.wait()
            ring.step(0)
            load_tokens(0).start()
            load_top.start()
            load_piece(0).start()

        @pl.when((index > 0) & (index <= lead) & (index % 3 == 0))
        def _():
            for extra in range(batch):
                distance = (index // 3 - 1) * batch + extra + 1

                @pl.when(distance <= ring.reach)
                def _():
                    ring.step(distance)

        work = index - lead

        @pl.when((work >= 0) & (work < 4 * blocks))
        def _():
            piece, stage = work // 4, work % 4

            @pl.when(stage == 0)
            def _():
                normalize(piece)

            @pl.when((stage == 1) | (stage == 2))
            def _():
                units_step(piece, (stage - 1) * (count // 2), count // 2)

            @pl.when(stage == 3)
            def _():
                backward_step(piece)
                leave_step(piece)

        @pl.when((work >= 4 * blocks) & (work < 4 * blocks + tiles))
        def _():
            tile_stage(work - 4 * blocks)

        @pl.when(index >= half + 5)
        def _():
            norm_stage(index - half - 5)

        return carry

    lax.fori_loop(0, pairs + 5, step, 0)

    def drain(pair, carry):
        line.drain(pair)

        @pl.when(pair >= half)
        def _():
            line.release(pair)

        return carry

    lax.fori_loop(0, pairs, drain, 0)
    ring.drain()
    store_leave(blocks - 1).wait()
    store_tile(tiles - 1).wait()
    store_sum.wait()
    for index in (half - 2, half - 1):
        for copy in store_middle(index):
            copy.wait()


def middle_stage(
    branch, tokens, top, gain, shift, mlp_shard, out_shard, collective_id, rows=32, block=256
):
    capacity, width = branch.shape
    units = out_shard.shape[1]
    ways = width // out_shard.shape[0]
    low, f32 = jnp.bfloat16, jnp.float32
    anywhere, held = pl.BlockSpec(memory_space=pl.ANY), pl.BlockSpec(memory_space=pltpu.VMEM)
    pair_sems = pltpu.SemaphoreType.DMA((2,))
    return pl.pallas_call(
        functools.partial(middle_kernel, rows, block),
        out_shape=(
            jax.ShapeDtypeStruct((capacity, width), low),
            jax.ShapeDtypeStruct((capacity, width), low),
            jax.ShapeDtypeStruct((width, 3 * units), low),
            jax.ShapeDtypeStruct((capacity, width), f32),
            jax.ShapeDtypeStruct((capacity, width), low),
            jax.ShapeDtypeStruct((2, width), f32),
        ),
        in_specs=[anywhere, anywhere, anywhere, held, held, anywhere, anywhere],
        out_specs=(anywhere,) * 5 + (held,),
        scratch_shapes=[pltpu.VMEM((2 * capacity, width), low)]
        + line_scratch(2 * capacity, width, rows)
        + [
            pltpu.VMEM((width, 2 * units), low),
            pltpu.VMEM((width, units), low),
            pltpu.VMEM((capacity, width), low),
            pltpu.VMEM((capacity, units), low),
            pltpu.VMEM((capacity, 2 * units), low),
            pltpu.VMEM((block, width), low),
            pltpu.VMEM((block, width), low),
            pltpu.VMEM((block, 3 * units), low),
            pltpu.VMEM((block, capacity), low),
            pltpu.VMEM((2, 2 * rows, width), low),
            pltpu.VMEM((2, 2 * rows, width), f32),
            pltpu.VMEM((2, 2 * rows, width), low),
            pltpu.SemaphoreType.DMA((5,)),
            pair_sems,
            pltpu.SemaphoreType.DMA((3,)),
            pair_sems,
            pair_sems,
        ]
        + ring_scratch(ways, 2),
        compiler_params=pltpu.CompilerParams(
            collective_id=collective_id, has_side_effects=True, vmem_limit_bytes=62 << 20
        ),
        cost_estimate=pl.CostEstimate(
            flops=200_000_000_000, bytes_accessed=40 << 20, transcendentals=0
        ),
    )(branch, tokens, top, gain[None], shift[None], mlp_shard, out_shard)


def turn(values, cosine, sine):
    half = values.shape[1] // 2
    front, back = values[:, :half], values[:, half:]
    return jnp.concatenate([front * cosine - back * sine, front * sine + back * cosine], axis=1)


def decay_block(ends_ref, log_keep, row_start, col_start, size):
    rows = row_start + lax.broadcasted_iota(jnp.int32, (size, 1), 0)
    cols = col_start + lax.broadcasted_iota(jnp.int32, (1, size), 1)
    row_slot = jnp.zeros((size, 1), jnp.int32)
    col_slot = jnp.zeros((1, size), jnp.int32)
    for slot in range(SLOTS):
        row_slot += (rows >= ends_ref[slot]).astype(jnp.int32)
        col_slot += (cols >= ends_ref[slot]).astype(jnp.int32)
    row_slot = jnp.where(rows < ends_ref[SLOTS - 1], row_slot, -1)
    distance = rows - cols
    allowed = (row_slot == col_slot) & (distance >= 0)
    distance = jnp.maximum(distance, 0).astype(jnp.float32)
    return jnp.where(allowed, jnp.exp(distance * log_keep), 0.0)


def group_stats(values):
    center = values - jnp.mean(values, axis=-1, keepdims=True)
    inverse = lax.rsqrt(jnp.mean(center * center, axis=-1, keepdims=True) + GROUP_EPS)
    return center * inverse, inverse


def retain_kernel(
    ends_ref,
    keep_ref,
    first_ref,
    query_w_ref,
    key_w_ref,
    value_w_ref,
    gate_w_ref,
    cos_ref,
    sin_ref,
    gain_ref,
    out_shard_ref,
    query_ref,
    key_ref,
    value_ref,
    gate_ref,
    retained_ref,
    gated_ref,
    branch_ref,
    out_w_ref,
    keys,
    values,
    gated_buf,
    out_w,
    out_sem,
    ring_recv_sem,
    ring_send_sem,
):
    head, block = pl.program_id(0), pl.program_id(1)
    blocks = pl.num_programs(1)
    index, final = head * blocks + block, pl.num_programs(0) * blocks - 1
    size = query_ref.shape[0]
    shard = out_shard_ref.shape[0]
    ring = Ring(out_w.shape[0] // shard, (out_w,), ring_recv_sem, ring_send_sem)
    batch = -(-ring.reach // 4)
    store = pltpu.make_async_copy(out_w, out_w_ref, out_sem.at[1])

    @pl.when(index == 0)
    def _():
        place = pl.ds(pl.multiple_of(ring.me * shard, shard), shard)
        load = pltpu.make_async_copy(out_shard_ref, out_w.at[place], out_sem.at[0])
        load.start()
        ring.greet()
        load.wait()
        ring.step(0)

    def ring_round(number):
        for extra in range(batch):
            distance = number * batch + extra + 1

            @pl.when(distance <= ring.reach)
            def _():
                ring.step(distance)

    @pl.when((index >= 2) & (index < final) & (index % 2 == 0))
    def _():
        ring_round(index // 2 - 1)

    here = pl.ds(pl.multiple_of(block * size, size), size)
    first = first_ref[here, :]
    cosine, sine = cos_ref[here, :], sin_ref[here, :]
    query = turn(row_product(first, query_w_ref[...]), cosine, sine).astype(jnp.bfloat16)
    key = turn(row_product(first, key_w_ref[...]), cosine, sine) * KH ** (-0.5)
    key = key.astype(jnp.bfloat16)
    value = row_product(first, value_w_ref[...]).astype(jnp.bfloat16)
    gate = row_product(first, gate_w_ref[...])
    query_ref[...] = query
    key_ref[...] = key
    value_ref[...] = value
    gate_ref[...] = gate
    keys[here, :] = key
    values[here, :] = value
    retained_ref[...] = jnp.zeros_like(retained_ref)

    def visit(other, carry):
        there = pl.ds(pl.multiple_of(other * size, size), size)
        decay = decay_block(ends_ref, keep_ref[head], block * size, other * size, size)
        weights = (turned_product(query, keys[there, :]) * decay).astype(jnp.bfloat16)
        retained_ref[...] += row_product(weights, values[there, :])
        return carry

    lax.fori_loop(0, block + 1, visit, 0)
    normed, inverse = group_stats(retained_ref[...])
    gated = (gate * jax.nn.sigmoid(gate) * (normed * gain_ref[0])).astype(jnp.bfloat16)
    gated_ref[...] = gated
    gated_buf[here, pl.ds(pl.multiple_of(head * VH, VH), VH)] = gated

    @pl.when(index == final)
    def _():
        ring_round(3)
        store.start()

        def one(number, carry):
            there = pl.ds(pl.multiple_of(number * 256, 256), 256)
            branch_ref[:, there] = turned_product(gated_buf[...], out_w[there, :]).astype(
                jnp.bfloat16
            )
            return carry

        lax.fori_loop(0, out_w.shape[0] // 256, one, 0, unroll=True)
        ring.drain()
        store.wait()


def retain(
    ends, log_keep, first_low, full, cosine, sine, group_values, out_shard, collective_id, size=256
):
    capacity, width = first_low.shape
    heads = group_values.shape[0]
    scalar = pl.BlockSpec(memory_space=pltpu.SMEM)
    table = pl.BlockSpec((capacity, KH // 2), lambda h, r: (0, 0))
    key_block = pl.BlockSpec((size, KH), lambda h, r: (r, h))
    value_block = pl.BlockSpec((size, VH), lambda h, r: (r, h))
    ratio = KH * heads * 2 // VH

    def shape(columns, kind):
        return jax.ShapeDtypeStruct((capacity, heads * columns), kind)

    return pl.pallas_call(
        retain_kernel,
        grid=(heads, capacity // size),
        out_shape=(
            shape(KH, jnp.bfloat16),
            shape(KH, jnp.bfloat16),
            shape(VH, jnp.bfloat16),
            shape(VH, jnp.float32),
            shape(VH, jnp.float32),
            shape(VH, jnp.bfloat16),
            jax.ShapeDtypeStruct((capacity, width), jnp.bfloat16),
            jax.ShapeDtypeStruct((width, heads * VH), jnp.bfloat16),
        ),
        in_specs=[
            scalar,
            scalar,
            pl.BlockSpec((capacity, width), lambda h, r: (0, 0)),
            pl.BlockSpec((width, KH), lambda h, r: (0, h)),
            pl.BlockSpec((width, KH), lambda h, r: (0, heads + h)),
            pl.BlockSpec((width, VH), lambda h, r: (0, ratio + h)),
            pl.BlockSpec((width, VH), lambda h, r: (0, ratio + heads + h)),
            table,
            table,
            pl.BlockSpec((1, 1, VH), lambda h, r: (h, 0, 0)),
            pl.BlockSpec(memory_space=pl.ANY),
        ],
        out_specs=(key_block, key_block, value_block, value_block, value_block, value_block)
        + (
            pl.BlockSpec((capacity, width), lambda h, r: (0, 0)),
            pl.BlockSpec(memory_space=pl.ANY),
        ),
        scratch_shapes=[
            pltpu.VMEM((capacity, KH), jnp.bfloat16),
            pltpu.VMEM((capacity, VH), jnp.bfloat16),
            pltpu.VMEM((capacity, heads * VH), jnp.bfloat16),
            pltpu.VMEM((width, heads * VH), jnp.bfloat16),
            pltpu.SemaphoreType.DMA((2,)),
        ]
        + ring_scratch(width // out_shard.shape[0], 1),
        compiler_params=pltpu.CompilerParams(
            collective_id=collective_id, has_side_effects=True, vmem_limit_bytes=56 << 20
        ),
        cost_estimate=pl.CostEstimate(
            flops=16_000_000_000, bytes_accessed=40 << 20, transcendentals=0
        ),
    )(
        ends,
        log_keep,
        first_low,
        full,
        full,
        full,
        full,
        cosine,
        sine,
        group_values[:, None, :],
        out_shard,
    )


def back_kernel(
    rows,
    block,
    heads,
    ends_ref,
    keep_ref,
    leave_ref,
    middle_low_ref,
    out_w_ref,
    retained_ref,
    gate_ref,
    group_gain_ref,
    query_ref,
    key_ref,
    value_ref,
    cos_ref,
    sin_ref,
    gated_ref,
    first_ref,
    full_ref,
    total,
    weight_grad_ref,
    input_grad_ref,
    group_grad_ref,
    mine,
    near,
    far,
    near_sem,
    far_sem,
    done_sem,
    out_sem,
    cross_sem,
    give_sem,
    out_w,
    query_buf,
    key_buf,
    value_buf,
    gated_buf,
    first_buf,
    middle_low,
    flip_buf,
    grad_buf,
    stream_buf,
    tile_buf,
    input_grad_buf,
    retained_buf,
    gate_buf,
    grad_gated_buf,
    upstream_buf,
    query_grad,
    key_grad,
    value_grad,
    load_sem,
    stream_sem,
    group_sem,
    store_sem,
):
    capacity, width = leave_ref.shape
    blocks, tiles = capacity // block, width // block
    pairs = capacity // (2 * rows)
    finish = heads * blocks
    pace = max(1, pairs // (finish + tiles))
    low, f32 = jnp.bfloat16, jnp.float32
    line = Line(rows, mine, near, far, total, near_sem, far_sem, done_sem, out_sem, cross_sem, give_sem)

    def part(index, size=block):
        return pl.ds(pl.multiple_of(index * size, size), size)

    held = [
        pltpu.make_async_copy(source, target, load_sem.at[index])
        for index, (source, target) in enumerate(
            (
                (leave_ref, mine),
                (middle_low_ref, middle_low),
                (out_w_ref, out_w),
                (query_ref, query_buf),
                (key_ref, key_buf),
                (value_ref, value_buf),
                (gated_ref, gated_buf),
                (first_ref, first_buf),
            )
        )
    ]

    def load_group(index):
        slot = index % 2
        here, there = part(index % blocks), part(index // blocks, VH)
        return [
            pltpu.make_async_copy(
                retained_ref.at[here, there], retained_buf.at[slot], group_sem.at[2 * slot]
            ),
            pltpu.make_async_copy(
                gate_ref.at[here, there], gate_buf.at[slot], group_sem.at[2 * slot + 1]
            ),
        ]

    def load_tile(index):
        slot = index % 2
        return pltpu.make_async_copy(
            full_ref.at[part(index)], stream_buf.at[slot], stream_sem.at[slot]
        )

    def store_tile(index):
        return pltpu.make_async_copy(tile_buf, weight_grad_ref.at[part(index)], store_sem.at[0])

    def store_input(index):
        return pltpu.make_async_copy(
            input_grad_buf, input_grad_ref.at[:, part(index)], store_sem.at[1]
        )

    held[0].start()
    group_grad_ref[...] = jnp.zeros_like(group_grad_ref)
    line.greet()
    held[0].wait()
    for copy in held[1:-2] + load_group(0):
        copy.start()

    def attend_stage(index):
        head, place = index // blocks, index % blocks

        @pl.when(index == 0)
        def _():
            for copy in held[1:-2]:
                copy.wait()
            for copy in held[-2:]:
                copy.start()
            load_tile(0).start()

        for copy in load_group(index):
            copy.wait()

        @pl.when(index < heads * blocks - 1)
        def _():
            for copy in load_group(index + 1):
                copy.start()

        @pl.when(place == 0)
        def _():
            key_grad[...] = jnp.zeros_like(key_grad)
            value_grad[...] = jnp.zeros_like(value_grad)

        slot = index % 2
        here = part(place)
        keys_here, values_here = part(head, KH), part(head, VH)
        gain = group_gain_ref[pl.ds(head, 1), :]
        gate_place = pl.ds(pl.multiple_of(heads * (2 * KH + VH) + head * VH, VH), VH)
        grad_gated_buf[...] = row_product(middle_low[here, :], out_w[:, values_here])

        def gate_rows(piece, carry):
            few = pl.ds(pl.multiple_of(piece * 32, 32), 32)
            there = pl.ds(pl.multiple_of(place * block + piece * 32, 32), 32)
            normed, inverse = group_stats(retained_buf[slot, few, :])
            gate, grad_gated = gate_buf[slot, few, :], grad_gated_buf[few, :]
            sigmoid = jax.nn.sigmoid(gate)
            slope = sigmoid * (1.0 + gate * (1.0 - sigmoid))
            grad_buf[there, gate_place] = (grad_gated * (normed * gain) * slope).astype(low)
            grad_out = grad_gated * (gate * sigmoid)
            group_grad_ref[pl.ds(head, 1), :] += jnp.sum(grad_out * normed, axis=0, keepdims=True)
            scaled = grad_out * gain
            plain_mean = jnp.mean(scaled, axis=-1, keepdims=True)
            cross_mean = jnp.mean(scaled * normed, axis=-1, keepdims=True)
            upstream_buf[few, :] = (
                inverse * (scaled - plain_mean - normed * cross_mean)
            ).astype(low)
            return carry

        lax.fori_loop(0, block // 32, gate_rows, 0, unroll=4)
        upstream = upstream_buf[...]
        query = query_buf[here, keys_here]
        query_grad[...] = jnp.zeros_like(query_grad)

        def visit(other, carry):
            there = part(other)
            decay = decay_block(ends_ref, keep_ref[head], place * block, other * block, block)
            key = key_buf[there, keys_here]
            weights = (turned_product(query, key) * decay).astype(low)
            value_grad[there, :] += outer_product(weights, upstream)
            scores = turned_product(upstream, value_buf[there, values_here]) * decay
            scores = scores.astype(low)
            query_grad[...] += row_product(scores, key)
            key_grad[there, :] += outer_product(scores, query)
            return carry

        lax.fori_loop(0, place + 1, visit, 0)
        cosine, sine = cos_ref[here, :], sin_ref[here, :]
        grad_buf[here, keys_here] = turn(query_grad[...], cosine, -sine).astype(low)

        @pl.when(place == blocks - 1)
        def _():
            def one(other, carry):
                there = part(other)
                turned = turn(key_grad[there, :] * KH ** (-0.5), cos_ref[there, :], -sin_ref[there, :])
                grad_buf[there, part(heads + head, KH)] = turned.astype(low)
                value_place = pl.ds(pl.multiple_of(heads * 2 * KH + head * VH, VH), VH)
                grad_buf[there, value_place] = value_grad[there, :].astype(low)
                return carry

            lax.fori_loop(0, blocks, one, 0)

    def tile_stage(index):
        columns = grad_buf.shape[1]

        @pl.when(index == 0)
        def _():
            for copy in held[-2:]:
                copy.wait()

        @pl.when(index < tiles - 1)
        def _():
            load_tile(index + 1).start()

        @pl.when(index > 0)
        def _():
            store_tile(index - 1).wait()
            store_input(index - 1).wait()

        load_tile(index).wait()
        here = part(index)
        flip_buf[...] = first_buf[:, here].T

        def one(number, carry):
            there = part(number, 512)
            tile_buf[:, there] = row_product(flip_buf[...], grad_buf[:, there]).astype(low)
            return carry

        lax.fori_loop(0, columns // 512, one, 0, unroll=True)

        flip_buf[...] = middle_low[:, here].T

        def last(number, carry):
            there = pl.ds(pl.multiple_of(columns + number * 512, 512), 512)
            tile_buf[:, there] = row_product(
                flip_buf[...], gated_buf[:, part(number, 512)]
            ).astype(low)
            return carry

        lax.fori_loop(0, gated_buf.shape[1] // 512, last, 0, unroll=True)
        store_tile(index).start()

        def inward(number, carry):
            there = part(number)
            input_grad_buf[there, :] = turned_product(
                grad_buf[there, :], stream_buf[index % 2]
            ).astype(low)
            return carry

        lax.fori_loop(0, blocks, inward, 0, unroll=True)
        store_input(index).start()

    def step(index, carry):
        line.step(index, pairs)

        work = index // pace

        @pl.when((index % pace == 0) & (work < finish))
        def _():
            attend_stage(work)

        @pl.when((index % pace == 0) & (work >= finish) & (work < finish + tiles))
        def _():
            tile_stage(work - finish)

        return carry

    lax.fori_loop(0, max(pairs + 3, (finish + tiles) * pace), step, 0)

    def drain(pair, carry):
        line.arrive(pair)
        line.release(pair)
        line.drain(pair)
        return carry

    lax.fori_loop(0, pairs, drain, 0)
    store_tile(tiles - 1).wait()
    store_input(tiles - 1).wait()


def back_stage(
    ends,
    log_keep,
    leave,
    middle_low,
    mix_out,
    retained,
    gate,
    group_values,
    query,
    key,
    value,
    cosine,
    sine,
    gated,
    first_low,
    full,
    collective_id,
    rows=32,
    block=256,
):
    capacity, width = leave.shape
    heads = group_values.shape[0]
    columns, units = full.shape[1], gated.shape[1]
    low, f32 = jnp.bfloat16, jnp.float32
    anywhere, kept = pl.BlockSpec(memory_space=pl.ANY), pl.BlockSpec(memory_space=pltpu.VMEM)
    scalar = pl.BlockSpec(memory_space=pltpu.SMEM)
    return pl.pallas_call(
        functools.partial(back_kernel, rows, block, heads),
        out_shape=(
            jax.ShapeDtypeStruct((capacity, width), low),
            jax.ShapeDtypeStruct((width, columns + units), low),
            jax.ShapeDtypeStruct((capacity, width), low),
            jax.ShapeDtypeStruct((heads, VH), f32),
        ),
        in_specs=[scalar] * 2
        + [anywhere] * 5
        + [kept]
        + [anywhere] * 3
        + [kept] * 2
        + [anywhere] * 3,
        out_specs=(kept, anywhere, anywhere, kept),
        scratch_shapes=line_scratch(capacity, width, rows)
        + [
            pltpu.VMEM((width, units), low),
            pltpu.VMEM(query.shape, low),
            pltpu.VMEM(key.shape, low),
            pltpu.VMEM(value.shape, low),
            pltpu.VMEM(gated.shape, low),
            pltpu.VMEM((capacity, width), low),
            pltpu.VMEM((capacity, width), low),
            pltpu.VMEM((block, capacity), low),
            pltpu.VMEM((capacity, columns), low),
            pltpu.VMEM((2, block, columns), low),
            pltpu.VMEM((block, columns + units), low),
            pltpu.VMEM((capacity, block), low),
            pltpu.VMEM((2, block, VH), f32),
            pltpu.VMEM((2, block, VH), f32),
            pltpu.VMEM((block, VH), f32),
            pltpu.VMEM((block, VH), low),
            pltpu.VMEM((block, KH), f32),
            pltpu.VMEM((capacity, KH), f32),
            pltpu.VMEM((capacity, VH), f32),
            pltpu.SemaphoreType.DMA((8,)),
            pltpu.SemaphoreType.DMA((2,)),
            pltpu.SemaphoreType.DMA((4,)),
            pltpu.SemaphoreType.DMA((2,)),
        ],
        compiler_params=pltpu.CompilerParams(
            collective_id=collective_id, has_side_effects=True, vmem_limit_bytes=62 << 20
        ),
        cost_estimate=pl.CostEstimate(
            flops=100_000_000_000, bytes_accessed=40 << 20, transcendentals=0
        ),
    )(
        ends,
        log_keep,
        leave,
        middle_low,
        mix_out,
        retained,
        gate,
        group_values,
        query,
        key,
        value,
        cosine,
        sine,
        gated,
        first_low,
        full,
    )


def last_kernel(
    rows,
    ways,
    back_ref,
    tokens_ref,
    middle_ref,
    sum_ref,
    leave_ref,
    norm_gain_ref,
    norm_grad_ref,
    group_grad_ref,
    token_grad_ref,
    layer_ref,
    small_ref,
    total,
    mine,
    near,
    far,
    near_sem,
    far_sem,
    done_sem,
    out_sem,
    cross_sem,
    give_sem,
    token_buf,
    middle_buf,
    sum_buf,
    leave_buf,
    layer_buf,
    small_buf,
    small_in,
    load_sem,
    store_sem,
    layer_sem,
    small_send_sem,
    small_recv_sem,
):
    capacity, width = back_ref.shape
    pairs = capacity // (2 * rows)
    heads, group = group_grad_ref.shape
    f32 = jnp.float32
    sems = (near_sem, far_sem, done_sem, out_sem, cross_sem, give_sem)
    line = Line(rows, mine, near, far, total, *sems, lags=(1, 2))
    me = lax.axis_index("dp")
    peers = [lax.rem(me + distance, ways) for distance in range(1, ways)]
    loads = [
        pltpu.make_async_copy(source, target, load_sem.at[index])
        for index, (source, target) in enumerate(
            (
                (back_ref, mine),
                (tokens_ref, token_buf),
                (middle_ref, middle_buf),
                (sum_ref, sum_buf),
                (leave_ref, leave_buf),
            )
        )
    ]

    def part(pair):
        return pl.ds(pl.multiple_of(pair * 2 * rows, 2 * rows), 2 * rows)

    def store(pair):
        return pltpu.make_async_copy(
            middle_buf.at[part(pair)], token_grad_ref.at[part(pair)], store_sem.at[pair]
        )

    def store_layer(pair):
        slot = pair % 2
        return pltpu.make_async_copy(
            layer_buf.at[slot], layer_ref.at[part(pair)], layer_sem.at[slot]
        )

    def share(distance):
        return pltpu.make_async_remote_copy(
            small_buf,
            small_in.at[distance],
            small_send_sem.at[distance],
            small_recv_sem.at[distance],
            device_id={"dp": peers[distance]},
            device_id_type=MESH,
        )

    loads[0].start()
    small_buf[...] = jnp.zeros_like(small_buf)
    small_buf[2:4, :] = norm_grad_ref[...]
    for head in range(heads):
        small_buf[4:5, head * group : (head + 1) * group] = group_grad_ref[head : head + 1, :]
    line.greet(peers)
    loads[0].wait()

    def norm_stage(pair):
        line.arrive(pair)

        @pl.when(pair == 0)
        def _():
            for copy in loads[1:]:
                copy.wait()

        @pl.when(pair > 1)
        def _():
            store_layer(pair - 2).wait()

        here = part(pair)
        values = token_buf[here, :].astype(f32)
        layer_buf[pair % 2] = (
            values + sum_buf[here, :].astype(f32) + leave_buf[here, :].astype(f32)
        )
        result, gain_grad, shift_grad = norm_back_rows(
            values, total[here, :].astype(f32), norm_gain_ref[...]
        )
        middle_buf[here, :] += result
        small_buf[0:1, :] += gain_grad
        small_buf[1:2, :] += shift_grad
        store(pair).start()
        store_layer(pair).start()

    def step(index, carry):
        line.step(index, pairs)

        @pl.when(index == 0)
        def _():
            for copy in loads[1:]:
                copy.start()

        @pl.when(index >= 5)
        def _():
            norm_stage(index - 5)

        return carry

    lax.fori_loop(0, pairs + 5, step, 0)
    for distance in range(ways - 1):
        share(distance).start()

    def drain(pair, carry):
        line.release(pair)
        line.drain(pair)
        store(pair).wait()
        return carry

    lax.fori_loop(0, pairs, drain, 0)
    store_layer(pairs - 2).wait()
    store_layer(pairs - 1).wait()
    for distance in range(ways - 1):
        share(distance).wait()
    small_ref[...] = small_buf[...]
    for distance in range(ways - 1):
        small_ref[...] += small_in[distance]


def last_stage(
    back,
    tokens,
    middle,
    branch_sum,
    leave_sum,
    norm_gain,
    norm_grad,
    group_grad,
    ways,
    collective_id,
    rows=32,
):
    capacity, width = back.shape
    low, f32 = jnp.bfloat16, jnp.float32
    anywhere, kept = pl.BlockSpec(memory_space=pl.ANY), pl.BlockSpec(memory_space=pltpu.VMEM)
    small = (8, width)
    return pl.pallas_call(
        functools.partial(last_kernel, rows, ways),
        out_shape=(
            jax.ShapeDtypeStruct((capacity, width), f32),
            jax.ShapeDtypeStruct((capacity, width), f32),
            jax.ShapeDtypeStruct(small, f32),
        ),
        in_specs=[anywhere] * 5 + [kept] * 3,
        out_specs=(anywhere, anywhere, kept),
        scratch_shapes=[pltpu.VMEM((capacity, width), low)]
        + line_scratch(capacity, width, rows)
        + [
            pltpu.VMEM((capacity, width), low),
            pltpu.VMEM((capacity, width), f32),
            pltpu.VMEM((capacity, width), low),
            pltpu.VMEM((capacity, width), low),
            pltpu.VMEM((2, 2 * rows, width), f32),
            pltpu.VMEM(small, f32),
            pltpu.VMEM((ways - 1, *small), f32),
            pltpu.SemaphoreType.DMA((5,)),
            pltpu.SemaphoreType.DMA((capacity // (2 * rows),)),
            pltpu.SemaphoreType.DMA((2,)),
            pltpu.SemaphoreType.DMA((ways - 1,)),
            pltpu.SemaphoreType.DMA((ways - 1,)),
        ],
        compiler_params=pltpu.CompilerParams(
            collective_id=collective_id, has_side_effects=True, vmem_limit_bytes=52 << 20
        ),
        cost_estimate=pl.CostEstimate(
            flops=100_000_000_000, bytes_accessed=40 << 20, transcendentals=0
        ),
    )(back, tokens, middle, branch_sum, leave_sum, norm_gain[None], norm_grad, group_grad)


def local(
    tokens,
    lengths,
    cotangent,
    qk_weight,
    qk_first,
    qk_second,
    inner_weight,
    inner_first,
    inner_second,
    outer_weight,
    outer_first,
    outer_second,
    norm_params,
    norm_first,
    norm_second,
    group_gain,
    group_first,
    group_second,
):
    capacity = tokens.shape[0]
    local_heads = group_gain.shape[0]
    low = jnp.bfloat16
    tensor_index, data_index = lax.axis_index("tensor"), lax.axis_index("dp")

    def joined(shards):
        return jnp.concatenate([part.astype(low) for part in shards], axis=1)

    def gather(shards):
        return lax.all_gather(joined(shards), "dp", axis=0, tiled=True)

    def scatter(grad):
        return lax.psum_scatter(grad, "dp", scatter_dimension=0, tiled=True)

    norm_cols, group_cols = norm_params.shape[1], group_gain.shape[1]
    small = lax.all_gather(
        jnp.concatenate([norm_params.reshape(-1), group_gain.reshape(-1)]).astype(low), "dp"
    ).astype(jnp.float32)
    ways = small.shape[0]
    norm_values = small[:, : 4 * norm_cols].reshape(ways, 4, norm_cols)
    norm_values = norm_values.transpose(1, 0, 2).reshape(4, -1)
    group_values = small[:, 4 * norm_cols :].reshape(ways, local_heads, group_cols)
    group_values = group_values.transpose(1, 0, 2).reshape(local_heads, -1)
    first_full = gather([qk_weight[0], qk_weight[1], inner_weight[0], inner_weight[1]])
    mix_shard = outer_weight[0].astype(low)
    mlp_shard = joined([inner_weight[2], inner_weight[3]])
    out_shard = outer_weight[1].astype(low)
    row_index, sequence_id, position, live_rows = sequence_layout(lengths[0], capacity)
    cosine, sine = rotation_tables(position, KH)
    ends = jnp.cumsum(lengths[0])
    head_ids = tensor_index * local_heads + jnp.arange(local_heads, dtype=jnp.int32)
    log_keep = jnp.log1p(-jnp.exp2(-(5.0 + head_ids.astype(jnp.float32))))
    inputs = tokens.astype(jnp.float32)
    first_out, unused_normed, unused_inverse = layer_norm(
        inputs, norm_values[0], norm_values[1], NORM_EPS
    )
    first_low = first_out.astype(low)
    query, key, value, gate, retained, gated, branch, mix_out = retain(
        ends, log_keep, first_low, first_full, cosine, sine, group_values, mix_shard, 3
    )
    grad_top = cotangent.astype(jnp.float32) * live_rows.astype(jnp.float32)[:, None]
    top_low = grad_top.astype(low)
    branch_sum, leave, mlp_grad, grad_middle, middle_low, norm_two = middle_stage(
        branch, tokens, top_low, norm_values[2], norm_values[3], mlp_shard, out_shard, 0
    )
    mlp_part = scatter(mlp_grad)
    leave_sum, first_grad, back_first, grad_group_gain = back_stage(
        ends,
        log_keep,
        leave,
        middle_low,
        mix_out,
        retained,
        gate,
        group_values,
        query,
        key,
        value,
        cosine,
        sine,
        gated,
        first_low,
        first_full,
        1,
    )
    first_part = scatter(first_grad)
    back_first, mlp_part = lax.optimization_barrier((back_first, mlp_part))
    token_grad, layer_out, small_grad = last_stage(
        back_first,
        tokens,
        grad_middle,
        branch_sum,
        leave_sum,
        norm_values[0],
        norm_two,
        grad_group_gain,
        ways,
        2,
    )
    norm_grad = lax.dynamic_slice(small_grad, (0, data_index * norm_cols), (4, norm_cols))
    group_grad = lax.dynamic_slice(
        small_grad[4, : local_heads * VH].reshape(local_heads, VH),
        (0, data_index * group_cols),
        (local_heads, group_cols),
    )
    qk_cols, mix_cols = local_heads * KH, local_heads * VH
    starts = [qk_cols, 2 * qk_cols, 2 * qk_cols + mix_cols, 2 * qk_cols + 2 * mix_cols]
    query_grad, key_grad, value_grad, gate_grad, mix_out_part = jnp.split(
        first_part, starts, axis=1
    )
    qk_grad = jnp.stack([query_grad, key_grad]).astype(jnp.float32)
    units = out_shard.shape[1]
    left_grad, right_grad, mlp_out_part = jnp.split(mlp_part, [units, 2 * units], axis=1)
    inner_grad = jnp.stack([value_grad, gate_grad, left_grad, right_grad]).astype(jnp.float32)
    outer_grad = jnp.stack([mix_out_part, mlp_out_part]).astype(jnp.float32)
    qk_new = adam_update(qk_weight, qk_grad, qk_first, qk_second, MATRIX_RATE, WEIGHT_DECAY)
    inner_new = adam_update(
        inner_weight, inner_grad, inner_first, inner_second, MATRIX_RATE, WEIGHT_DECAY
    )
    outer_new = adam_update(
        outer_weight, outer_grad, outer_first, outer_second, MATRIX_RATE, WEIGHT_DECAY
    )
    norm_new = adam_update(norm_params, norm_grad, norm_first, norm_second, VECTOR_RATE, 0.0)
    group_new = adam_update(group_gain, group_grad, group_first, group_second, VECTOR_RATE, 0.0)
    return (layer_out, token_grad, *qk_new, *inner_new, *outer_new, *norm_new, *group_new)


def solution(mesh):
    in_specs = (
        P("dp", None),
        P("dp", None),
        P("dp", None),
        P(None, "dp", "tensor"),
        P(None, "dp", "tensor"),
        P(None, "dp", "tensor"),
        P(None, "dp", "tensor"),
        P(None, "dp", "tensor"),
        P(None, "dp", "tensor"),
        P(None, "dp", "tensor"),
        P(None, "dp", "tensor"),
        P(None, "dp", "tensor"),
        P(None, "dp"),
        P(None, "dp"),
        P(None, "dp"),
        P("tensor", "dp"),
        P("tensor", "dp"),
        P("tensor", "dp"),
    )
    out_specs = (
        P("dp", None),
        P("dp", None),
        P(None, "dp", "tensor"),
        P(None, "dp", "tensor"),
        P(None, "dp", "tensor"),
        P(None, "dp", "tensor"),
        P(None, "dp", "tensor"),
        P(None, "dp", "tensor"),
        P(None, "dp", "tensor"),
        P(None, "dp", "tensor"),
        P(None, "dp", "tensor"),
        P(None, "dp"),
        P(None, "dp"),
        P(None, "dp"),
        P("tensor", "dp"),
        P("tensor", "dp"),
        P("tensor", "dp"),
    )
    return jax.shard_map(local, mesh=mesh, in_specs=in_specs, out_specs=out_specs, check_vma=False)
```

```python
import functools
import math

import jax
import jax.numpy as jnp
from jax import lax
from jax.experimental import pallas as pl
from jax.experimental.pallas import tpu as pltpu
from jax.sharding import PartitionSpec as P

MESH = pl.DeviceIdType.MESH

KH = 256
VH = 512
SLOTS = 4
STEP = 10


NORM_EPS = 1e-05
GROUP_EPS = 1.0
BETA_FIRST = 0.9
BETA_SECOND = 0.95
ADAM_EPS = 1e-08
MATRIX_RATE = 0.05
VECTOR_RATE = 0.5
WEIGHT_DECAY = 0.1


def layer_norm(values, gain_row, shift_row, epsilon):
    center = values - jnp.mean(values, axis=-1, keepdims=True)
    inverse = lax.rsqrt(jnp.mean(center * center, axis=-1, keepdims=True) + epsilon)
    normed = center * inverse
    return (normed * gain_row + shift_row, normed, inverse)


def norm_back(upstream, normed, inverse, gain_row):
    scaled = upstream * gain_row
    plain_mean = jnp.mean(scaled, axis=-1, keepdims=True)
    cross_mean = jnp.mean(scaled * normed, axis=-1, keepdims=True)
    result = inverse * (scaled - plain_mean - normed * cross_mean)
    return (result, jnp.sum(upstream * normed, axis=0), jnp.sum(upstream, axis=0))


def sequence_layout(lengths_row, capacity):
    seq_ends = jnp.cumsum(lengths_row)
    row_index = jnp.arange(capacity, dtype=jnp.int32)
    sequence_id = jnp.sum((row_index[:, None] >= seq_ends[None, :]).astype(jnp.int32), axis=1)
    starts = seq_ends - lengths_row
    slot_index = jnp.arange(lengths_row.shape[0], dtype=jnp.int32)
    row_start = jnp.sum(
        jnp.where(sequence_id[:, None] == slot_index[None, :], starts[None, :], 0), axis=1
    )
    position = row_index - row_start
    live_rows = row_index < seq_ends[-1]
    return (row_index, sequence_id, position, live_rows)


def decay_table(row_index, sequence_id, live_rows, head_ids):
    allowed = (
        (sequence_id[:, None] == sequence_id[None, :])
        & (row_index[:, None] >= row_index[None, :])
        & live_rows[:, None]
        & live_rows[None, :]
    )
    distance = jnp.maximum(row_index[:, None] - row_index[None, :], 0).astype(jnp.float32)
    log_keep = jnp.log1p(-jnp.exp2(-(5.0 + head_ids.astype(jnp.float32))))
    return jnp.where(allowed[None], jnp.exp(distance[None] * log_keep[:, None, None]), 0.0)


def rotation_tables(position, head_size):
    half_size = head_size // 2
    frequency = jnp.exp(
        -math.log(10000.0) * 2.0 * jnp.arange(half_size, dtype=jnp.float32) / head_size
    )
    angles = position.astype(jnp.float32)[:, None] * frequency[None, :]
    return (jnp.cos(angles), jnp.sin(angles))


def rotate(values, cosine, sine, head_size):
    row_count = values.shape[0]
    shaped = values.reshape(row_count, -1, 2, head_size // 2)
    front_half = shaped[:, :, 0]
    back_half = shaped[:, :, 1]
    cos_rows = cosine[:, None, :]
    sin_rows = sine[:, None, :]
    turned = jnp.stack(
        [
            front_half * cos_rows - back_half * sin_rows,
            front_half * sin_rows + back_half * cos_rows,
        ],
        axis=2,
    )
    return turned.reshape(row_count, -1)


def row_product(left, right):
    return jnp.dot(left, right, preferred_element_type=jnp.float32)


def turned_product(left, right):
    return lax.dot_general(
        left, right, (((1,), (1,)), ((), ())), preferred_element_type=jnp.float32
    )


def outer_product(left, right):
    return lax.dot_general(
        left, right, (((0,), (0,)), ((), ())), preferred_element_type=jnp.float32
    )


def adam_update(weight, gradient, moment, square, rate, decay_rate):
    moment_new = BETA_FIRST * moment + (1.0 - BETA_FIRST) * gradient
    square_new = BETA_SECOND * square + (1.0 - BETA_SECOND) * gradient * gradient
    first_hat = moment_new / (1.0 - BETA_FIRST**STEP)
    second_hat = square_new / (1.0 - BETA_SECOND**STEP)
    weight_new = weight - rate * (
        first_hat / (jnp.sqrt(second_hat) + ADAM_EPS) + decay_rate * weight
    )
    return (moment_new, square_new, weight_new)


class Ring:
    def __init__(self, count, results, recv_sem, send_sem):
        self.count, self.results, self.recv_sem, self.send_sem = count, results, recv_sem, send_sem
        me = lax.axis_index("dp")
        self.me, self.place = me, self.swap(me)
        self.right, self.left = self.owner(1), self.owner(-1)
        self.reach = count // 2

    def swap(self, index):
        if self.count != 8:
            return index
        return jnp.where(index < 4, index, jnp.where(index < 6, index + 2, index - 2))

    def owner(self, distance):
        return self.swap(lax.rem(self.place + distance + self.count, self.count))

    def greet(self):
        barrier = pltpu.get_barrier_semaphore()
        for device in (self.left, self.right):
            pl.semaphore_signal(barrier, inc=1, device_id={"dp": device}, device_id_type=MESH)
        pl.semaphore_wait(barrier, 2)

    def copies(self, owner, half, way):
        made = []
        for index, result in enumerate(self.results):
            rows = result.shape[0] // (2 * self.count)
            here = result.at[pl.ds(pl.multiple_of((owner * 2 + half) * rows, rows), rows)]
            made.append(
                pltpu.make_async_remote_copy(
                    here,
                    here,
                    self.send_sem.at[((way * 2 + half) * len(self.results) + index) * self.count + owner],
                    self.recv_sem.at[(half * len(self.results) + index) * self.count + owner],
                    device_id={"dp": self.left if way else self.right},
                    device_id_type=MESH,
                )
            )
        return made

    def streams(self):
        for half in range(2):
            for way in range(2):
                yield half, way, self.reach - (half + way) % 2

    def step(self, distance):
        for half, way, hops in self.streams():
            owner = self.owner(distance if way else -distance)

            @pl.when((distance >= 1) & (distance <= hops))
            def _():
                for copy in self.copies(owner, half, way):
                    copy.wait_recv()

            @pl.when(distance < hops)
            def _():
                for copy in self.copies(owner, half, way):
                    copy.start()

    def drain(self):
        for half, way, hops in self.streams():

            def one(distance, carry):
                for copy in self.copies(self.owner(distance if way else -distance), half, way):
                    copy.wait_send()
                return carry

            lax.fori_loop(0, hops, one, 0)


def ring_scratch(count, results):
    return [
        pltpu.SemaphoreType.DMA((2 * results * count,)),
        pltpu.SemaphoreType.DMA((4 * results * count,)),
    ]


class Line:
    def __init__(self, rows, mine, near, far, total, near_sem, far_sem, done_sem, out_sem, cross_sem, give_sem, lags=(1, 3)):
        self.lags = lags
        self.rows, self.mine, self.near, self.far, self.total = rows, mine, near, far, total
        self.near_sem, self.far_sem, self.done_sem = near_sem, far_sem, done_sem
        self.out_sem, self.cross_sem, self.give_sem = out_sem, cross_sem, give_sem
        me = lax.axis_index("tensor")
        self.me = me
        self.inner = (me == 1) | (me == 2)
        self.outer = (me == 0) | (me == 3)
        self.relay_to = jnp.where(self.inner, 3 - me, 1 + me // 3)
        self.away = jnp.where(self.inner, 3 * (me - 1), 1 + me // 3)
        owner = jnp.where(self.inner, me, 1 + me // 3)
        self.kept, self.passed = owner - 1, 2 - owner

    def at(self, chunk):
        return pl.ds(pl.multiple_of(chunk * self.rows, self.rows), self.rows)

    def greet(self, also=()):
        barrier = pltpu.get_barrier_semaphore()
        for device in also:
            pl.semaphore_signal(barrier, inc=1, device_id={"dp": device}, device_id_type=MESH)
        pl.semaphore_signal(barrier, inc=1, device_id={"tensor": self.away}, device_id_type=MESH)

        @pl.when(self.inner)
        def _():
            pl.semaphore_signal(
                barrier, inc=1, device_id={"tensor": self.relay_to}, device_id_type=MESH
            )
            pl.semaphore_wait(barrier, 2 + len(also))

        @pl.when(self.outer)
        def _():
            pl.semaphore_wait(barrier, 1 + len(also))

    def copy(self, source, target, send_sem, recv_sem, device):
        return pltpu.make_async_remote_copy(
            source, target, send_sem, recv_sem, device_id={"tensor": device}, device_id_type=MESH
        )

    def send_in(self, chunk):
        return self.copy(
            self.mine.at[self.at(chunk)],
            self.near.at[self.at(chunk)],
            self.out_sem.at[chunk],
            self.near_sem.at[chunk],
            self.away,
        )

    def send_across(self, pair, chunk):
        return self.copy(
            self.near.at[self.at(chunk)],
            self.far.at[self.at(pair)],
            self.out_sem.at[chunk],
            self.far_sem.at[pair],
            self.relay_to,
        )

    def give(self, chunk, send_sem, device):
        place = self.total.at[self.at(chunk)]
        return self.copy(place, place, send_sem, self.done_sem.at[chunk], device)

    def give_out(self, chunk):
        return self.give(chunk, self.give_sem.at[chunk], self.away)

    def give_across(self, pair, chunk):
        return self.give(chunk, self.cross_sem.at[pair], self.relay_to)

    def wide(self, ref, chunk):
        return ref[self.at(chunk), :].astype(jnp.float32)

    def relay(self, pair):
        passed, kept = 2 * pair + self.passed, 2 * pair + self.kept

        @pl.when(self.outer)
        def _():
            self.send_in(passed).start()
            self.send_in(kept).start()

        @pl.when(self.inner)
        def _():
            self.send_in(passed).wait_recv()
            added = self.wide(self.near, passed) + self.wide(self.mine, passed)
            self.near[self.at(passed), :] = added.astype(jnp.bfloat16)
            self.send_across(pair, passed).start()

    def own(self, pair):
        kept = 2 * pair + self.kept

        @pl.when(self.inner)
        def _():
            self.send_in(kept).wait_recv()
            self.send_across(pair, kept).wait_recv()
            added = self.wide(self.near, kept) + self.wide(self.mine, kept)
            added = added + self.wide(self.far, pair)
            self.total[self.at(kept), :] = added.astype(jnp.bfloat16)
            self.give_across(pair, kept).start()
            self.give_out(kept).start()

    def forward(self, pair):
        passed = 2 * pair + self.passed

        @pl.when(self.inner)
        def _():
            self.give_out(passed).wait_recv()
            self.give_out(passed).start()

    def step(self, index, pairs):
        own_lag, forward_lag = self.lags

        @pl.when(index < pairs)
        def _():
            self.relay(index)

        @pl.when((index >= own_lag) & (index < pairs + own_lag))
        def _():
            self.own(index - own_lag)

        @pl.when((index >= forward_lag) & (index < pairs + forward_lag))
        def _():
            self.forward(index - forward_lag)

    def arrive(self, pair):
        @pl.when(self.outer)
        def _():
            self.give_out(2 * pair).wait_recv()
            self.give_out(2 * pair + 1).wait_recv()

    def release(self, pair):
        @pl.when(self.outer)
        def _():
            self.send_in(2 * pair).wait_send()
            self.send_in(2 * pair + 1).wait_send()

    def drain(self, pair):
        passed, kept = 2 * pair + self.passed, 2 * pair + self.kept

        @pl.when(self.inner)
        def _():
            self.send_across(pair, passed).wait_send()
            self.give_across(pair, kept).wait_send()
            self.give_out(kept).wait_send()
            self.give_out(passed).wait_send()


def line_scratch(height, width, rows):
    chunks = height // rows
    wide = pltpu.VMEM((height, width), jnp.bfloat16)
    sems, half_sems = pltpu.SemaphoreType.DMA((chunks,)), pltpu.SemaphoreType.DMA((chunks // 2,))
    return [
        wide,
        wide,
        pltpu.VMEM((height // 2, width), jnp.bfloat16),
        sems,
        half_sems,
        sems,
        sems,
        half_sems,
        sems,
    ]


def norm_back_rows(values, back, gain_row):
    center = values - jnp.mean(values, axis=-1, keepdims=True)
    inverse = lax.rsqrt(jnp.mean(center * center, axis=-1, keepdims=True) + NORM_EPS)
    normed = center * inverse
    result, gain_grad, shift_grad = norm_back(back, normed, inverse, gain_row)
    return result, gain_grad[None], shift_grad[None]


def middle_kernel(
    rows,
    block,
    branch_ref,
    tokens_ref,
    top_ref,
    gain_ref,
    shift_ref,
    mlp_ref,
    out_w_ref,
    sum_ref,
    leave_ref,
    weight_grad_ref,
    middle_ref,
    middle_low_ref,
    norm_grad_ref,
    total,
    mine,
    near,
    far,
    near_sem,
    far_sem,
    done_sem,
    out_sem,
    cross_sem,
    give_sem,
    mlp_w,
    out_w,
    top_buf,
    hidden_buf,
    pair_buf,
    token_buf,
    leave_buf,
    tile_buf,
    flip_buf,
    piece_buf,
    wide_buf,
    low_buf,
    load_sem,
    piece_sem,
    store_sem,
    wide_sem,
    low_sem,
    ring_recv_sem,
    ring_send_sem,
):
    capacity, width = branch_ref.shape
    units = hidden_buf.shape[1]
    ways = width // mlp_ref.shape[0]
    ring = Ring(ways, (mlp_w, out_w), ring_recv_sem, ring_send_sem)
    blocks, tiles = capacity // block, width // block
    span = 2 * rows
    per, half = block // span, capacity // span
    pairs = 2 * half
    low, f32 = jnp.bfloat16, jnp.float32
    line = Line(rows, mine, near, far, total, near_sem, far_sem, done_sem, out_sem, cross_sem, give_sem)

    def part(index, size=block):
        return pl.ds(pl.multiple_of(index * size, size), size)

    def load_tokens(index):
        return pltpu.make_async_copy(tokens_ref.at[part(index)], token_buf, load_sem.at[3])

    def load_piece(index):
        slot = index % 2
        return pltpu.make_async_copy(
            tokens_ref.at[part(index, span)], piece_buf.at[slot], piece_sem.at[slot]
        )

    def store_leave(index):
        return pltpu.make_async_copy(leave_buf, leave_ref.at[part(index)], store_sem.at[0])

    def store_tile(index):
        return pltpu.make_async_copy(tile_buf, weight_grad_ref.at[part(index)], store_sem.at[1])

    store_sum = pltpu.make_async_copy(total.at[pl.ds(0, capacity)], sum_ref, store_sem.at[2])

    def store_middle(index):
        slot = index % 2
        return [
            pltpu.make_async_copy(
                wide_buf.at[slot], middle_ref.at[part(index, span)], wide_sem.at[slot]
            ),
            pltpu.make_async_copy(
                low_buf.at[slot], middle_low_ref.at[part(index, span)], low_sem.at[slot]
            ),
        ]

    shard = part(ring.me, mlp_ref.shape[0])
    load_mlp = pltpu.make_async_copy(mlp_ref, mlp_w.at[shard], load_sem.at[1])
    load_out = pltpu.make_async_copy(out_w_ref, out_w.at[shard], load_sem.at[2])
    load_mine = pltpu.make_async_copy(branch_ref, mine.at[pl.ds(0, capacity)], load_sem.at[0])
    load_top = pltpu.make_async_copy(top_ref, top_buf, load_sem.at[4])
    load_mine.start()
    norm_grad_ref[...] = jnp.zeros_like(norm_grad_ref)
    line.greet((ring.left, ring.right))
    load_mine.wait()
    load_mlp.start()
    load_out.start()

    def normalize(index):
        def wait(pair, carry):
            line.arrive(pair)
            line.release(pair)
            return carry

        lax.fori_loop(index * per, index * per + per, wait, 0)
        load_tokens(index).wait()

        def normalize_rows(piece, carry):
            here = part(piece, 32)
            there = part(index * (block // 32) + piece, 32)
            values = token_buf[here, :].astype(f32) + total[there, :].astype(f32)
            values, unused_normed, unused_inverse = layer_norm(
                values, gain_ref[...], shift_ref[...], NORM_EPS
            )
            mine[there, :] = values.astype(low)
            return carry

        lax.fori_loop(0, block // 32, normalize_rows, 0)

        @pl.when(index < blocks - 1)
        def _():
            load_tokens(index + 1).start()

        @pl.when(index == blocks - 1)
        def _():
            store_sum.start()

    def units_step(index, start, count):
        @pl.when((index == 0) & (start == 0))
        def _():
            load_top.wait()

        here = part(index)

        def one(number, carry):
            first = part(number, 256)
            second = pl.ds(pl.multiple_of(units + number * 256, 256), 256)
            left = row_product(mine[here, :], mlp_w[:, first])
            right = row_product(mine[here, :], mlp_w[:, second])
            back = row_product(top_buf[here, :], out_w[:, first])
            cdf = 0.5 * (1.0 + lax.erf(left * (1.0 / math.sqrt(2.0))))
            pdf = jnp.exp(-0.5 * left * left) * (1.0 / math.sqrt(2.0 * math.pi))
            gelu = left * cdf
            hidden_buf[here, first] = (gelu * right).astype(low)
            pair_buf[here, first] = (back * right * (cdf + left * pdf)).astype(low)
            pair_buf[here, second] = (back * gelu).astype(low)
            return carry

        lax.fori_loop(start, start + count, one, 0)

    def backward_step(index):
        here = part(index)

        def one(number, carry):
            there = part(number, 256)
            mine[part(blocks + index), there] = turned_product(
                pair_buf[here, :], mlp_w[there, :]
            ).astype(low)
            return carry

        lax.fori_loop(0, width // 256, one, 0, unroll=True)

    def leave_step(index):
        @pl.when(index > 0)
        def _():
            store_leave(index - 1).wait()

        here = part(index)

        def one(number, carry):
            there = part(number, 256)
            leave_buf[:, there] = turned_product(hidden_buf[here, :], out_w[there, :]).astype(low)
            return carry

        lax.fori_loop(0, width // 256, one, 0, unroll=True)
        store_leave(index).start()

    def tile_stage(index):
        @pl.when(index > 0)
        def _():
            store_tile(index - 1).wait()

        here = part(index)
        flip_buf[...] = mine[pl.ds(0, capacity), here].T

        def one(number, carry):
            there = part(number, 512)
            tile_buf[:, there] = row_product(flip_buf[...], pair_buf[:, there]).astype(low)
            return carry

        lax.fori_loop(0, 2 * units // 512, one, 0, unroll=True)
        flip_buf[...] = top_buf[:, here].T

        def last(number, carry):
            there = pl.ds(pl.multiple_of(2 * units + number * 512, 512), 512)
            tile_buf[:, there] = row_product(
                flip_buf[...], hidden_buf[:, part(number, 512)]
            ).astype(low)
            return carry

        lax.fori_loop(0, units // 512, last, 0, unroll=True)
        store_tile(index).start()

    def norm_stage(index):
        line.arrive(half + index)
        load_piece(index).wait()

        @pl.when(index < half - 1)
        def _():
            load_piece(index + 1).start()

        @pl.when(index > 1)
        def _():
            for copy in store_middle(index - 2):
                copy.wait()

        slot, here = index % 2, part(index, span)
        values = piece_buf[slot].astype(f32) + total[here, :].astype(f32)
        back = total[part(half + index, span), :].astype(f32)
        result, gain_grad, shift_grad = norm_back_rows(values, back, gain_ref[...])
        middle = top_buf[here, :].astype(f32) + result
        wide_buf[slot] = middle
        low_buf[slot] = middle.astype(low)
        norm_grad_ref[0:1, :] += gain_grad
        norm_grad_ref[1:2, :] += shift_grad
        for copy in store_middle(index):
            copy.start()

    count = units // 256
    lead = per + 8
    batch = -(-ring.reach // (lead // 3))

    def step(index, carry):
        line.step(index, pairs)

        @pl.when(index == 0)
        def _():
            load_mlp.wait()
            load_out.wait()
            ring.step(0)
            load_tokens(0).start()
            load_top.start()
            load_piece(0).start()

        @pl.when((index > 0) & (index <= lead) & (index % 3 == 0))
        def _():
            for extra in range(batch):
                distance = (index // 3 - 1) * batch + extra + 1

                @pl.when(distance <= ring.reach)
                def _():
                    ring.step(distance)

        work = index - lead

        @pl.when((work >= 0) & (work < 4 * blocks))
        def _():
            piece, stage = work // 4, work % 4

            @pl.when(stage == 0)
            def _():
                normalize(piece)

            @pl.when((stage == 1) | (stage == 2))
            def _():
                units_step(piece, (stage - 1) * (count // 2), count // 2)

            @pl.when(stage == 3)
            def _():
                backward_step(piece)
                leave_step(piece)

        @pl.when((work >= 4 * blocks) & (work < 4 * blocks + tiles))
        def _():
            tile_stage(work - 4 * blocks)

        @pl.when(index >= half + 5)
        def _():
            norm_stage(index - half - 5)

        return carry

    lax.fori_loop(0, pairs + 5, step, 0)

    def drain(pair, carry):
        line.drain(pair)

        @pl.when(pair >= half)
        def _():
            line.release(pair)

        return carry

    lax.fori_loop(0, pairs, drain, 0)
    ring.drain()
    store_leave(blocks - 1).wait()
    store_tile(tiles - 1).wait()
    store_sum.wait()
    for index in (half - 2, half - 1):
        for copy in store_middle(index):
            copy.wait()


def middle_stage(
    branch, tokens, top, gain, shift, mlp_shard, out_shard, collective_id, rows=32, block=256
):
    capacity, width = branch.shape
    units = out_shard.shape[1]
    ways = width // out_shard.shape[0]
    low, f32 = jnp.bfloat16, jnp.float32
    anywhere, held = pl.BlockSpec(memory_space=pl.ANY), pl.BlockSpec(memory_space=pltpu.VMEM)
    pair_sems = pltpu.SemaphoreType.DMA((2,))
    return pl.pallas_call(
        functools.partial(middle_kernel, rows, block),
        out_shape=(
            jax.ShapeDtypeStruct((capacity, width), low),
            jax.ShapeDtypeStruct((capacity, width), low),
            jax.ShapeDtypeStruct((width, 3 * units), low),
            jax.ShapeDtypeStruct((capacity, width), f32),
            jax.ShapeDtypeStruct((capacity, width), low),
            jax.ShapeDtypeStruct((2, width), f32),
        ),
        in_specs=[anywhere, anywhere, anywhere, held, held, anywhere, anywhere],
        out_specs=(anywhere,) * 5 + (held,),
        scratch_shapes=[pltpu.VMEM((2 * capacity, width), low)]
        + line_scratch(2 * capacity, width, rows)
        + [
            pltpu.VMEM((width, 2 * units), low),
            pltpu.VMEM((width, units), low),
            pltpu.VMEM((capacity, width), low),
            pltpu.VMEM((capacity, units), low),
            pltpu.VMEM((capacity, 2 * units), low),
            pltpu.VMEM((block, width), low),
            pltpu.VMEM((block, width), low),
            pltpu.VMEM((block, 3 * units), low),
            pltpu.VMEM((block, capacity), low),
            pltpu.VMEM((2, 2 * rows, width), low),
            pltpu.VMEM((2, 2 * rows, width), f32),
            pltpu.VMEM((2, 2 * rows, width), low),
            pltpu.SemaphoreType.DMA((5,)),
            pair_sems,
            pltpu.SemaphoreType.DMA((3,)),
            pair_sems,
            pair_sems,
        ]
        + ring_scratch(ways, 2),
        compiler_params=pltpu.CompilerParams(
            collective_id=collective_id, has_side_effects=True, vmem_limit_bytes=62 << 20
        ),
        cost_estimate=pl.CostEstimate(
            flops=200_000_000_000, bytes_accessed=40 << 20, transcendentals=0
        ),
    )(branch, tokens, top, gain[None], shift[None], mlp_shard, out_shard)


def turn(values, cosine, sine):
    half = values.shape[1] // 2
    front, back = values[:, :half], values[:, half:]
    return jnp.concatenate([front * cosine - back * sine, front * sine + back * cosine], axis=1)


def decay_block(ends_ref, log_keep, row_start, col_start, size):
    rows = row_start + lax.broadcasted_iota(jnp.int32, (size, 1), 0)
    cols = col_start + lax.broadcasted_iota(jnp.int32, (1, size), 1)
    row_slot = jnp.zeros((size, 1), jnp.int32)
    col_slot = jnp.zeros((1, size), jnp.int32)
    for slot in range(SLOTS):
        row_slot += (rows >= ends_ref[slot]).astype(jnp.int32)
        col_slot += (cols >= ends_ref[slot]).astype(jnp.int32)
    row_slot = jnp.where(rows < ends_ref[SLOTS - 1], row_slot, -1)
    distance = rows - cols
    allowed = (row_slot == col_slot) & (distance >= 0)
    distance = jnp.maximum(distance, 0).astype(jnp.float32)
    return jnp.where(allowed, jnp.exp(distance * log_keep), 0.0)


def group_stats(values):
    center = values - jnp.mean(values, axis=-1, keepdims=True)
    inverse = lax.rsqrt(jnp.mean(center * center, axis=-1, keepdims=True) + GROUP_EPS)
    return center * inverse, inverse


def retain_kernel(
    ends_ref,
    keep_ref,
    first_ref,
    query_w_ref,
    key_w_ref,
    value_w_ref,
    gate_w_ref,
    cos_ref,
    sin_ref,
    gain_ref,
    out_shard_ref,
    query_ref,
    key_ref,
    value_ref,
    gate_ref,
    retained_ref,
    gated_ref,
    branch_ref,
    out_w_ref,
    keys,
    values,
    gated_buf,
    out_w,
    out_sem,
    ring_recv_sem,
    ring_send_sem,
):
    head, block = pl.program_id(0), pl.program_id(1)
    blocks = pl.num_programs(1)
    index, final = head * blocks + block, pl.num_programs(0) * blocks - 1
    size = query_ref.shape[0]
    shard = out_shard_ref.shape[0]
    ring = Ring(out_w.shape[0] // shard, (out_w,), ring_recv_sem, ring_send_sem)
    batch = -(-ring.reach // 4)
    store = pltpu.make_async_copy(out_w, out_w_ref, out_sem.at[1])

    @pl.when(index == 0)
    def _():
        place = pl.ds(pl.multiple_of(ring.me * shard, shard), shard)
        load = pltpu.make_async_copy(out_shard_ref, out_w.at[place], out_sem.at[0])
        load.start()
        ring.greet()
        load.wait()

    @pl.when(index == 1)
    def _():
        ring.step(0)

    def ring_round(number):
        for extra in range(batch):
            distance = number * batch + extra + 1

            @pl.when(distance <= ring.reach)
            def _():
                ring.step(distance)

    @pl.when((index >= 3) & (index % 2 == 1))
    def _():
        ring_round(index // 2 - 1)

    here = pl.ds(pl.multiple_of(block * size, size), size)
    first = first_ref[here, :]
    cosine, sine = cos_ref[here, :], sin_ref[here, :]
    query = turn(row_product(first, query_w_ref[...]), cosine, sine).astype(jnp.bfloat16)
    key = turn(row_product(first, key_w_ref[...]), cosine, sine) * KH ** (-0.5)
    key = key.astype(jnp.bfloat16)
    value = row_product(first, value_w_ref[...]).astype(jnp.bfloat16)
    gate = row_product(first, gate_w_ref[...])
    query_ref[...] = query
    key_ref[...] = key
    value_ref[...] = value
    gate_ref[...] = gate
    keys[here, :] = key
    values[here, :] = value
    retained_ref[...] = jnp.zeros_like(retained_ref)

    def visit(other, carry):
        there = pl.ds(pl.multiple_of(other * size, size), size)
        decay = decay_block(ends_ref, keep_ref[head], block * size, other * size, size)
        weights = (turned_product(query, keys[there, :]) * decay).astype(jnp.bfloat16)
        retained_ref[...] += row_product(weights, values[there, :])
        return carry

    lax.fori_loop(0, block + 1, visit, 0)
    normed, inverse = group_stats(retained_ref[...])
    gated = (gate * jax.nn.sigmoid(gate) * (normed * gain_ref[0])).astype(jnp.bfloat16)
    gated_ref[...] = gated
    gated_buf[here, pl.ds(pl.multiple_of(head * VH, VH), VH)] = gated

    @pl.when(index == final)
    def _():
        ring_round(3)
        store.start()

        def one(number, carry):
            there = pl.ds(pl.multiple_of(number * 256, 256), 256)
            branch_ref[:, there] = turned_product(gated_buf[...], out_w[there, :]).astype(
                jnp.bfloat16
            )
            return carry

        lax.fori_loop(0, out_w.shape[0] // 256, one, 0, unroll=True)
        ring.drain()
        store.wait()


def retain(
    ends, log_keep, first_low, full, cosine, sine, group_values, out_shard, collective_id, size=256
):
    capacity, width = first_low.shape
    heads = group_values.shape[0]
    scalar = pl.BlockSpec(memory_space=pltpu.SMEM)
    table = pl.BlockSpec((capacity, KH // 2), lambda h, r: (0, 0))
    key_block = pl.BlockSpec((size, KH), lambda h, r: (r, h))
    value_block = pl.BlockSpec((size, VH), lambda h, r: (r, h))
    ratio = KH * heads * 2 // VH

    def shape(columns, kind):
        return jax.ShapeDtypeStruct((capacity, heads * columns), kind)

    return pl.pallas_call(
        retain_kernel,
        grid=(heads, capacity // size),
        out_shape=(
            shape(KH, jnp.bfloat16),
            shape(KH, jnp.bfloat16),
            shape(VH, jnp.bfloat16),
            shape(VH, jnp.float32),
            shape(VH, jnp.float32),
            shape(VH, jnp.bfloat16),
            jax.ShapeDtypeStruct((capacity, width), jnp.bfloat16),
            jax.ShapeDtypeStruct((width, heads * VH), jnp.bfloat16),
        ),
        in_specs=[
            scalar,
            scalar,
            pl.BlockSpec((capacity, width), lambda h, r: (0, 0)),
            pl.BlockSpec((width, KH), lambda h, r: (0, h)),
            pl.BlockSpec((width, KH), lambda h, r: (0, heads + h)),
            pl.BlockSpec((width, VH), lambda h, r: (0, ratio + h)),
            pl.BlockSpec((width, VH), lambda h, r: (0, ratio + heads + h)),
            table,
            table,
            pl.BlockSpec((1, 1, VH), lambda h, r: (h, 0, 0)),
            pl.BlockSpec(memory_space=pl.ANY),
        ],
        out_specs=(key_block, key_block, value_block, value_block, value_block, value_block)
        + (
            pl.BlockSpec((capacity, width), lambda h, r: (0, 0)),
            pl.BlockSpec(memory_space=pl.ANY),
        ),
        scratch_shapes=[
            pltpu.VMEM((capacity, KH), jnp.bfloat16),
            pltpu.VMEM((capacity, VH), jnp.bfloat16),
            pltpu.VMEM((capacity, heads * VH), jnp.bfloat16),
            pltpu.VMEM((width, heads * VH), jnp.bfloat16),
            pltpu.SemaphoreType.DMA((2,)),
        ]
        + ring_scratch(width // out_shard.shape[0], 1),
        compiler_params=pltpu.CompilerParams(
            collective_id=collective_id, has_side_effects=True, vmem_limit_bytes=56 << 20
        ),
        cost_estimate=pl.CostEstimate(
            flops=16_000_000_000, bytes_accessed=40 << 20, transcendentals=0
        ),
    )(
        ends,
        log_keep,
        first_low,
        full,
        full,
        full,
        full,
        cosine,
        sine,
        group_values[:, None, :],
        out_shard,
    )


def back_kernel(
    rows,
    block,
    heads,
    ends_ref,
    keep_ref,
    leave_ref,
    middle_low_ref,
    out_w_ref,
    retained_ref,
    gate_ref,
    group_gain_ref,
    query_ref,
    key_ref,
    value_ref,
    cos_ref,
    sin_ref,
    gated_ref,
    first_ref,
    full_ref,
    total,
    weight_grad_ref,
    input_grad_ref,
    group_grad_ref,
    mine,
    near,
    far,
    near_sem,
    far_sem,
    done_sem,
    out_sem,
    cross_sem,
    give_sem,
    out_w,
    query_buf,
    key_buf,
    value_buf,
    gated_buf,
    first_buf,
    middle_low,
    flip_buf,
    grad_buf,
    stream_buf,
    tile_buf,
    input_grad_buf,
    retained_buf,
    gate_buf,
    grad_gated_buf,
    upstream_buf,
    query_grad,
    key_grad,
    value_grad,
    load_sem,
    stream_sem,
    group_sem,
    store_sem,
):
    capacity, width = leave_ref.shape
    blocks, tiles = capacity // block, width // block
    pairs = capacity // (2 * rows)
    finish = heads * blocks
    pace = max(1, pairs // (finish + tiles))
    low, f32 = jnp.bfloat16, jnp.float32
    sems = (near_sem, far_sem, done_sem, out_sem, cross_sem, give_sem)
    line = Line(rows, mine, near, far, total, *sems, lags=(1, 2))

    def part(index, size=block):
        return pl.ds(pl.multiple_of(index * size, size), size)

    held = [
        pltpu.make_async_copy(source, target, load_sem.at[index])
        for index, (source, target) in enumerate(
            (
                (leave_ref, mine),
                (middle_low_ref, middle_low),
                (out_w_ref, out_w),
                (query_ref, query_buf),
                (key_ref, key_buf),
                (value_ref, value_buf),
                (gated_ref, gated_buf),
                (first_ref, first_buf),
            )
        )
    ]

    def load_group(index):
        slot = index % 2
        here, there = part(index % blocks), part(index // blocks, VH)
        return [
            pltpu.make_async_copy(
                retained_ref.at[here, there], retained_buf.at[slot], group_sem.at[2 * slot]
            ),
            pltpu.make_async_copy(
                gate_ref.at[here, there], gate_buf.at[slot], group_sem.at[2 * slot + 1]
            ),
        ]

    def load_tile(index):
        slot = index % 2
        return pltpu.make_async_copy(
            full_ref.at[part(index)], stream_buf.at[slot], stream_sem.at[slot]
        )

    def store_tile(index):
        return pltpu.make_async_copy(tile_buf, weight_grad_ref.at[part(index)], store_sem.at[0])

    def store_input(index):
        return pltpu.make_async_copy(
            input_grad_buf, input_grad_ref.at[:, part(index)], store_sem.at[1]
        )

    held[0].start()
    group_grad_ref[...] = jnp.zeros_like(group_grad_ref)
    line.greet()
    held[0].wait()
    for copy in held[1:-2] + load_group(0):
        copy.start()

    def attend_stage(index):
        head, place = index // blocks, index % blocks

        @pl.when(index == 0)
        def _():
            for copy in held[1:-2]:
                copy.wait()
            for copy in held[-2:]:
                copy.start()
            load_tile(0).start()

        for copy in load_group(index):
            copy.wait()

        @pl.when(index < heads * blocks - 1)
        def _():
            for copy in load_group(index + 1):
                copy.start()

        @pl.when(place == 0)
        def _():
            key_grad[...] = jnp.zeros_like(key_grad)
            value_grad[...] = jnp.zeros_like(value_grad)

        slot = index % 2
        here = part(place)
        keys_here, values_here = part(head, KH), part(head, VH)
        gain = group_gain_ref[pl.ds(head, 1), :]
        gate_place = pl.ds(pl.multiple_of(heads * (2 * KH + VH) + head * VH, VH), VH)
        grad_gated_buf[...] = row_product(middle_low[here, :], out_w[:, values_here])

        def gate_rows(piece, carry):
            few = pl.ds(pl.multiple_of(piece * 32, 32), 32)
            there = pl.ds(pl.multiple_of(place * block + piece * 32, 32), 32)
            normed, inverse = group_stats(retained_buf[slot, few, :])
            gate, grad_gated = gate_buf[slot, few, :], grad_gated_buf[few, :]
            sigmoid = jax.nn.sigmoid(gate)
            slope = sigmoid * (1.0 + gate * (1.0 - sigmoid))
            grad_buf[there, gate_place] = (grad_gated * (normed * gain) * slope).astype(low)
            grad_out = grad_gated * (gate * sigmoid)
            group_grad_ref[pl.ds(head, 1), :] += jnp.sum(grad_out * normed, axis=0, keepdims=True)
            scaled = grad_out * gain
            plain_mean = jnp.mean(scaled, axis=-1, keepdims=True)
            cross_mean = jnp.mean(scaled * normed, axis=-1, keepdims=True)
            upstream_buf[few, :] = (
                inverse * (scaled - plain_mean - normed * cross_mean)
            ).astype(low)
            return carry

        lax.fori_loop(0, block // 32, gate_rows, 0, unroll=4)
        upstream = upstream_buf[...]
        query = query_buf[here, keys_here]
        query_grad[...] = jnp.zeros_like(query_grad)

        def visit(other, carry):
            there = part(other)
            decay = decay_block(ends_ref, keep_ref[head], place * block, other * block, block)
            key = key_buf[there, keys_here]
            weights = (turned_product(query, key) * decay).astype(low)
            value_grad[there, :] += outer_product(weights, upstream)
            scores = turned_product(upstream, value_buf[there, values_here]) * decay
            scores = scores.astype(low)
            query_grad[...] += row_product(scores, key)
            key_grad[there, :] += outer_product(scores, query)
            return carry

        lax.fori_loop(0, place + 1, visit, 0)
        cosine, sine = cos_ref[here, :], sin_ref[here, :]
        grad_buf[here, keys_here] = turn(query_grad[...], cosine, -sine).astype(low)

        @pl.when(place == blocks - 1)
        def _():
            def one(other, carry):
                there = part(other)
                turned = turn(key_grad[there, :] * KH ** (-0.5), cos_ref[there, :], -sin_ref[there, :])
                grad_buf[there, part(heads + head, KH)] = turned.astype(low)
                value_place = pl.ds(pl.multiple_of(heads * 2 * KH + head * VH, VH), VH)
                grad_buf[there, value_place] = value_grad[there, :].astype(low)
                return carry

            lax.fori_loop(0, blocks, one, 0)

    def tile_stage(index):
        columns = grad_buf.shape[1]

        @pl.when(index == 0)
        def _():
            for copy in held[-2:]:
                copy.wait()

        @pl.when(index < tiles - 1)
        def _():
            load_tile(index + 1).start()

        @pl.when(index > 0)
        def _():
            store_tile(index - 1).wait()
            store_input(index - 1).wait()

        load_tile(index).wait()
        here = part(index)
        flip_buf[...] = first_buf[:, here].T

        def one(number, carry):
            there = part(number, 512)
            tile_buf[:, there] = row_product(flip_buf[...], grad_buf[:, there]).astype(low)
            return carry

        lax.fori_loop(0, columns // 512, one, 0, unroll=True)

        flip_buf[...] = middle_low[:, here].T

        def last(number, carry):
            there = pl.ds(pl.multiple_of(columns + number * 512, 512), 512)
            tile_buf[:, there] = row_product(
                flip_buf[...], gated_buf[:, part(number, 512)]
            ).astype(low)
            return carry

        lax.fori_loop(0, gated_buf.shape[1] // 512, last, 0, unroll=True)
        store_tile(index).start()

        def inward(number, carry):
            there = part(number)
            input_grad_buf[there, :] = turned_product(
                grad_buf[there, :], stream_buf[index % 2]
            ).astype(low)
            return carry

        lax.fori_loop(0, blocks, inward, 0, unroll=True)
        store_input(index).start()

    def step(index, carry):
        line.step(index, pairs)

        work = index // pace

        @pl.when((index % pace == 0) & (work < finish))
        def _():
            attend_stage(work)

        @pl.when((index % pace == 0) & (work >= finish) & (work < finish + tiles))
        def _():
            tile_stage(work - finish)

        return carry

    lax.fori_loop(0, max(pairs + 3, (finish + tiles) * pace), step, 0)

    def drain(pair, carry):
        line.arrive(pair)
        line.release(pair)
        line.drain(pair)
        return carry

    lax.fori_loop(0, pairs, drain, 0)
    store_tile(tiles - 1).wait()
    store_input(tiles - 1).wait()


def back_stage(
    ends,
    log_keep,
    leave,
    middle_low,
    mix_out,
    retained,
    gate,
    group_values,
    query,
    key,
    value,
    cosine,
    sine,
    gated,
    first_low,
    full,
    collective_id,
    rows=32,
    block=256,
):
    capacity, width = leave.shape
    heads = group_values.shape[0]
    columns, units = full.shape[1], gated.shape[1]
    low, f32 = jnp.bfloat16, jnp.float32
    anywhere, kept = pl.BlockSpec(memory_space=pl.ANY), pl.BlockSpec(memory_space=pltpu.VMEM)
    scalar = pl.BlockSpec(memory_space=pltpu.SMEM)
    return pl.pallas_call(
        functools.partial(back_kernel, rows, block, heads),
        out_shape=(
            jax.ShapeDtypeStruct((capacity, width), low),
            jax.ShapeDtypeStruct((width, columns + units), low),
            jax.ShapeDtypeStruct((capacity, width), low),
            jax.ShapeDtypeStruct((heads, VH), f32),
        ),
        in_specs=[scalar] * 2
        + [anywhere] * 5
        + [kept]
        + [anywhere] * 3
        + [kept] * 2
        + [anywhere] * 3,
        out_specs=(kept, anywhere, anywhere, kept),
        scratch_shapes=line_scratch(capacity, width, rows)
        + [
            pltpu.VMEM((width, units), low),
            pltpu.VMEM(query.shape, low),
            pltpu.VMEM(key.shape, low),
            pltpu.VMEM(value.shape, low),
            pltpu.VMEM(gated.shape, low),
            pltpu.VMEM((capacity, width), low),
            pltpu.VMEM((capacity, width), low),
            pltpu.VMEM((block, capacity), low),
            pltpu.VMEM((capacity, columns), low),
            pltpu.VMEM((2, block, columns), low),
            pltpu.VMEM((block, columns + units), low),
            pltpu.VMEM((capacity, block), low),
            pltpu.VMEM((2, block, VH), f32),
            pltpu.VMEM((2, block, VH), f32),
            pltpu.VMEM((block, VH), f32),
            pltpu.VMEM((block, VH), low),
            pltpu.VMEM((block, KH), f32),
            pltpu.VMEM((capacity, KH), f32),
            pltpu.VMEM((capacity, VH), f32),
            pltpu.SemaphoreType.DMA((8,)),
            pltpu.SemaphoreType.DMA((2,)),
            pltpu.SemaphoreType.DMA((4,)),
            pltpu.SemaphoreType.DMA((2,)),
        ],
        compiler_params=pltpu.CompilerParams(
            collective_id=collective_id, has_side_effects=True, vmem_limit_bytes=62 << 20
        ),
        cost_estimate=pl.CostEstimate(
            flops=100_000_000_000, bytes_accessed=40 << 20, transcendentals=0
        ),
    )(
        ends,
        log_keep,
        leave,
        middle_low,
        mix_out,
        retained,
        gate,
        group_values,
        query,
        key,
        value,
        cosine,
        sine,
        gated,
        first_low,
        full,
    )


def last_kernel(
    rows,
    ways,
    back_ref,
    tokens_ref,
    middle_ref,
    sum_ref,
    leave_ref,
    norm_gain_ref,
    norm_grad_ref,
    group_grad_ref,
    token_grad_ref,
    layer_ref,
    small_ref,
    total,
    mine,
    near,
    far,
    near_sem,
    far_sem,
    done_sem,
    out_sem,
    cross_sem,
    give_sem,
    token_buf,
    middle_buf,
    sum_buf,
    leave_buf,
    layer_buf,
    small_buf,
    small_in,
    load_sem,
    store_sem,
    layer_sem,
    small_send_sem,
    small_recv_sem,
):
    capacity, width = back_ref.shape
    pairs = capacity // (2 * rows)
    heads, group = group_grad_ref.shape
    f32 = jnp.float32
    sems = (near_sem, far_sem, done_sem, out_sem, cross_sem, give_sem)
    line = Line(rows, mine, near, far, total, *sems, lags=(1, 2))
    me = lax.axis_index("dp")
    peers = [lax.rem(me + distance, ways) for distance in range(1, ways)]
    loads = [
        pltpu.make_async_copy(source, target, load_sem.at[index])
        for index, (source, target) in enumerate(
            (
                (back_ref, mine),
                (tokens_ref, token_buf),
                (middle_ref, middle_buf),
                (sum_ref, sum_buf),
                (leave_ref, leave_buf),
            )
        )
    ]

    def part(pair):
        return pl.ds(pl.multiple_of(pair * 2 * rows, 2 * rows), 2 * rows)

    def store(pair):
        return pltpu.make_async_copy(
            middle_buf.at[part(pair)], token_grad_ref.at[part(pair)], store_sem.at[pair]
        )

    def store_layer(pair):
        slot = pair % 2
        return pltpu.make_async_copy(
            layer_buf.at[slot], layer_ref.at[part(pair)], layer_sem.at[slot]
        )

    def share(distance):
        return pltpu.make_async_remote_copy(
            small_buf,
            small_in.at[distance],
            small_send_sem.at[distance],
            small_recv_sem.at[distance],
            device_id={"dp": peers[distance]},
            device_id_type=MESH,
        )

    loads[0].start()
    small_buf[...] = jnp.zeros_like(small_buf)
    small_buf[2:4, :] = norm_grad_ref[...]
    for head in range(heads):
        small_buf[4:5, head * group : (head + 1) * group] = group_grad_ref[head : head + 1, :]
    line.greet(peers)
    loads[0].wait()

    def norm_stage(pair):
        line.arrive(pair)

        @pl.when(pair == 0)
        def _():
            for copy in loads[1:]:
                copy.wait()

        @pl.when(pair > 1)
        def _():
            store_layer(pair - 2).wait()

        here = part(pair)
        values = token_buf[here, :].astype(f32)
        layer_buf[pair % 2] = (
            values + sum_buf[here, :].astype(f32) + leave_buf[here, :].astype(f32)
        )
        result, gain_grad, shift_grad = norm_back_rows(
            values, total[here, :].astype(f32), norm_gain_ref[...]
        )
        middle_buf[here, :] += result
        small_buf[0:1, :] += gain_grad
        small_buf[1:2, :] += shift_grad
        store(pair).start()
        store_layer(pair).start()

    def step(index, carry):
        line.step(index, pairs)

        @pl.when(index == 0)
        def _():
            for copy in loads[1:]:
                copy.start()

        @pl.when(index >= 5)
        def _():
            norm_stage(index - 5)

        return carry

    lax.fori_loop(0, pairs + 5, step, 0)
    for distance in range(ways - 1):
        share(distance).start()

    def drain(pair, carry):
        line.release(pair)
        line.drain(pair)
        store(pair).wait()
        return carry

    lax.fori_loop(0, pairs, drain, 0)
    store_layer(pairs - 2).wait()
    store_layer(pairs - 1).wait()
    for distance in range(ways - 1):
        share(distance).wait()
    small_ref[...] = small_buf[...]
    for distance in range(ways - 1):
        small_ref[...] += small_in[distance]


def last_stage(
    back,
    tokens,
    middle,
    branch_sum,
    leave_sum,
    norm_gain,
    norm_grad,
    group_grad,
    ways,
    collective_id,
    rows=32,
):
    capacity, width = back.shape
    low, f32 = jnp.bfloat16, jnp.float32
    anywhere, kept = pl.BlockSpec(memory_space=pl.ANY), pl.BlockSpec(memory_space=pltpu.VMEM)
    small = (8, width)
    return pl.pallas_call(
        functools.partial(last_kernel, rows, ways),
        out_shape=(
            jax.ShapeDtypeStruct((capacity, width), f32),
            jax.ShapeDtypeStruct((capacity, width), f32),
            jax.ShapeDtypeStruct(small, f32),
        ),
        in_specs=[anywhere] * 5 + [kept] * 3,
        out_specs=(anywhere, anywhere, kept),
        scratch_shapes=[pltpu.VMEM((capacity, width), low)]
        + line_scratch(capacity, width, rows)
        + [
            pltpu.VMEM((capacity, width), low),
            pltpu.VMEM((capacity, width), f32),
            pltpu.VMEM((capacity, width), low),
            pltpu.VMEM((capacity, width), low),
            pltpu.VMEM((2, 2 * rows, width), f32),
            pltpu.VMEM(small, f32),
            pltpu.VMEM((ways - 1, *small), f32),
            pltpu.SemaphoreType.DMA((5,)),
            pltpu.SemaphoreType.DMA((capacity // (2 * rows),)),
            pltpu.SemaphoreType.DMA((2,)),
            pltpu.SemaphoreType.DMA((ways - 1,)),
            pltpu.SemaphoreType.DMA((ways - 1,)),
        ],
        compiler_params=pltpu.CompilerParams(
            collective_id=collective_id, has_side_effects=True, vmem_limit_bytes=52 << 20
        ),
        cost_estimate=pl.CostEstimate(
            flops=100_000_000_000, bytes_accessed=40 << 20, transcendentals=0
        ),
    )(back, tokens, middle, branch_sum, leave_sum, norm_gain[None], norm_grad, group_grad)


def local(
    tokens,
    lengths,
    cotangent,
    qk_weight,
    qk_first,
    qk_second,
    inner_weight,
    inner_first,
    inner_second,
    outer_weight,
    outer_first,
    outer_second,
    norm_params,
    norm_first,
    norm_second,
    group_gain,
    group_first,
    group_second,
):
    capacity = tokens.shape[0]
    local_heads = group_gain.shape[0]
    low = jnp.bfloat16
    tensor_index, data_index = lax.axis_index("tensor"), lax.axis_index("dp")

    def joined(shards):
        return jnp.concatenate([part.astype(low) for part in shards], axis=1)

    def gather(shards):
        return lax.all_gather(joined(shards), "dp", axis=0, tiled=True)

    def scatter(grad):
        return lax.psum_scatter(grad, "dp", scatter_dimension=0, tiled=True)

    norm_cols, group_cols = norm_params.shape[1], group_gain.shape[1]
    small = lax.all_gather(
        jnp.concatenate([norm_params.reshape(-1), group_gain.reshape(-1)]).astype(low), "dp"
    ).astype(jnp.float32)
    ways = small.shape[0]
    norm_values = small[:, : 4 * norm_cols].reshape(ways, 4, norm_cols)
    norm_values = norm_values.transpose(1, 0, 2).reshape(4, -1)
    group_values = small[:, 4 * norm_cols :].reshape(ways, local_heads, group_cols)
    group_values = group_values.transpose(1, 0, 2).reshape(local_heads, -1)
    first_full = gather([qk_weight[0], qk_weight[1], inner_weight[0], inner_weight[1]])
    mix_shard = outer_weight[0].astype(low)
    mlp_shard = joined([inner_weight[2], inner_weight[3]])
    out_shard = outer_weight[1].astype(low)
    row_index, sequence_id, position, live_rows = sequence_layout(lengths[0], capacity)
    cosine, sine = rotation_tables(position, KH)
    ends = jnp.cumsum(lengths[0])
    head_ids = tensor_index * local_heads + jnp.arange(local_heads, dtype=jnp.int32)
    log_keep = jnp.log1p(-jnp.exp2(-(5.0 + head_ids.astype(jnp.float32))))
    inputs = tokens.astype(jnp.float32)
    first_out, unused_normed, unused_inverse = layer_norm(
        inputs, norm_values[0], norm_values[1], NORM_EPS
    )
    first_low = first_out.astype(low)
    query, key, value, gate, retained, gated, branch, mix_out = retain(
        ends, log_keep, first_low, first_full, cosine, sine, group_values, mix_shard, 3
    )
    grad_top = cotangent.astype(jnp.float32) * live_rows.astype(jnp.float32)[:, None]
    top_low = grad_top.astype(low)
    branch_sum, leave, mlp_grad, grad_middle, middle_low, norm_two = middle_stage(
        branch, tokens, top_low, norm_values[2], norm_values[3], mlp_shard, out_shard, 0
    )
    mlp_part = scatter(mlp_grad)
    leave_sum, first_grad, back_first, grad_group_gain = back_stage(
        ends,
        log_keep,
        leave,
        middle_low,
        mix_out,
        retained,
        gate,
        group_values,
        query,
        key,
        value,
        cosine,
        sine,
        gated,
        first_low,
        first_full,
        1,
    )
    first_part = scatter(first_grad)
    back_first, mlp_part = lax.optimization_barrier((back_first, mlp_part))
    token_grad, layer_out, small_grad = last_stage(
        back_first,
        tokens,
        grad_middle,
        branch_sum,
        leave_sum,
        norm_values[0],
        norm_two,
        grad_group_gain,
        ways,
        2,
    )
    norm_grad = lax.dynamic_slice(small_grad, (0, data_index * norm_cols), (4, norm_cols))
    group_grad = lax.dynamic_slice(
        small_grad[4, : local_heads * VH].reshape(local_heads, VH),
        (0, data_index * group_cols),
        (local_heads, group_cols),
    )
    qk_cols, mix_cols = local_heads * KH, local_heads * VH
    starts = [qk_cols, 2 * qk_cols, 2 * qk_cols + mix_cols, 2 * qk_cols + 2 * mix_cols]
    query_grad, key_grad, value_grad, gate_grad, mix_out_part = jnp.split(
        first_part, starts, axis=1
    )
    qk_grad = jnp.stack([query_grad, key_grad]).astype(jnp.float32)
    units = out_shard.shape[1]
    left_grad, right_grad, mlp_out_part = jnp.split(mlp_part, [units, 2 * units], axis=1)
    inner_grad = jnp.stack([value_grad, gate_grad, left_grad, right_grad]).astype(jnp.float32)
    outer_grad = jnp.stack([mix_out_part, mlp_out_part]).astype(jnp.float32)
    qk_new = adam_update(qk_weight, qk_grad, qk_first, qk_second, MATRIX_RATE, WEIGHT_DECAY)
    inner_new = adam_update(
        inner_weight, inner_grad, inner_first, inner_second, MATRIX_RATE, WEIGHT_DECAY
    )
    outer_new = adam_update(
        outer_weight, outer_grad, outer_first, outer_second, MATRIX_RATE, WEIGHT_DECAY
    )
    norm_new = adam_update(norm_params, norm_grad, norm_first, norm_second, VECTOR_RATE, 0.0)
    group_new = adam_update(group_gain, group_grad, group_first, group_second, VECTOR_RATE, 0.0)
    return (layer_out, token_grad, *qk_new, *inner_new, *outer_new, *norm_new, *group_new)


def solution(mesh):
    in_specs = (
        P("dp", None),
        P("dp", None),
        P("dp", None),
        P(None, "dp", "tensor"),
        P(None, "dp", "tensor"),
        P(None, "dp", "tensor"),
        P(None, "dp", "tensor"),
        P(None, "dp", "tensor"),
        P(None, "dp", "tensor"),
        P(None, "dp", "tensor"),
        P(None, "dp", "tensor"),
        P(None, "dp", "tensor"),
        P(None, "dp"),
        P(None, "dp"),
        P(None, "dp"),
        P("tensor", "dp"),
        P("tensor", "dp"),
        P("tensor", "dp"),
    )
    out_specs = (
        P("dp", None),
        P("dp", None),
        P(None, "dp", "tensor"),
        P(None, "dp", "tensor"),
        P(None, "dp", "tensor"),
        P(None, "dp", "tensor"),
        P(None, "dp", "tensor"),
        P(None, "dp", "tensor"),
        P(None, "dp", "tensor"),
        P(None, "dp", "tensor"),
        P(None, "dp", "tensor"),
        P(None, "dp"),
        P(None, "dp"),
        P(None, "dp"),
        P("tensor", "dp"),
        P("tensor", "dp"),
        P("tensor", "dp"),
    )
    return jax.shard_map(local, mesh=mesh, in_specs=in_specs, out_specs=out_specs, check_vma=False)
```

```python
import functools
import math

import jax
import jax.numpy as jnp
from jax import lax
from jax.experimental import pallas as pl
from jax.experimental.pallas import tpu as pltpu
from jax.sharding import PartitionSpec as P

MESH = pl.DeviceIdType.MESH

KH = 256
VH = 512
SLOTS = 4
STEP = 10


NORM_EPS = 1e-05
GROUP_EPS = 1.0
BETA_FIRST = 0.9
BETA_SECOND = 0.95
ADAM_EPS = 1e-08
MATRIX_RATE = 0.05
VECTOR_RATE = 0.5
WEIGHT_DECAY = 0.1


def layer_norm(values, gain_row, shift_row, epsilon):
    center = values - jnp.mean(values, axis=-1, keepdims=True)
    inverse = lax.rsqrt(jnp.mean(center * center, axis=-1, keepdims=True) + epsilon)
    normed = center * inverse
    return (normed * gain_row + shift_row, normed, inverse)


def norm_back(upstream, normed, inverse, gain_row):
    scaled = upstream * gain_row
    plain_mean = jnp.mean(scaled, axis=-1, keepdims=True)
    cross_mean = jnp.mean(scaled * normed, axis=-1, keepdims=True)
    result = inverse * (scaled - plain_mean - normed * cross_mean)
    return (result, jnp.sum(upstream * normed, axis=0), jnp.sum(upstream, axis=0))


def sequence_layout(lengths_row, capacity):
    seq_ends = jnp.cumsum(lengths_row)
    row_index = jnp.arange(capacity, dtype=jnp.int32)
    sequence_id = jnp.sum((row_index[:, None] >= seq_ends[None, :]).astype(jnp.int32), axis=1)
    starts = seq_ends - lengths_row
    slot_index = jnp.arange(lengths_row.shape[0], dtype=jnp.int32)
    row_start = jnp.sum(
        jnp.where(sequence_id[:, None] == slot_index[None, :], starts[None, :], 0), axis=1
    )
    position = row_index - row_start
    live_rows = row_index < seq_ends[-1]
    return (row_index, sequence_id, position, live_rows)


def decay_table(row_index, sequence_id, live_rows, head_ids):
    allowed = (
        (sequence_id[:, None] == sequence_id[None, :])
        & (row_index[:, None] >= row_index[None, :])
        & live_rows[:, None]
        & live_rows[None, :]
    )
    distance = jnp.maximum(row_index[:, None] - row_index[None, :], 0).astype(jnp.float32)
    log_keep = jnp.log1p(-jnp.exp2(-(5.0 + head_ids.astype(jnp.float32))))
    return jnp.where(allowed[None], jnp.exp(distance[None] * log_keep[:, None, None]), 0.0)


def rotation_tables(position, head_size):
    half_size = head_size // 2
    frequency = jnp.exp(
        -math.log(10000.0) * 2.0 * jnp.arange(half_size, dtype=jnp.float32) / head_size
    )
    angles = position.astype(jnp.float32)[:, None] * frequency[None, :]
    return (jnp.cos(angles), jnp.sin(angles))


def rotate(values, cosine, sine, head_size):
    row_count = values.shape[0]
    shaped = values.reshape(row_count, -1, 2, head_size // 2)
    front_half = shaped[:, :, 0]
    back_half = shaped[:, :, 1]
    cos_rows = cosine[:, None, :]
    sin_rows = sine[:, None, :]
    turned = jnp.stack(
        [
            front_half * cos_rows - back_half * sin_rows,
            front_half * sin_rows + back_half * cos_rows,
        ],
        axis=2,
    )
    return turned.reshape(row_count, -1)


def row_product(left, right):
    return jnp.dot(left, right, preferred_element_type=jnp.float32)


def turned_product(left, right):
    return lax.dot_general(
        left, right, (((1,), (1,)), ((), ())), preferred_element_type=jnp.float32
    )


def outer_product(left, right):
    return lax.dot_general(
        left, right, (((0,), (0,)), ((), ())), preferred_element_type=jnp.float32
    )


def adam_update(weight, gradient, moment, square, rate, decay_rate):
    moment_new = BETA_FIRST * moment + (1.0 - BETA_FIRST) * gradient
    square_new = BETA_SECOND * square + (1.0 - BETA_SECOND) * gradient * gradient
    first_hat = moment_new / (1.0 - BETA_FIRST**STEP)
    second_hat = square_new / (1.0 - BETA_SECOND**STEP)
    weight_new = weight - rate * (
        first_hat / (jnp.sqrt(second_hat) + ADAM_EPS) + decay_rate * weight
    )
    return (moment_new, square_new, weight_new)


class Ring:
    def __init__(self, count, results, recv_sem, send_sem):
        self.count, self.results, self.recv_sem, self.send_sem = count, results, recv_sem, send_sem
        me = lax.axis_index("dp")
        self.me, self.place = me, self.swap(me)
        self.right, self.left = self.owner(1), self.owner(-1)
        self.reach = count // 2

    def swap(self, index):
        if self.count != 8:
            return index
        return jnp.where(index < 4, index, jnp.where(index < 6, index + 2, index - 2))

    def owner(self, distance):
        return self.swap(lax.rem(self.place + distance + self.count, self.count))

    def greet(self):
        barrier = pltpu.get_barrier_semaphore()
        for device in (self.left, self.right):
            pl.semaphore_signal(barrier, inc=1, device_id={"dp": device}, device_id_type=MESH)
        pl.semaphore_wait(barrier, 2)

    def copies(self, owner, half, way):
        made = []
        for index, result in enumerate(self.results):
            rows = result.shape[0] // (2 * self.count)
            here = result.at[pl.ds(pl.multiple_of((owner * 2 + half) * rows, rows), rows)]
            made.append(
                pltpu.make_async_remote_copy(
                    here,
                    here,
                    self.send_sem.at[((way * 2 + half) * len(self.results) + index) * self.count + owner],
                    self.recv_sem.at[(half * len(self.results) + index) * self.count + owner],
                    device_id={"dp": self.left if way else self.right},
                    device_id_type=MESH,
                )
            )
        return made

    def streams(self):
        for half in range(2):
            for way in range(2):
                yield half, way, self.reach - (half + way) % 2

    def step(self, distance):
        for half, way, hops in self.streams():
            owner = self.owner(distance if way else -distance)

            @pl.when((distance >= 1) & (distance <= hops))
            def _():
                for copy in self.copies(owner, half, way):
                    copy.wait_recv()

            @pl.when(distance < hops)
            def _():
                for copy in self.copies(owner, half, way):
                    copy.start()

    def drain(self):
        for half, way, hops in self.streams():

            def one(distance, carry):
                for copy in self.copies(self.owner(distance if way else -distance), half, way):
                    copy.wait_send()
                return carry

            lax.fori_loop(0, hops, one, 0)


def ring_scratch(count, results):
    return [
        pltpu.SemaphoreType.DMA((2 * results * count,)),
        pltpu.SemaphoreType.DMA((4 * results * count,)),
    ]


class Line:
    def __init__(self, rows, mine, near, far, total, near_sem, far_sem, done_sem, out_sem, cross_sem, give_sem, lags=(1, 3)):
        self.lags = lags
        self.rows, self.mine, self.near, self.far, self.total = rows, mine, near, far, total
        self.near_sem, self.far_sem, self.done_sem = near_sem, far_sem, done_sem
        self.out_sem, self.cross_sem, self.give_sem = out_sem, cross_sem, give_sem
        me = lax.axis_index("tensor")
        self.me = me
        self.inner = (me == 1) | (me == 2)
        self.outer = (me == 0) | (me == 3)
        self.relay_to = jnp.where(self.inner, 3 - me, 1 + me // 3)
        self.away = jnp.where(self.inner, 3 * (me - 1), 1 + me // 3)
        owner = jnp.where(self.inner, me, 1 + me // 3)
        self.kept, self.passed = owner - 1, 2 - owner

    def at(self, chunk):
        return pl.ds(pl.multiple_of(chunk * self.rows, self.rows), self.rows)

    def greet(self, also=()):
        barrier = pltpu.get_barrier_semaphore()
        for device in also:
            pl.semaphore_signal(barrier, inc=1, device_id={"dp": device}, device_id_type=MESH)
        pl.semaphore_signal(barrier, inc=1, device_id={"tensor": self.away}, device_id_type=MESH)

        @pl.when(self.inner)
        def _():
            pl.semaphore_signal(
                barrier, inc=1, device_id={"tensor": self.relay_to}, device_id_type=MESH
            )
            pl.semaphore_wait(barrier, 2 + len(also))

        @pl.when(self.outer)
        def _():
            pl.semaphore_wait(barrier, 1 + len(also))

    def copy(self, source, target, send_sem, recv_sem, device):
        return pltpu.make_async_remote_copy(
            source, target, send_sem, recv_sem, device_id={"tensor": device}, device_id_type=MESH
        )

    def send_in(self, chunk):
        return self.copy(
            self.mine.at[self.at(chunk)],
            self.near.at[self.at(chunk)],
            self.out_sem.at[chunk],
            self.near_sem.at[chunk],
            self.away,
        )

    def send_across(self, pair, chunk):
        return self.copy(
            self.near.at[self.at(chunk)],
            self.far.at[self.at(pair)],
            self.out_sem.at[chunk],
            self.far_sem.at[pair],
            self.relay_to,
        )

    def give(self, chunk, send_sem, device):
        place = self.total.at[self.at(chunk)]
        return self.copy(place, place, send_sem, self.done_sem.at[chunk], device)

    def give_out(self, chunk):
        return self.give(chunk, self.give_sem.at[chunk], self.away)

    def give_across(self, pair, chunk):
        return self.give(chunk, self.cross_sem.at[pair], self.relay_to)

    def wide(self, ref, chunk):
        return ref[self.at(chunk), :].astype(jnp.float32)

    def relay(self, pair):
        passed, kept = 2 * pair + self.passed, 2 * pair + self.kept

        @pl.when(self.outer)
        def _():
            self.send_in(passed).start()
            self.send_in(kept).start()

        @pl.when(self.inner)
        def _():
            self.send_in(passed).wait_recv()
            added = self.wide(self.near, passed) + self.wide(self.mine, passed)
            self.near[self.at(passed), :] = added.astype(jnp.bfloat16)
            self.send_across(pair, passed).start()

    def own(self, pair):
        kept = 2 * pair + self.kept

        @pl.when(self.inner)
        def _():
            self.send_in(kept).wait_recv()
            self.send_across(pair, kept).wait_recv()
            added = self.wide(self.near, kept) + self.wide(self.mine, kept)
            added = added + self.wide(self.far, pair)
            self.total[self.at(kept), :] = added.astype(jnp.bfloat16)
            self.give_across(pair, kept).start()
            self.give_out(kept).start()

    def forward(self, pair):
        passed = 2 * pair + self.passed

        @pl.when(self.inner)
        def _():
            self.give_out(passed).wait_recv()
            self.give_out(passed).start()

    def step(self, index, pairs):
        own_lag, forward_lag = self.lags

        @pl.when(index < pairs)
        def _():
            self.relay(index)

        @pl.when((index >= own_lag) & (index < pairs + own_lag))
        def _():
            self.own(index - own_lag)

        @pl.when((index >= forward_lag) & (index < pairs + forward_lag))
        def _():
            self.forward(index - forward_lag)

    def arrive(self, pair):
        @pl.when(self.outer)
        def _():
            self.give_out(2 * pair).wait_recv()
            self.give_out(2 * pair + 1).wait_recv()

    def release(self, pair):
        @pl.when(self.outer)
        def _():
            self.send_in(2 * pair).wait_send()
            self.send_in(2 * pair + 1).wait_send()

    def drain(self, pair):
        passed, kept = 2 * pair + self.passed, 2 * pair + self.kept

        @pl.when(self.inner)
        def _():
            self.send_across(pair, passed).wait_send()
            self.give_across(pair, kept).wait_send()
            self.give_out(kept).wait_send()
            self.give_out(passed).wait_send()


def line_scratch(height, width, rows):
    chunks = height // rows
    wide = pltpu.VMEM((height, width), jnp.bfloat16)
    sems, half_sems = pltpu.SemaphoreType.DMA((chunks,)), pltpu.SemaphoreType.DMA((chunks // 2,))
    return [
        wide,
        wide,
        pltpu.VMEM((height // 2, width), jnp.bfloat16),
        sems,
        half_sems,
        sems,
        sems,
        half_sems,
        sems,
    ]


def norm_back_rows(values, back, gain_row):
    center = values - jnp.mean(values, axis=-1, keepdims=True)
    inverse = lax.rsqrt(jnp.mean(center * center, axis=-1, keepdims=True) + NORM_EPS)
    normed = center * inverse
    result, gain_grad, shift_grad = norm_back(back, normed, inverse, gain_row)
    return result, gain_grad[None], shift_grad[None]


def middle_kernel(
    rows,
    block,
    branch_ref,
    tokens_ref,
    top_ref,
    gain_ref,
    shift_ref,
    mlp_ref,
    out_w_ref,
    sum_ref,
    leave_ref,
    weight_grad_ref,
    middle_ref,
    middle_low_ref,
    norm_grad_ref,
    total,
    mine,
    near,
    far,
    near_sem,
    far_sem,
    done_sem,
    out_sem,
    cross_sem,
    give_sem,
    mlp_w,
    out_w,
    top_buf,
    hidden_buf,
    pair_buf,
    token_buf,
    leave_buf,
    tile_buf,
    flip_buf,
    piece_buf,
    wide_buf,
    low_buf,
    load_sem,
    piece_sem,
    store_sem,
    wide_sem,
    low_sem,
    ring_recv_sem,
    ring_send_sem,
):
    capacity, width = branch_ref.shape
    units = hidden_buf.shape[1]
    ways = width // mlp_ref.shape[0]
    ring = Ring(ways, (mlp_w, out_w), ring_recv_sem, ring_send_sem)
    blocks, tiles = capacity // block, width // block
    span = 2 * rows
    per, half = block // span, capacity // span
    pairs = 2 * half
    low, f32 = jnp.bfloat16, jnp.float32
    line = Line(rows, mine, near, far, total, near_sem, far_sem, done_sem, out_sem, cross_sem, give_sem)

    def part(index, size=block):
        return pl.ds(pl.multiple_of(index * size, size), size)

    def load_tokens(index):
        return pltpu.make_async_copy(tokens_ref.at[part(index)], token_buf, load_sem.at[3])

    def load_piece(index):
        slot = index % 2
        return pltpu.make_async_copy(
            tokens_ref.at[part(index, span)], piece_buf.at[slot], piece_sem.at[slot]
        )

    def store_leave(index):
        return pltpu.make_async_copy(leave_buf, leave_ref.at[part(index)], store_sem.at[0])

    def store_tile(index):
        return pltpu.make_async_copy(tile_buf, weight_grad_ref.at[part(index)], store_sem.at[1])

    store_sum = pltpu.make_async_copy(total.at[pl.ds(0, capacity)], sum_ref, store_sem.at[2])

    def store_middle(index):
        slot = index % 2
        return [
            pltpu.make_async_copy(
                wide_buf.at[slot], middle_ref.at[part(index, span)], wide_sem.at[slot]
            ),
            pltpu.make_async_copy(
                low_buf.at[slot], middle_low_ref.at[part(index, span)], low_sem.at[slot]
            ),
        ]

    shard = part(ring.me, mlp_ref.shape[0])
    load_mlp = pltpu.make_async_copy(mlp_ref, mlp_w.at[shard], load_sem.at[1])
    load_out = pltpu.make_async_copy(out_w_ref, out_w.at[shard], load_sem.at[2])
    load_mine = pltpu.make_async_copy(branch_ref, mine.at[pl.ds(0, capacity)], load_sem.at[0])
    load_top = pltpu.make_async_copy(top_ref, top_buf, load_sem.at[4])
    load_mine.start()
    norm_grad_ref[...] = jnp.zeros_like(norm_grad_ref)
    line.greet((ring.left, ring.right))
    load_mine.wait()
    load_mlp.start()
    load_out.start()

    def normalize(index):
        def wait(pair, carry):
            line.arrive(pair)
            line.release(pair)
            return carry

        lax.fori_loop(index * per, index * per + per, wait, 0)
        load_tokens(index).wait()

        def normalize_rows(piece, carry):
            here = part(piece, 32)
            there = part(index * (block // 32) + piece, 32)
            values = token_buf[here, :].astype(f32) + total[there, :].astype(f32)
            values, unused_normed, unused_inverse = layer_norm(
                values, gain_ref[...], shift_ref[...], NORM_EPS
            )
            mine[there, :] = values.astype(low)
            return carry

        lax.fori_loop(0, block // 32, normalize_rows, 0)

        @pl.when(index < blocks - 1)
        def _():
            load_tokens(index + 1).start()

        @pl.when(index == blocks - 1)
        def _():
            store_sum.start()

    def units_step(index, start, count):
        @pl.when((index == 0) & (start == 0))
        def _():
            load_top.wait()

        here = part(index)

        def one(number, carry):
            first = part(number, 256)
            second = pl.ds(pl.multiple_of(units + number * 256, 256), 256)
            left = row_product(mine[here, :], mlp_w[:, first])
            right = row_product(mine[here, :], mlp_w[:, second])
            back = row_product(top_buf[here, :], out_w[:, first])
            cdf = 0.5 * (1.0 + lax.erf(left * (1.0 / math.sqrt(2.0))))
            pdf = jnp.exp(-0.5 * left * left) * (1.0 / math.sqrt(2.0 * math.pi))
            gelu = left * cdf
            hidden_buf[here, first] = (gelu * right).astype(low)
            pair_buf[here, first] = (back * right * (cdf + left * pdf)).astype(low)
            pair_buf[here, second] = (back * gelu).astype(low)
            return carry

        lax.fori_loop(start, start + count, one, 0)

    def backward_step(index):
        here = part(index)

        def one(number, carry):
            there = part(number, 256)
            mine[part(blocks + index), there] = turned_product(
                pair_buf[here, :], mlp_w[there, :]
            ).astype(low)
            return carry

        lax.fori_loop(0, width // 256, one, 0, unroll=True)

    def leave_step(index):
        @pl.when(index > 0)
        def _():
            store_leave(index - 1).wait()

        here = part(index)

        def one(number, carry):
            there = part(number, 256)
            leave_buf[:, there] = turned_product(hidden_buf[here, :], out_w[there, :]).astype(low)
            return carry

        lax.fori_loop(0, width // 256, one, 0, unroll=True)
        store_leave(index).start()

    def tile_stage(index):
        @pl.when(index > 0)
        def _():
            store_tile(index - 1).wait()

        here = part(index)
        flip_buf[...] = mine[pl.ds(0, capacity), here].T

        def one(number, carry):
            there = part(number, 512)
            tile_buf[:, there] = row_product(flip_buf[...], pair_buf[:, there]).astype(low)
            return carry

        lax.fori_loop(0, 2 * units // 512, one, 0, unroll=True)
        flip_buf[...] = top_buf[:, here].T

        def last(number, carry):
            there = pl.ds(pl.multiple_of(2 * units + number * 512, 512), 512)
            tile_buf[:, there] = row_product(
                flip_buf[...], hidden_buf[:, part(number, 512)]
            ).astype(low)
            return carry

        lax.fori_loop(0, units // 512, last, 0, unroll=True)
        store_tile(index).start()

    def norm_stage(index):
        line.arrive(half + index)
        load_piece(index).wait()

        @pl.when(index < half - 1)
        def _():
            load_piece(index + 1).start()

        @pl.when(index > 1)
        def _():
            for copy in store_middle(index - 2):
                copy.wait()

        slot, here = index % 2, part(index, span)
        values = piece_buf[slot].astype(f32) + total[here, :].astype(f32)
        back = total[part(half + index, span), :].astype(f32)
        result, gain_grad, shift_grad = norm_back_rows(values, back, gain_ref[...])
        middle = top_buf[here, :].astype(f32) + result
        wide_buf[slot] = middle
        low_buf[slot] = middle.astype(low)
        norm_grad_ref[0:1, :] += gain_grad
        norm_grad_ref[1:2, :] += shift_grad
        for copy in store_middle(index):
            copy.start()

    count = units // 256
    lead = per + 8
    batch = -(-ring.reach // (lead // 3))

    def step(index, carry):
        line.step(index, pairs)

        @pl.when(index == 0)
        def _():
            load_mlp.wait()
            load_out.wait()
            ring.step(0)
            load_tokens(0).start()
            load_top.start()
            load_piece(0).start()

        @pl.when((index > 0) & (index <= lead) & (index % 3 == 0))
        def _():
            for extra in range(batch):
                distance = (index // 3 - 1) * batch + extra + 1

                @pl.when(distance <= ring.reach)
                def _():
                    ring.step(distance)

        work = index - lead

        @pl.when((work >= 0) & (work < 4 * blocks))
        def _():
            piece, stage = work // 4, work % 4

            @pl.when(stage == 0)
            def _():
                normalize(piece)

            @pl.when((stage == 1) | (stage == 2))
            def _():
                units_step(piece, (stage - 1) * (count // 2), count // 2)

            @pl.when(stage == 3)
            def _():
                backward_step(piece)
                leave_step(piece)

        @pl.when((work >= 4 * blocks) & (work < 4 * blocks + tiles))
        def _():
            tile_stage(work - 4 * blocks)

        @pl.when(index >= half + 5)
        def _():
            norm_stage(index - half - 5)

        return carry

    lax.fori_loop(0, pairs + 5, step, 0)

    def drain(pair, carry):
        line.drain(pair)

        @pl.when(pair >= half)
        def _():
            line.release(pair)

        return carry

    lax.fori_loop(0, pairs, drain, 0)
    ring.drain()
    store_leave(blocks - 1).wait()
    store_tile(tiles - 1).wait()
    store_sum.wait()
    for index in (half - 2, half - 1):
        for copy in store_middle(index):
            copy.wait()


def middle_stage(
    branch, tokens, top, gain, shift, mlp_shard, out_shard, collective_id, rows=32, block=256
):
    capacity, width = branch.shape
    units = out_shard.shape[1]
    ways = width // out_shard.shape[0]
    low, f32 = jnp.bfloat16, jnp.float32
    anywhere, held = pl.BlockSpec(memory_space=pl.ANY), pl.BlockSpec(memory_space=pltpu.VMEM)
    pair_sems = pltpu.SemaphoreType.DMA((2,))
    return pl.pallas_call(
        functools.partial(middle_kernel, rows, block),
        out_shape=(
            jax.ShapeDtypeStruct((capacity, width), low),
            jax.ShapeDtypeStruct((capacity, width), low),
            jax.ShapeDtypeStruct((width, 3 * units), low),
            jax.ShapeDtypeStruct((capacity, width), f32),
            jax.ShapeDtypeStruct((capacity, width), low),
            jax.ShapeDtypeStruct((2, width), f32),
        ),
        in_specs=[anywhere, anywhere, anywhere, held, held, anywhere, anywhere],
        out_specs=(anywhere,) * 5 + (held,),
        scratch_shapes=[pltpu.VMEM((2 * capacity, width), low)]
        + line_scratch(2 * capacity, width, rows)
        + [
            pltpu.VMEM((width, 2 * units), low),
            pltpu.VMEM((width, units), low),
            pltpu.VMEM((capacity, width), low),
            pltpu.VMEM((capacity, units), low),
            pltpu.VMEM((capacity, 2 * units), low),
            pltpu.VMEM((block, width), low),
            pltpu.VMEM((block, width), low),
            pltpu.VMEM((block, 3 * units), low),
            pltpu.VMEM((block, capacity), low),
            pltpu.VMEM((2, 2 * rows, width), low),
            pltpu.VMEM((2, 2 * rows, width), f32),
            pltpu.VMEM((2, 2 * rows, width), low),
            pltpu.SemaphoreType.DMA((5,)),
            pair_sems,
            pltpu.SemaphoreType.DMA((3,)),
            pair_sems,
            pair_sems,
        ]
        + ring_scratch(ways, 2),
        compiler_params=pltpu.CompilerParams(
            collective_id=collective_id, has_side_effects=True, vmem_limit_bytes=62 << 20
        ),
        cost_estimate=pl.CostEstimate(
            flops=200_000_000_000, bytes_accessed=40 << 20, transcendentals=0
        ),
    )(branch, tokens, top, gain[None], shift[None], mlp_shard, out_shard)


def turn(values, cosine, sine):
    half = values.shape[1] // 2
    front, back = values[:, :half], values[:, half:]
    return jnp.concatenate([front * cosine - back * sine, front * sine + back * cosine], axis=1)


def decay_block(ends_ref, log_keep, row_start, col_start, size):
    rows = row_start + lax.broadcasted_iota(jnp.int32, (size, 1), 0)
    cols = col_start + lax.broadcasted_iota(jnp.int32, (1, size), 1)
    row_slot = jnp.zeros((size, 1), jnp.int32)
    col_slot = jnp.zeros((1, size), jnp.int32)
    for slot in range(SLOTS):
        row_slot += (rows >= ends_ref[slot]).astype(jnp.int32)
        col_slot += (cols >= ends_ref[slot]).astype(jnp.int32)
    row_slot = jnp.where(rows < ends_ref[SLOTS - 1], row_slot, -1)
    distance = rows - cols
    allowed = (row_slot == col_slot) & (distance >= 0)
    distance = jnp.maximum(distance, 0).astype(jnp.float32)
    return jnp.where(allowed, jnp.exp(distance * log_keep), 0.0)


def group_stats(values):
    center = values - jnp.mean(values, axis=-1, keepdims=True)
    inverse = lax.rsqrt(jnp.mean(center * center, axis=-1, keepdims=True) + GROUP_EPS)
    return center * inverse, inverse


def retain_kernel(
    ends_ref,
    keep_ref,
    first_ref,
    query_w_ref,
    key_w_ref,
    value_w_ref,
    gate_w_ref,
    cos_ref,
    sin_ref,
    gain_ref,
    out_shard_ref,
    query_ref,
    key_ref,
    value_ref,
    gate_ref,
    retained_ref,
    gated_ref,
    branch_ref,
    out_w_ref,
    keys,
    values,
    gated_buf,
    out_w,
    out_sem,
    ring_recv_sem,
    ring_send_sem,
):
    head, block = pl.program_id(0), pl.program_id(1)
    blocks = pl.num_programs(1)
    index, final = head * blocks + block, pl.num_programs(0) * blocks - 1
    size = query_ref.shape[0]
    shard = out_shard_ref.shape[0]
    ring = Ring(out_w.shape[0] // shard, (out_w,), ring_recv_sem, ring_send_sem)
    batch = -(-ring.reach // 4)
    store = pltpu.make_async_copy(out_w, out_w_ref, out_sem.at[1])

    @pl.when(index == 0)
    def _():
        place = pl.ds(pl.multiple_of(ring.me * shard, shard), shard)
        load = pltpu.make_async_copy(out_shard_ref, out_w.at[place], out_sem.at[0])
        load.start()
        ring.greet()
        load.wait()
        ring.step(0)

    def ring_round(number):
        for extra in range(batch):
            distance = number * batch + extra + 1

            @pl.when(distance <= ring.reach)
            def _():
                ring.step(distance)

    @pl.when((index >= 1) & (index < 4))
    def _():
        ring_round(index - 1)

    here = pl.ds(pl.multiple_of(block * size, size), size)
    first = first_ref[here, :]
    cosine, sine = cos_ref[here, :], sin_ref[here, :]
    query = turn(row_product(first, query_w_ref[...]), cosine, sine).astype(jnp.bfloat16)
    key = turn(row_product(first, key_w_ref[...]), cosine, sine) * KH ** (-0.5)
    key = key.astype(jnp.bfloat16)
    value = row_product(first, value_w_ref[...]).astype(jnp.bfloat16)
    gate = row_product(first, gate_w_ref[...])
    query_ref[...] = query
    key_ref[...] = key
    value_ref[...] = value
    gate_ref[...] = gate
    keys[here, :] = key
    values[here, :] = value
    retained_ref[...] = jnp.zeros_like(retained_ref)

    def visit(other, carry):
        there = pl.ds(pl.multiple_of(other * size, size), size)
        decay = decay_block(ends_ref, keep_ref[head], block * size, other * size, size)
        weights = (turned_product(query, keys[there, :]) * decay).astype(jnp.bfloat16)
        retained_ref[...] += row_product(weights, values[there, :])
        return carry

    lax.fori_loop(0, block + 1, visit, 0)
    normed, inverse = group_stats(retained_ref[...])
    gated = (gate * jax.nn.sigmoid(gate) * (normed * gain_ref[0])).astype(jnp.bfloat16)
    gated_ref[...] = gated
    gated_buf[here, pl.ds(pl.multiple_of(head * VH, VH), VH)] = gated

    @pl.when(index == final)
    def _():
        ring_round(3)
        store.start()

        def one(number, carry):
            there = pl.ds(pl.multiple_of(number * 256, 256), 256)
            branch_ref[:, there] = turned_product(gated_buf[...], out_w[there, :]).astype(
                jnp.bfloat16
            )
            return carry

        lax.fori_loop(0, out_w.shape[0] // 256, one, 0, unroll=True)
        ring.drain()
        store.wait()


def retain(
    ends, log_keep, first_low, full, cosine, sine, group_values, out_shard, collective_id, size=512
):
    capacity, width = first_low.shape
    heads = group_values.shape[0]
    scalar = pl.BlockSpec(memory_space=pltpu.SMEM)
    table = pl.BlockSpec((capacity, KH // 2), lambda h, r: (0, 0))
    key_block = pl.BlockSpec((size, KH), lambda h, r: (r, h))
    value_block = pl.BlockSpec((size, VH), lambda h, r: (r, h))
    ratio = KH * heads * 2 // VH

    def shape(columns, kind):
        return jax.ShapeDtypeStruct((capacity, heads * columns), kind)

    return pl.pallas_call(
        retain_kernel,
        grid=(heads, capacity // size),
        out_shape=(
            shape(KH, jnp.bfloat16),
            shape(KH, jnp.bfloat16),
            shape(VH, jnp.bfloat16),
            shape(VH, jnp.float32),
            shape(VH, jnp.float32),
            shape(VH, jnp.bfloat16),
            jax.ShapeDtypeStruct((capacity, width), jnp.bfloat16),
            jax.ShapeDtypeStruct((width, heads * VH), jnp.bfloat16),
        ),
        in_specs=[
            scalar,
            scalar,
            pl.BlockSpec((capacity, width), lambda h, r: (0, 0)),
            pl.BlockSpec((width, KH), lambda h, r: (0, h)),
            pl.BlockSpec((width, KH), lambda h, r: (0, heads + h)),
            pl.BlockSpec((width, VH), lambda h, r: (0, ratio + h)),
            pl.BlockSpec((width, VH), lambda h, r: (0, ratio + heads + h)),
            table,
            table,
            pl.BlockSpec((1, 1, VH), lambda h, r: (h, 0, 0)),
            pl.BlockSpec(memory_space=pl.ANY),
        ],
        out_specs=(key_block, key_block, value_block, value_block, value_block, value_block)
        + (
            pl.BlockSpec((capacity, width), lambda h, r: (0, 0)),
            pl.BlockSpec(memory_space=pl.ANY),
        ),
        scratch_shapes=[
            pltpu.VMEM((capacity, KH), jnp.bfloat16),
            pltpu.VMEM((capacity, VH), jnp.bfloat16),
            pltpu.VMEM((capacity, heads * VH), jnp.bfloat16),
            pltpu.VMEM((width, heads * VH), jnp.bfloat16),
            pltpu.SemaphoreType.DMA((2,)),
        ]
        + ring_scratch(width // out_shard.shape[0], 1),
        compiler_params=pltpu.CompilerParams(
            collective_id=collective_id, has_side_effects=True, vmem_limit_bytes=56 << 20
        ),
        cost_estimate=pl.CostEstimate(
            flops=16_000_000_000, bytes_accessed=40 << 20, transcendentals=0
        ),
    )(
        ends,
        log_keep,
        first_low,
        full,
        full,
        full,
        full,
        cosine,
        sine,
        group_values[:, None, :],
        out_shard,
    )


def back_kernel(
    rows,
    block,
    heads,
    ends_ref,
    keep_ref,
    leave_ref,
    middle_low_ref,
    out_w_ref,
    retained_ref,
    gate_ref,
    group_gain_ref,
    query_ref,
    key_ref,
    value_ref,
    cos_ref,
    sin_ref,
    gated_ref,
    first_ref,
    full_ref,
    total,
    weight_grad_ref,
    input_grad_ref,
    group_grad_ref,
    mine,
    near,
    far,
    near_sem,
    far_sem,
    done_sem,
    out_sem,
    cross_sem,
    give_sem,
    out_w,
    query_buf,
    key_buf,
    value_buf,
    gated_buf,
    first_buf,
    middle_low,
    flip_buf,
    grad_buf,
    stream_buf,
    tile_buf,
    input_grad_buf,
    retained_buf,
    gate_buf,
    grad_gated_buf,
    upstream_buf,
    query_grad,
    key_grad,
    value_grad,
    load_sem,
    stream_sem,
    group_sem,
    store_sem,
):
    capacity, width = leave_ref.shape
    blocks, tiles = capacity // block, width // block
    pairs = capacity // (2 * rows)
    finish = heads * blocks
    pace = max(1, pairs // (finish + tiles))
    low, f32 = jnp.bfloat16, jnp.float32
    sems = (near_sem, far_sem, done_sem, out_sem, cross_sem, give_sem)
    line = Line(rows, mine, near, far, total, *sems, lags=(1, 2))

    def part(index, size=block):
        return pl.ds(pl.multiple_of(index * size, size), size)

    held = [
        pltpu.make_async_copy(source, target, load_sem.at[index])
        for index, (source, target) in enumerate(
            (
                (leave_ref, mine),
                (middle_low_ref, middle_low),
                (out_w_ref, out_w),
                (query_ref, query_buf),
                (key_ref, key_buf),
                (value_ref, value_buf),
                (gated_ref, gated_buf),
                (first_ref, first_buf),
            )
        )
    ]

    def load_group(index):
        slot = index % 2
        here, there = part(index % blocks), part(index // blocks, VH)
        return [
            pltpu.make_async_copy(
                retained_ref.at[here, there], retained_buf.at[slot], group_sem.at[2 * slot]
            ),
            pltpu.make_async_copy(
                gate_ref.at[here, there], gate_buf.at[slot], group_sem.at[2 * slot + 1]
            ),
        ]

    def load_tile(index):
        slot = index % 2
        return pltpu.make_async_copy(
            full_ref.at[part(index)], stream_buf.at[slot], stream_sem.at[slot]
        )

    def store_tile(index):
        return pltpu.make_async_copy(tile_buf, weight_grad_ref.at[part(index)], store_sem.at[0])

    def store_input(index):
        return pltpu.make_async_copy(
            input_grad_buf, input_grad_ref.at[:, part(index)], store_sem.at[1]
        )

    held[0].start()
    group_grad_ref[...] = jnp.zeros_like(group_grad_ref)
    line.greet()
    held[0].wait()
    for copy in held[1:-2] + load_group(0):
        copy.start()

    def attend_stage(index):
        head, place = index // blocks, index % blocks

        @pl.when(index == 0)
        def _():
            for copy in held[1:-2]:
                copy.wait()
            for copy in held[-2:]:
                copy.start()
            load_tile(0).start()

        for copy in load_group(index):
            copy.wait()

        @pl.when(index < heads * blocks - 1)
        def _():
            for copy in load_group(index + 1):
                copy.start()

        @pl.when(place == 0)
        def _():
            key_grad[...] = jnp.zeros_like(key_grad)
            value_grad[...] = jnp.zeros_like(value_grad)

        slot = index % 2
        here = part(place)
        keys_here, values_here = part(head, KH), part(head, VH)
        gain = group_gain_ref[pl.ds(head, 1), :]
        gate_place = pl.ds(pl.multiple_of(heads * (2 * KH + VH) + head * VH, VH), VH)
        grad_gated_buf[...] = row_product(middle_low[here, :], out_w[:, values_here])

        def gate_rows(piece, carry):
            few = pl.ds(pl.multiple_of(piece * 32, 32), 32)
            there = pl.ds(pl.multiple_of(place * block + piece * 32, 32), 32)
            normed, inverse = group_stats(retained_buf[slot, few, :])
            gate, grad_gated = gate_buf[slot, few, :], grad_gated_buf[few, :]
            sigmoid = jax.nn.sigmoid(gate)
            slope = sigmoid * (1.0 + gate * (1.0 - sigmoid))
            grad_buf[there, gate_place] = (grad_gated * (normed * gain) * slope).astype(low)
            grad_out = grad_gated * (gate * sigmoid)
            group_grad_ref[pl.ds(head, 1), :] += jnp.sum(grad_out * normed, axis=0, keepdims=True)
            scaled = grad_out * gain
            plain_mean = jnp.mean(scaled, axis=-1, keepdims=True)
            cross_mean = jnp.mean(scaled * normed, axis=-1, keepdims=True)
            upstream_buf[few, :] = (
                inverse * (scaled - plain_mean - normed * cross_mean)
            ).astype(low)
            return carry

        lax.fori_loop(0, block // 32, gate_rows, 0, unroll=4)
        upstream = upstream_buf[...]
        query = query_buf[here, keys_here]
        query_grad[...] = jnp.zeros_like(query_grad)

        def visit(other, carry):
            there = part(other)
            decay = decay_block(ends_ref, keep_ref[head], place * block, other * block, block)
            key = key_buf[there, keys_here]
            weights = (turned_product(query, key) * decay).astype(low)
            value_grad[there, :] += outer_product(weights, upstream)
            scores = turned_product(upstream, value_buf[there, values_here]) * decay
            scores = scores.astype(low)
            query_grad[...] += row_product(scores, key)
            key_grad[there, :] += outer_product(scores, query)
            return carry

        lax.fori_loop(0, place + 1, visit, 0)
        cosine, sine = cos_ref[here, :], sin_ref[here, :]
        grad_buf[here, keys_here] = turn(query_grad[...], cosine, -sine).astype(low)

        @pl.when(place == blocks - 1)
        def _():
            def one(other, carry):
                there = part(other)
                turned = turn(key_grad[there, :] * KH ** (-0.5), cos_ref[there, :], -sin_ref[there, :])
                grad_buf[there, part(heads + head, KH)] = turned.astype(low)
                value_place = pl.ds(pl.multiple_of(heads * 2 * KH + head * VH, VH), VH)
                grad_buf[there, value_place] = value_grad[there, :].astype(low)
                return carry

            lax.fori_loop(0, blocks, one, 0)

    def tile_stage(index):
        columns = grad_buf.shape[1]

        @pl.when(index == 0)
        def _():
            for copy in held[-2:]:
                copy.wait()

        @pl.when(index < tiles - 1)
        def _():
            load_tile(index + 1).start()

        @pl.when(index > 0)
        def _():
            store_tile(index - 1).wait()
            store_input(index - 1).wait()

        load_tile(index).wait()
        here = part(index)
        flip_buf[...] = first_buf[:, here].T

        def one(number, carry):
            there = part(number, 512)
            tile_buf[:, there] = row_product(flip_buf[...], grad_buf[:, there]).astype(low)
            return carry

        lax.fori_loop(0, columns // 512, one, 0, unroll=True)

        flip_buf[...] = middle_low[:, here].T

        def last(number, carry):
            there = pl.ds(pl.multiple_of(columns + number * 512, 512), 512)
            tile_buf[:, there] = row_product(
                flip_buf[...], gated_buf[:, part(number, 512)]
            ).astype(low)
            return carry

        lax.fori_loop(0, gated_buf.shape[1] // 512, last, 0, unroll=True)
        store_tile(index).start()

        def inward(number, carry):
            there = part(number)
            input_grad_buf[there, :] = turned_product(
                grad_buf[there, :], stream_buf[index % 2]
            ).astype(low)
            return carry

        lax.fori_loop(0, blocks, inward, 0, unroll=True)
        store_input(index).start()

    def step(index, carry):
        line.step(index, pairs)

        work = index // pace

        @pl.when((index % pace == 0) & (work < finish))
        def _():
            attend_stage(work)

        @pl.when((index % pace == 0) & (work >= finish) & (work < finish + tiles))
        def _():
            tile_stage(work - finish)

        return carry

    lax.fori_loop(0, max(pairs + 3, (finish + tiles) * pace), step, 0)

    def drain(pair, carry):
        line.arrive(pair)
        line.release(pair)
        line.drain(pair)
        return carry

    lax.fori_loop(0, pairs, drain, 0)
    store_tile(tiles - 1).wait()
    store_input(tiles - 1).wait()


def back_stage(
    ends,
    log_keep,
    leave,
    middle_low,
    mix_out,
    retained,
    gate,
    group_values,
    query,
    key,
    value,
    cosine,
    sine,
    gated,
    first_low,
    full,
    collective_id,
    rows=32,
    block=256,
):
    capacity, width = leave.shape
    heads = group_values.shape[0]
    columns, units = full.shape[1], gated.shape[1]
    low, f32 = jnp.bfloat16, jnp.float32
    anywhere, kept = pl.BlockSpec(memory_space=pl.ANY), pl.BlockSpec(memory_space=pltpu.VMEM)
    scalar = pl.BlockSpec(memory_space=pltpu.SMEM)
    return pl.pallas_call(
        functools.partial(back_kernel, rows, block, heads),
        out_shape=(
            jax.ShapeDtypeStruct((capacity, width), low),
            jax.ShapeDtypeStruct((width, columns + units), low),
            jax.ShapeDtypeStruct((capacity, width), low),
            jax.ShapeDtypeStruct((heads, VH), f32),
        ),
        in_specs=[scalar] * 2
        + [anywhere] * 5
        + [kept]
        + [anywhere] * 3
        + [kept] * 2
        + [anywhere] * 3,
        out_specs=(kept, anywhere, anywhere, kept),
        scratch_shapes=line_scratch(capacity, width, rows)
        + [
            pltpu.VMEM((width, units), low),
            pltpu.VMEM(query.shape, low),
            pltpu.VMEM(key.shape, low),
            pltpu.VMEM(value.shape, low),
            pltpu.VMEM(gated.shape, low),
            pltpu.VMEM((capacity, width), low),
            pltpu.VMEM((capacity, width), low),
            pltpu.VMEM((block, capacity), low),
            pltpu.VMEM((capacity, columns), low),
            pltpu.VMEM((2, block, columns), low),
            pltpu.VMEM((block, columns + units), low),
            pltpu.VMEM((capacity, block), low),
            pltpu.VMEM((2, block, VH), f32),
            pltpu.VMEM((2, block, VH), f32),
            pltpu.VMEM((block, VH), f32),
            pltpu.VMEM((block, VH), low),
            pltpu.VMEM((block, KH), f32),
            pltpu.VMEM((capacity, KH), f32),
            pltpu.VMEM((capacity, VH), f32),
            pltpu.SemaphoreType.DMA((8,)),
            pltpu.SemaphoreType.DMA((2,)),
            pltpu.SemaphoreType.DMA((4,)),
            pltpu.SemaphoreType.DMA((2,)),
        ],
        compiler_params=pltpu.CompilerParams(
            collective_id=collective_id, has_side_effects=True, vmem_limit_bytes=62 << 20
        ),
        cost_estimate=pl.CostEstimate(
            flops=100_000_000_000, bytes_accessed=40 << 20, transcendentals=0
        ),
    )(
        ends,
        log_keep,
        leave,
        middle_low,
        mix_out,
        retained,
        gate,
        group_values,
        query,
        key,
        value,
        cosine,
        sine,
        gated,
        first_low,
        full,
    )


def last_kernel(
    rows,
    ways,
    back_ref,
    tokens_ref,
    middle_ref,
    sum_ref,
    leave_ref,
    norm_gain_ref,
    norm_grad_ref,
    group_grad_ref,
    token_grad_ref,
    layer_ref,
    small_ref,
    total,
    mine,
    near,
    far,
    near_sem,
    far_sem,
    done_sem,
    out_sem,
    cross_sem,
    give_sem,
    token_buf,
    middle_buf,
    sum_buf,
    leave_buf,
    layer_buf,
    small_buf,
    small_in,
    load_sem,
    store_sem,
    layer_sem,
    small_send_sem,
    small_recv_sem,
):
    capacity, width = back_ref.shape
    pairs = capacity // (2 * rows)
    heads, group = group_grad_ref.shape
    f32 = jnp.float32
    sems = (near_sem, far_sem, done_sem, out_sem, cross_sem, give_sem)
    line = Line(rows, mine, near, far, total, *sems, lags=(1, 2))
    me = lax.axis_index("dp")
    peers = [lax.rem(me + distance, ways) for distance in range(1, ways)]
    loads = [
        pltpu.make_async_copy(source, target, load_sem.at[index])
        for index, (source, target) in enumerate(
            (
                (back_ref, mine),
                (tokens_ref, token_buf),
                (middle_ref, middle_buf),
                (sum_ref, sum_buf),
                (leave_ref, leave_buf),
            )
        )
    ]

    def part(pair):
        return pl.ds(pl.multiple_of(pair * 2 * rows, 2 * rows), 2 * rows)

    def store(pair):
        return pltpu.make_async_copy(
            middle_buf.at[part(pair)], token_grad_ref.at[part(pair)], store_sem.at[pair]
        )

    def store_layer(pair):
        slot = pair % 2
        return pltpu.make_async_copy(
            layer_buf.at[slot], layer_ref.at[part(pair)], layer_sem.at[slot]
        )

    def share(distance):
        return pltpu.make_async_remote_copy(
            small_buf,
            small_in.at[distance],
            small_send_sem.at[distance],
            small_recv_sem.at[distance],
            device_id={"dp": peers[distance]},
            device_id_type=MESH,
        )

    loads[0].start()
    small_buf[...] = jnp.zeros_like(small_buf)
    small_buf[2:4, :] = norm_grad_ref[...]
    for head in range(heads):
        small_buf[4:5, head * group : (head + 1) * group] = group_grad_ref[head : head + 1, :]
    line.greet(peers)
    loads[0].wait()

    def norm_stage(pair):
        line.arrive(pair)

        @pl.when(pair == 0)
        def _():
            for copy in loads[1:]:
                copy.wait()

        @pl.when(pair > 1)
        def _():
            store_layer(pair - 2).wait()

        here = part(pair)
        values = token_buf[here, :].astype(f32)
        layer_buf[pair % 2] = (
            values + sum_buf[here, :].astype(f32) + leave_buf[here, :].astype(f32)
        )
        result, gain_grad, shift_grad = norm_back_rows(
            values, total[here, :].astype(f32), norm_gain_ref[...]
        )
        middle_buf[here, :] += result
        small_buf[0:1, :] += gain_grad
        small_buf[1:2, :] += shift_grad
        store(pair).start()
        store_layer(pair).start()

    def step(index, carry):
        line.step(index, pairs)

        @pl.when(index == 0)
        def _():
            for copy in loads[1:]:
                copy.start()

        @pl.when(index >= 5)
        def _():
            norm_stage(index - 5)

        return carry

    lax.fori_loop(0, pairs + 5, step, 0)
    for distance in range(ways - 1):
        share(distance).start()

    def drain(pair, carry):
        line.release(pair)
        line.drain(pair)
        store(pair).wait()
        return carry

    lax.fori_loop(0, pairs, drain, 0)
    store_layer(pairs - 2).wait()
    store_layer(pairs - 1).wait()
    for distance in range(ways - 1):
        share(distance).wait()
    small_ref[...] = small_buf[...]
    for distance in range(ways - 1):
        small_ref[...] += small_in[distance]


def last_stage(
    back,
    tokens,
    middle,
    branch_sum,
    leave_sum,
    norm_gain,
    norm_grad,
    group_grad,
    ways,
    collective_id,
    rows=32,
):
    capacity, width = back.shape
    low, f32 = jnp.bfloat16, jnp.float32
    anywhere, kept = pl.BlockSpec(memory_space=pl.ANY), pl.BlockSpec(memory_space=pltpu.VMEM)
    small = (8, width)
    return pl.pallas_call(
        functools.partial(last_kernel, rows, ways),
        out_shape=(
            jax.ShapeDtypeStruct((capacity, width), f32),
            jax.ShapeDtypeStruct((capacity, width), f32),
            jax.ShapeDtypeStruct(small, f32),
        ),
        in_specs=[anywhere] * 5 + [kept] * 3,
        out_specs=(anywhere, anywhere, kept),
        scratch_shapes=[pltpu.VMEM((capacity, width), low)]
        + line_scratch(capacity, width, rows)
        + [
            pltpu.VMEM((capacity, width), low),
            pltpu.VMEM((capacity, width), f32),
            pltpu.VMEM((capacity, width), low),
            pltpu.VMEM((capacity, width), low),
            pltpu.VMEM((2, 2 * rows, width), f32),
            pltpu.VMEM(small, f32),
            pltpu.VMEM((ways - 1, *small), f32),
            pltpu.SemaphoreType.DMA((5,)),
            pltpu.SemaphoreType.DMA((capacity // (2 * rows),)),
            pltpu.SemaphoreType.DMA((2,)),
            pltpu.SemaphoreType.DMA((ways - 1,)),
            pltpu.SemaphoreType.DMA((ways - 1,)),
        ],
        compiler_params=pltpu.CompilerParams(
            collective_id=collective_id, has_side_effects=True, vmem_limit_bytes=52 << 20
        ),
        cost_estimate=pl.CostEstimate(
            flops=100_000_000_000, bytes_accessed=40 << 20, transcendentals=0
        ),
    )(back, tokens, middle, branch_sum, leave_sum, norm_gain[None], norm_grad, group_grad)


def local(
    tokens,
    lengths,
    cotangent,
    qk_weight,
    qk_first,
    qk_second,
    inner_weight,
    inner_first,
    inner_second,
    outer_weight,
    outer_first,
    outer_second,
    norm_params,
    norm_first,
    norm_second,
    group_gain,
    group_first,
    group_second,
):
    capacity = tokens.shape[0]
    local_heads = group_gain.shape[0]
    low = jnp.bfloat16
    tensor_index, data_index = lax.axis_index("tensor"), lax.axis_index("dp")

    def joined(shards):
        return jnp.concatenate([part.astype(low) for part in shards], axis=1)

    def gather(shards):
        return lax.all_gather(joined(shards), "dp", axis=0, tiled=True)

    def scatter(grad):
        return lax.psum_scatter(grad, "dp", scatter_dimension=0, tiled=True)

    norm_cols, group_cols = norm_params.shape[1], group_gain.shape[1]
    small = lax.all_gather(
        jnp.concatenate([norm_params.reshape(-1), group_gain.reshape(-1)]).astype(low), "dp"
    ).astype(jnp.float32)
    ways = small.shape[0]
    norm_values = small[:, : 4 * norm_cols].reshape(ways, 4, norm_cols)
    norm_values = norm_values.transpose(1, 0, 2).reshape(4, -1)
    group_values = small[:, 4 * norm_cols :].reshape(ways, local_heads, group_cols)
    group_values = group_values.transpose(1, 0, 2).reshape(local_heads, -1)
    first_full = gather([qk_weight[0], qk_weight[1], inner_weight[0], inner_weight[1]])
    mix_shard = outer_weight[0].astype(low)
    mlp_shard = joined([inner_weight[2], inner_weight[3]])
    out_shard = outer_weight[1].astype(low)
    row_index, sequence_id, position, live_rows = sequence_layout(lengths[0], capacity)
    cosine, sine = rotation_tables(position, KH)
    ends = jnp.cumsum(lengths[0])
    head_ids = tensor_index * local_heads + jnp.arange(local_heads, dtype=jnp.int32)
    log_keep = jnp.log1p(-jnp.exp2(-(5.0 + head_ids.astype(jnp.float32))))
    inputs = tokens.astype(jnp.float32)
    first_out, unused_normed, unused_inverse = layer_norm(
        inputs, norm_values[0], norm_values[1], NORM_EPS
    )
    first_low = first_out.astype(low)
    query, key, value, gate, retained, gated, branch, mix_out = retain(
        ends, log_keep, first_low, first_full, cosine, sine, group_values, mix_shard, 3
    )
    grad_top = cotangent.astype(jnp.float32) * live_rows.astype(jnp.float32)[:, None]
    top_low = grad_top.astype(low)
    branch_sum, leave, mlp_grad, grad_middle, middle_low, norm_two = middle_stage(
        branch, tokens, top_low, norm_values[2], norm_values[3], mlp_shard, out_shard, 0
    )
    mlp_part = scatter(mlp_grad)
    leave_sum, first_grad, back_first, grad_group_gain = back_stage(
        ends,
        log_keep,
        leave,
        middle_low,
        mix_out,
        retained,
        gate,
        group_values,
        query,
        key,
        value,
        cosine,
        sine,
        gated,
        first_low,
        first_full,
        1,
    )
    first_part = scatter(first_grad)
    back_first, mlp_part = lax.optimization_barrier((back_first, mlp_part))
    token_grad, layer_out, small_grad = last_stage(
        back_first,
        tokens,
        grad_middle,
        branch_sum,
        leave_sum,
        norm_values[0],
        norm_two,
        grad_group_gain,
        ways,
        2,
    )
    norm_grad = lax.dynamic_slice(small_grad, (0, data_index * norm_cols), (4, norm_cols))
    group_grad = lax.dynamic_slice(
        small_grad[4, : local_heads * VH].reshape(local_heads, VH),
        (0, data_index * group_cols),
        (local_heads, group_cols),
    )
    qk_cols, mix_cols = local_heads * KH, local_heads * VH
    starts = [qk_cols, 2 * qk_cols, 2 * qk_cols + mix_cols, 2 * qk_cols + 2 * mix_cols]
    query_grad, key_grad, value_grad, gate_grad, mix_out_part = jnp.split(
        first_part, starts, axis=1
    )
    qk_grad = jnp.stack([query_grad, key_grad]).astype(jnp.float32)
    units = out_shard.shape[1]
    left_grad, right_grad, mlp_out_part = jnp.split(mlp_part, [units, 2 * units], axis=1)
    inner_grad = jnp.stack([value_grad, gate_grad, left_grad, right_grad]).astype(jnp.float32)
    outer_grad = jnp.stack([mix_out_part, mlp_out_part]).astype(jnp.float32)
    qk_new = adam_update(qk_weight, qk_grad, qk_first, qk_second, MATRIX_RATE, WEIGHT_DECAY)
    inner_new = adam_update(
        inner_weight, inner_grad, inner_first, inner_second, MATRIX_RATE, WEIGHT_DECAY
    )
    outer_new = adam_update(
        outer_weight, outer_grad, outer_first, outer_second, MATRIX_RATE, WEIGHT_DECAY
    )
    norm_new = adam_update(norm_params, norm_grad, norm_first, norm_second, VECTOR_RATE, 0.0)
    group_new = adam_update(group_gain, group_grad, group_first, group_second, VECTOR_RATE, 0.0)
    return (layer_out, token_grad, *qk_new, *inner_new, *outer_new, *norm_new, *group_new)


def solution(mesh):
    in_specs = (
        P("dp", None),
        P("dp", None),
        P("dp", None),
        P(None, "dp", "tensor"),
        P(None, "dp", "tensor"),
        P(None, "dp", "tensor"),
        P(None, "dp", "tensor"),
        P(None, "dp", "tensor"),
        P(None, "dp", "tensor"),
        P(None, "dp", "tensor"),
        P(None, "dp", "tensor"),
        P(None, "dp", "tensor"),
        P(None, "dp"),
        P(None, "dp"),
        P(None, "dp"),
        P("tensor", "dp"),
        P("tensor", "dp"),
        P("tensor", "dp"),
    )
    out_specs = (
        P("dp", None),
        P("dp", None),
        P(None, "dp", "tensor"),
        P(None, "dp", "tensor"),
        P(None, "dp", "tensor"),
        P(None, "dp", "tensor"),
        P(None, "dp", "tensor"),
        P(None, "dp", "tensor"),
        P(None, "dp", "tensor"),
        P(None, "dp", "tensor"),
        P(None, "dp", "tensor"),
        P(None, "dp"),
        P(None, "dp"),
        P(None, "dp"),
        P("tensor", "dp"),
        P("tensor", "dp"),
        P("tensor", "dp"),
    )
    return jax.shard_map(local, mesh=mesh, in_specs=in_specs, out_specs=out_specs, check_vma=False)
```
